32 devices in a mesh: seq: 8 (over z, y), mp: 4 (over x, core).
Axes of the slice: x: 2, y: 2, z: 4, core: 2. Of those that a mesh axis runs over, the one named last changes fastest.
Arguments:
- block_input: float32 [2, 512, 768], P(None, 'seq', 'mp'), may hold values from -6 to 6
- out_grad: float32 [2, 512, 768], P(None, 'seq', 'mp'), may hold values from -6 to 6
- lengths: int32 [2], replicated, may hold values from 128 to 512, as said below
- square_factors: float32 [4, 4, 192, 192], P(None, 'mp'), may hold values from -0.4375 to 0.4375
- square_moment: float32 [4, 4, 192, 192], P(None, 'mp'), may hold values from -56 to 56
- input_left: float32 [4, 192, 576], P('mp'), may hold values from -0.4375 to 0.4375
- input_left_moment: float32 [4, 192, 576], P('mp'), may hold values from -56 to 56
- up_left: float32 [4, 192, 1536], P('mp'), may hold values from -0.4375 to 0.4375
- up_left_moment: float32 [4, 192, 1536], P('mp'), may hold values from -56 to 56
- down_right: float32 [4, 768, 768], P('mp'), may hold values from -0.21875 to 0.21875
- down_right_moment: float32 [4, 768, 768], P('mp'), may hold values from -56 to 56
- down_left: float32 [4, 768, 192], P('mp'), may hold values from -0.21875 to 0.21875
- down_left_moment: float32 [4, 768, 192], P('mp'), may hold values from -56 to 56
- vectors: float32 [13, 768], P(None, 'mp')
- vectors_first: float32 [13, 768], P(None, 'mp'), may hold values from -10 to 10
- vectors_second: float32 [13, 768], P(None, 'mp'), may hold values from 12.8 to 51.2
- filter_hidden: float32 [133, 128], replicated
- hidden_first: float32 [133, 128], replicated
- hidden_second: float32 [133, 128], replicated
- filter_out: float32 [128, 768], P(None, 'mp'), may hold values from -0.5 to 0.5
- filter_out_first: float32 [128, 768], P(None, 'mp'), may hold values from -10 to 10
- filter_out_second: float32 [128, 768], P(None, 'mp'), may hold values from 12.8 to 51.2
Outputs:
- block_output: float32 [2, 512, 768], P(None, 'seq', 'mp')
- input_grad: float32 [2, 512, 768], P(None, 'seq', 'mp')
- square_moment_new: float32 [4, 4, 192, 192], P(None, 'mp')
- square_new: float32 [4, 4, 192, 192], P(None, 'mp')
- square_copy: bfloat16 [4, 4, 192, 192], P(None, 'mp')
- input_left_moment_new: float32 [4, 192, 576], P('mp')
- input_left_new: float32 [4, 192, 576], P('mp')
- input_left_copy: bfloat16 [4, 192, 576], P('mp')
- up_left_moment_new: float32 [4, 192, 1536], P('mp')
- up_left_new: float32 [4, 192, 1536], P('mp')
- up_left_copy: bfloat16 [4, 192, 1536], P('mp')
- down_right_moment_new: float32 [4, 768, 768], P('mp')
- down_right_new: float32 [4, 768, 768], P('mp')
- down_right_copy: bfloat16 [4, 768, 768], P('mp')
- down_left_moment_new: float32 [4, 768, 192], P('mp')
- down_left_new: float32 [4, 768, 192], P('mp')
- down_left_copy: bfloat16 [4, 768, 192], P('mp')
- vectors_first_new: float32 [13, 768], P(None, 'mp')
- vectors_second_new: float32 [13, 768], P(None, 'mp')
- vectors_new: float32 [13, 768], P(None, 'mp')
- vectors_copy: bfloat16 [13, 768], P(None, 'mp')
- hidden_first_new: float32 [133, 128], replicated
- hidden_second_new: float32 [133, 128], replicated
- filter_hidden_new: float32 [133, 128], replicated
- filter_hidden_copy: bfloat16 [133, 128], replicated
- filter_out_first_new: float32 [128, 768], P(None, 'mp')
- filter_out_second_new: float32 [128, 768], P(None, 'mp')
- filter_out_new: float32 [128, 768], P(None, 'mp')
- filter_out_copy: bfloat16 [128, 768], P(None, 'mp')
The draws below stay inside these ranges and needn't reach their ends.
Inputs may be any that keep to these rules, and one draw needn't show every extreme that they name: `lengths`: positions from a sequence's length on are padding; one sequence of the batch, drawn from the seed, has no padding.
All inputs are finite; a program needn't handle non-finite values.
Results may differ from the reference program's by a relative error of at most 0.001.
Values sent between devices are 32-bit elements; how exact they have to be, the bound alone decides.
A program may use at most 256 MiB of HBM per device.

```python
import math
import jax
import jax.numpy as jnp
from jax import lax

D = 768
NB = 4
ORDER = 128
EMB = 5
KS = 3
STEP = 10
SEQS = 2
BW = 192
FB = 768
LEN = 512


def draw_lengths(key, part):
    key = jax.random.fold_in(key, 11)
    key_lengths, key_complete = jax.random.split(key)
    drawn = jax.random.randint(key_lengths, (SEQS,), LEN // 4, LEN + 1)
    complete = jax.random.randint(key_complete, (), 0, SEQS)
    return jnp.where(jnp.arange(SEQS) == complete, LEN, drawn).astype(jnp.int32)


def draw_vectors(key, part):
    key = jax.random.fold_in(key, 23)
    key_gains, key_decay, key_skip, key_taps, key_leading = jax.random.split(key, 5)
    gains = jax.random.uniform(key_gains, (2, D), jnp.float32, 0.7, 1.3)
    decay_rates = jnp.exp(jax.random.uniform(key_decay, (1, D), jnp.float32, math.log(0.2), math.log(20.0)))
    skip_gains = jax.random.uniform(key_skip, (1, D), jnp.float32, 0.5, 1.5)
    conv_taps = 0.5 * jax.random.normal(key_taps, (3, KS, D), jnp.float32)
    leading = jax.random.uniform(key_leading, (3, 1, D), jnp.float32, 0.6, 1.4)
    first_tap = (jnp.arange(KS) == 0)[None, :, None]
    conv_taps = jnp.where(first_tap, leading, conv_taps)
    return jnp.concatenate([gains, decay_rates, skip_gains, conv_taps.reshape(3 * KS, D)], axis=0)


def draw_filter_hidden(key, part):
    key = jax.random.fold_in(key, 37)
    key_first, key_second = jax.random.split(key)
    first_layer = 2.0 * jax.random.normal(key_first, (EMB, ORDER), jnp.float32)
    second_layer = 2.0 * ORDER ** (-0.5) * jax.random.normal(key_second, (ORDER, ORDER), jnp.float32)
    return jnp.concatenate([first_layer, second_layer], axis=0)


def row_factors(first_rows):
    return jnp.where(jnp.arange(EMB + ORDER) < EMB, first_rows, 1.0).astype(jnp.float32)[:, None]


def draw_hidden_first(key, part):
    key = jax.random.fold_in(key, 41)
    scale = 0.28 * (SEQS * LEN * D / ORDER) ** 0.5
    return scale * row_factors(14.0) * jax.random.normal(key, (EMB + ORDER, ORDER), jnp.float32)


def draw_hidden_second(key, part):
    key = jax.random.fold_in(key, 43)
    spread = jnp.exp(jax.random.uniform(key, (EMB + ORDER, ORDER), jnp.float32, math.log(0.33), math.log(1.3)))
    return spread * (SEQS * LEN * D / ORDER) * row_factors(196.0)


def block_levels(key, dims, cuts, smallest, largest):
    loudness = 1.0
    for dim, shards_of in cuts:
        draws = jax.random.uniform(jax.random.fold_in(jax.random.fold_in(key, 6), dim), (shards_of,), jnp.float32, smallest / len(cuts), largest / len(cuts))
        loudness = loudness * jnp.repeat(jnp.exp(draws), dims[dim] // shards_of).reshape((-1,) + (1,) * (len(dims) - 1 - dim))
    return loudness


def normal_values(key, shape, scale, bound, cuts=(), dtype=jnp.bfloat16):
    entries = jax.random.normal(key, shape, jnp.float32) * scale
    if len(cuts) > 0:
        entries = block_levels(key, shape, cuts, -0.22, 0.18) * entries
    return jnp.clip(entries, min=-bound, max=bound).astype(dtype)


def setup_inputs(seed: int = 0) -> dict:
    key_of = jax.random.split(jax.random.key(seed), 23)
    block_input = normal_values(key_of[0], (SEQS, LEN, D), 1.0, 6.0, ((1, 8), (2, 4)), jnp.float32)
    out_grad = normal_values(key_of[1], (SEQS, LEN, D), 1.0, 6.0, ((1, 8), (2, 4)), jnp.float32)
    lengths = draw_lengths(jax.random.fold_in(key_of[22], 71), 0)
    square_factors = normal_values(key_of[3], (4, NB, BW, BW), BW ** -0.5, 0.4375, ((1, 4),), jnp.float32)
    square_moment = normal_values(key_of[4], (4, NB, BW, BW), (0.3 * (SEQS * LEN) ** 0.5), 56.0, ((1, 4),), jnp.float32)
    input_left = normal_values(key_of[5], (NB, BW, 3 * BW), BW ** -0.5, 0.4375, ((0, 4),), jnp.float32)
    input_left_moment = normal_values(key_of[6], (NB, BW, 3 * BW), (0.3 * (SEQS * LEN) ** 0.5), 56.0, ((0, 4),), jnp.float32)
    up_left = normal_values(key_of[7], (NB, BW, 2 * FB), BW ** -0.5, 0.4375, ((0, 4),), jnp.float32)
    up_left_moment = normal_values(key_of[8], (NB, BW, 2 * FB), (0.3 * (SEQS * LEN) ** 0.5), 56.0, ((0, 4),), jnp.float32)
    down_right = normal_values(key_of[9], (NB, FB, FB), FB ** -0.5, 0.21875, ((0, 4),), jnp.float32)
    down_right_moment = normal_values(key_of[10], (NB, FB, FB), (0.3 * (SEQS * LEN) ** 0.5), 56.0, ((0, 4),), jnp.float32)
    down_left = normal_values(key_of[11], (NB, FB, BW), FB ** -0.5, 0.21875, ((0, 4),), jnp.float32)
    down_left_moment = normal_values(key_of[12], (NB, FB, BW), (0.3 * (SEQS * LEN) ** 0.5), 56.0, ((0, 4),), jnp.float32)
    vectors = draw_vectors(jax.random.fold_in(key_of[22], 71), 0)
    vectors_first = normal_values(key_of[14], (4 + 3 * KS, D), (0.05 * (SEQS * LEN) ** 0.5), 10.0, ((1, 4),), jnp.float32)
    vectors_second = jnp.clip(jnp.exp(math.log(51.2) - 1.3862944 * jax.random.uniform(key_of[15], (4 + 3 * KS, D), jnp.float32) ** block_levels(key_of[15], (4 + 3 * KS, D), ((1, 4),), -0.2, 0.2)), 12.8, 51.2)
    filter_hidden = draw_filter_hidden(jax.random.fold_in(key_of[22], 71), 0)
    hidden_first = draw_hidden_first(jax.random.fold_in(key_of[22], 71), 0)
    hidden_second = draw_hidden_second(jax.random.fold_in(key_of[22], 71), 0)
    filter_out = normal_values(key_of[19], (ORDER, D), ORDER ** -0.5, 0.5, ((1, 4),), jnp.float32)
    filter_out_first = normal_values(key_of[20], (ORDER, D), (0.05 * (SEQS * LEN) ** 0.5), 10.0, ((1, 4),), jnp.float32)
    filter_out_second = jnp.clip(jnp.exp(math.log(51.2) - 1.3862944 * jax.random.uniform(key_of[21], (ORDER, D), jnp.float32) ** block_levels(key_of[21], (ORDER, D), ((1, 4),), -0.2, 0.2)), 12.8, 51.2)
    return dict(block_input=block_input, out_grad=out_grad, lengths=lengths, square_factors=square_factors, square_moment=square_moment, input_left=input_left, input_left_moment=input_left_moment, up_left=up_left, up_left_moment=up_left_moment, down_right=down_right, down_right_moment=down_right_moment, down_left=down_left, down_left_moment=down_left_moment, vectors=vectors, vectors_first=vectors_first, vectors_second=vectors_second, filter_hidden=filter_hidden, hidden_first=hidden_first, hidden_second=hidden_second, filter_out=filter_out, filter_out_first=filter_out_first, filter_out_second=filter_out_second)


@jax.custom_vjp
def low(v):
    return lax.optimization_barrier(v.astype(jnp.bfloat16)).astype(jnp.float32)

@jax.custom_vjp
def low_back(v):
    return v

def low_keep(v):
    return (low(v), None)

def low_pass(kept, grad):
    return (grad,)

def back_keep(v):
    return (v, None)

def back_low(kept, grad):
    return (low(grad),)
low.defvjp(low_keep, low_pass)
low_back.defvjp(back_keep, back_low)
highest = lax.Precision.HIGHEST
norm_epsilon = 1e-05
beta_first = 0.9
beta_second = 0.95
adam_epsilon = 1e-08
weight_decay = 0.01
rate_vectors = 0.2
rate_hidden = 0.05
rate_output = 0.05
muon_rate = 0.5
momentum_decay = 0.5
schulz_first = 3.4445
schulz_second = -4.775
schulz_third = 2.0315
filter_frequency = 10.0

def monarch(values, right, left):
    leading = values.shape[:-1]
    blocks = right.shape[0]
    pieces = values.reshape(leading + (blocks, right.shape[1]))
    middle = jnp.einsum('...bi,bim->...bm', pieces, right, precision=highest)
    quarter = right.shape[2] // blocks
    middle = middle.reshape(leading + (blocks, blocks, quarter))
    mixture = jnp.swapaxes(middle, -3, -2).reshape(leading + (blocks, blocks * quarter))
    return jnp.einsum('...em,emo->...eo', mixture, left, precision=highest)

def normalize(values, gain):
    return values * lax.rsqrt(lax.optimization_barrier(jnp.mean(values * values, axis=-1, keepdims=True)) + norm_epsilon) * gain

def features(length):
    fraction = jnp.arange(length).astype(jnp.float32) / length
    angle = 2.0 * math.pi * fraction
    stacked = jnp.stack([fraction, jnp.cos(angle), jnp.sin(angle), jnp.cos(2.0 * angle), jnp.sin(2.0 * angle)], axis=1)
    return (stacked, fraction)

def filter_taps(hidden_weights, out_weights, decay_rates, length):
    stacked, fraction = features(length)
    layer_one = jnp.sin(filter_frequency * jnp.dot(stacked, hidden_weights[:EMB], precision=highest, preferred_element_type=jnp.float32))
    layer_two = jnp.sin(filter_frequency * jnp.dot(layer_one, hidden_weights[EMB:], precision=highest, preferred_element_type=jnp.float32))
    shaped = jnp.dot(layer_two, out_weights, precision=highest, preferred_element_type=jnp.float32)
    return shaped * jnp.exp(-fraction[:, None] * decay_rates[None, :]) * length ** (-0.5)

def short_conv(values, kernel):
    padded = jnp.pad(values, ((0, 0), (2, 0), (0, 0)))
    return kernel[0] * values + kernel[1] * padded[:, 1:-1] + kernel[2] * padded[:, :-2]

def forward(block_input, lengths, square_factors, input_left, up_left, down_right, down_left, vectors, filter_hidden, filter_out):
    seqs_count, length, model_width = block_input.shape
    blocks = square_factors.shape[1]
    block_width = model_width // blocks
    normed_one = normalize(block_input, vectors[0])
    projected = monarch(normed_one, square_factors[0], input_left).reshape(seqs_count, length, blocks, 3, block_width)
    conv_taps = vectors[4:].reshape(3, KS, model_width)
    stream_one = short_conv(projected[:, :, :, 0, :].reshape(seqs_count, length, model_width), conv_taps[0])
    stream_two = short_conv(projected[:, :, :, 1, :].reshape(seqs_count, length, model_width), conv_taps[1])
    stream_three = short_conv(projected[:, :, :, 2, :].reshape(seqs_count, length, model_width), conv_taps[2])
    validity = (jnp.arange(length)[None, :] < lengths[:, None]).astype(jnp.float32)[:, :, None]
    product_in = stream_one * stream_three * validity
    kernel = filter_taps(filter_hidden, filter_out, vectors[2], length)
    spectrum = jnp.fft.rfft(product_in, n=2 * length, axis=1) * jnp.fft.rfft(kernel, n=2 * length, axis=0)[None]
    long_out = jnp.fft.irfft(spectrum, n=2 * length, axis=1)[:, :length]
    gated_mix = stream_two * (long_out + vectors[3] * product_in)
    mixed_out = monarch(gated_mix, square_factors[1], square_factors[2]).reshape(seqs_count, length, model_width)
    hidden_state = block_input + mixed_out
    normed_two = normalize(hidden_state, vectors[1])
    gate_up = monarch(normed_two, square_factors[3], up_left).reshape(seqs_count, length, blocks, 2, -1)
    gate_values = gate_up[:, :, :, 0, :].reshape(seqs_count, length, -1)
    upward = gate_up[:, :, :, 1, :].reshape(seqs_count, length, -1)
    activated = jax.nn.gelu(gate_values) * upward
    down_out = monarch(activated, down_right, down_left).reshape(seqs_count, length, model_width)
    return hidden_state + down_out

def newton_schulz(matrix):
    rows_count, cols_count = matrix.shape
    current = matrix / (jnp.sqrt(jnp.sum(matrix * matrix)) + 1e-07)
    flipped = rows_count > cols_count
    if flipped:
        current = current.T
    for repeat in range(5):
        square = jnp.dot(current, current.T, precision=highest, preferred_element_type=jnp.float32)
        polynomial = schulz_second * square + schulz_third * jnp.dot(square, square, precision=highest, preferred_element_type=jnp.float32)
        current = schulz_first * current + jnp.dot(polynomial, current, precision=highest, preferred_element_type=jnp.float32)
    if flipped:
        current = current.T
    return current

def muon_update(weights, moment, gradient):
    moment_new = momentum_decay * moment + gradient
    rows_count, cols_count = weights.shape[-2:]
    flat = moment_new.reshape((-1, rows_count, cols_count))
    orthogonal = jax.vmap(newton_schulz)(flat).reshape(weights.shape)
    new_weights = weights - muon_rate * math.sqrt(max(rows_count, cols_count) / rows_count) * orthogonal
    return (moment_new, new_weights, new_weights.astype(jnp.bfloat16))

def adam_update(weights, first, second, gradient, rate):
    first_new = beta_first * first + (1.0 - beta_first) * gradient
    second_new = beta_second * second + (1.0 - beta_second) * gradient * gradient
    corrected_first = first_new / (1.0 - beta_first ** STEP)
    corrected_second = second_new / (1.0 - beta_second ** STEP)
    new_weights = weights - rate * (corrected_first / (jnp.sqrt(corrected_second) + adam_epsilon) + weight_decay * weights)
    return (first_new, second_new, new_weights, new_weights.astype(jnp.bfloat16))

def reference(block_input, out_grad, lengths, square_factors, square_moment, input_left, input_left_moment, up_left, up_left_moment, down_right, down_right_moment, down_left, down_left_moment, vectors, vectors_first, vectors_second, filter_hidden, hidden_first, hidden_second, filter_out, filter_out_first, filter_out_second):

    def closure(inputs, square_w, input_w, up_w, down_r_w, down_l_w, vector_w, hidden_w, out_w):
        return forward(inputs, lengths, square_w, input_w, up_w, down_r_w, down_l_w, vector_w, hidden_w, out_w)
    block_output, pull = jax.vjp(closure, block_input, square_factors, input_left, up_left, down_right, down_left, vectors, filter_hidden, filter_out)
    input_grad, square_grad, input_left_grad, up_left_grad, down_right_grad, down_left_grad, vectors_grad, hidden_grad, filter_out_grad = pull(out_grad)
    square_moment_new, square_new, square_copy = muon_update(square_factors, square_moment, square_grad)
    input_left_moment_new, input_left_new, input_left_copy = muon_update(input_left, input_left_moment, input_left_grad)
    up_left_moment_new, up_left_new, up_left_copy = muon_update(up_left, up_left_moment, up_left_grad)
    down_right_moment_new, down_right_new, down_right_copy = muon_update(down_right, down_right_moment, down_right_grad)
    down_left_moment_new, down_left_new, down_left_copy = muon_update(down_left, down_left_moment, down_left_grad)
    vectors_first_new, vectors_second_new, vectors_new, vectors_copy = adam_update(vectors, vectors_first, vectors_second, vectors_grad, rate_vectors)
    hidden_first_new, hidden_second_new, filter_hidden_new, filter_hidden_copy = adam_update(filter_hidden, hidden_first, hidden_second, hidden_grad, rate_hidden)
    filter_out_first_new, filter_out_second_new, filter_out_new, filter_out_copy = adam_update(filter_out, filter_out_first, filter_out_second, filter_out_grad, rate_output)
    return (block_output, input_grad, square_moment_new, square_new, square_copy, input_left_moment_new, input_left_new, input_left_copy, up_left_moment_new, up_left_new, up_left_copy, down_right_moment_new, down_right_new, down_right_copy, down_left_moment_new, down_left_new, down_left_copy, vectors_first_new, vectors_second_new, vectors_new, vectors_copy, hidden_first_new, hidden_second_new, filter_hidden_new, filter_hidden_copy, filter_out_first_new, filter_out_second_new, filter_out_new, filter_out_copy)
```

```python
import functools
import math

import jax
import jax.numpy as jnp
import numpy as np
from jax import lax
from jax.experimental import pallas as pl
from jax.experimental.pallas import tpu as pltpu
from jax.sharding import PartitionSpec as P

EMB = 5
KS = 3
STEP = 10
SEQS = 2

HIGH = lax.Precision.HIGH
HIGHEST = lax.Precision.HIGHEST
MESH = pl.DeviceIdType.MESH
norm_epsilon = 1e-05
beta_first = 0.9
beta_second = 0.95
adam_epsilon = 1e-08
weight_decay = 0.01
rate_vectors = 0.2
rate_hidden = 0.05
rate_output = 0.05
muon_rate = 0.5
momentum_decay = 0.5
schulz_first = 3.4445
schulz_second = -4.775
schulz_third = 2.0315
filter_frequency = 10.0
gelu_scale = math.sqrt(2.0 / math.pi)
gelu_cubic = 0.044715


def contract(a, b, dim_a, dim_b, precision=HIGH):
    return lax.dot_general(
        a,
        b,
        (((dim_a,), (dim_b,)), ((), ())),
        precision=precision,
        preferred_element_type=jnp.float32,
    )


def nn(a, b, precision=HIGH):
    return contract(a, b, 1, 0, precision)


def nt(a, b, precision=HIGH):
    return contract(a, b, 1, 1, precision)


def tn(a, b, precision=HIGH):
    return contract(a, b, 0, 0, precision)


def spectrum_tables(group_len):
    rows = SEQS * group_len
    period = 2 * group_len
    time = np.arange(group_len)
    lags = np.arange(period)
    bins = np.arange(group_len)
    angle = 2.0 * np.pi * (np.outer(time, bins) % period) / period
    real = np.cos(angle)
    imag = -np.sin(angle)
    imag[:, 0] = (-1.0) ** time
    forward = np.zeros((rows, 2 * rows))
    for s in range(SEQS):
        part = slice(s * group_len, (s + 1) * group_len)
        forward[part, part] = real
        forward[part, rows + s * group_len : rows + (s + 1) * group_len] = imag
    of_taps = np.concatenate([real] * SEQS + [imag] * SEQS, axis=1)
    angle = 2.0 * np.pi * (np.outer(bins, lags) % period) / period
    back_real = 2.0 * np.cos(angle) / period
    back_real[0] = 1.0 / period
    back_imag = -2.0 * np.sin(angle) / period
    back_imag[0] = (-1.0) ** lags / period
    inverse = np.zeros((2 * rows, rows))
    for s in range(SEQS):
        part = slice(s * group_len, (s + 1) * group_len)
        inverse[part, part] = back_real[:, :group_len]
        inverse[rows + s * group_len : rows + (s + 1) * group_len, part] = back_imag[:, :group_len]
    window = np.concatenate([back_real] * SEQS + [back_imag] * SEQS, axis=0)
    return tuple(
        v.astype(np.float32)
        for v in (forward, of_taps, inverse, window[:, :group_len], window[:, group_len:])
    )


def feature_table(length):
    fraction = np.arange(length).astype(np.float32) / np.float32(length)
    angle = np.float32(2.0 * math.pi) * fraction
    wide = angle.astype(np.float64)
    twice = (np.float32(2.0) * angle).astype(np.float64)
    columns = [fraction, np.cos(wide), np.sin(wide), np.cos(twice), np.sin(twice)]
    table = np.zeros((length, 8), np.float32)
    for i, column in enumerate(columns):
        table[:, i] = column.astype(np.float32)
    return table


def chain_kernel(
    dims,
    x_ref,
    og_ref,
    len_ref,
    vec_ref,
    fh_ref,
    fo_ref,
    feat_ref,
    tfwd_ref,
    ttap_ref,
    tinv_ref,
    tw1_ref,
    tw2_ref,
    sq_hbm,
    inl_hbm,
    ul_hbm,
    dr_hbm,
    dl_hbm,
    bo_ref,
    ig_ref,
    gsq_ref,
    ginl_ref,
    gul_ref,
    gdr_ref,
    gdl_ref,
    gvec_ref,
    gfo_ref,
    gdec_ref,
    gw1_ref,
    gw2_ref,
    sq_v,
    inl_v,
    ul_v,
    dr_v,
    dl_v,
    vecp_v,
    vt_v,
    vtc_v,
    foc_v,
    xt_v,
    ogt_v,
    u0_v,
    z_v,
    z1_v,
    z2_v,
    conv_v,
    convh_v,
    prod_v,
    insum_v,
    gated_v,
    w0_v,
    w1_v,
    w3_v,
    h_v,
    n2_v,
    gu_v,
    act_v,
    dact_v,
    dgu_v,
    hg_v,
    inner_v,
    d1_v,
    d1h_v,
    dz_v,
    l1_v,
    c1_v,
    l2_v,
    c2_v,
    taps_v,
    decay_v,
    draw_v,
    kr_v,
    km_v,
    k4_v,
    us_v,
    um_v,
    u4_v,
    vs_v,
    zs_v,
    s0,
    r0,
    hp0,
    hn0,
    s1,
    r1,
    s2,
    r2,
    s3,
    r3,
    s4,
    r4,
    s5,
    r5,
    s6,
    r6,
    s7,
    r7,
    ps,
    ur,
    ys,
    yr,
    is_,
    vr,
    ds_,
    dmain,
    dhalo,
    wsem,
    ssem,
    mpsem,
    hpsem,
    hnsem,
    seqsem,
    d1sem,
):
    C, M, Q, GL, CP, cpd, F, LEN = dims
    R = SEQS * GL
    PW = C // M
    FW = F // M
    D = C * M
    r = lax.axis_index("seq")
    e = lax.axis_index("mp")
    nxt = lax.rem(r + 1, Q)
    prv = lax.rem(r + Q - 1, Q)
    sends = []

    def send(src, dst, rsem, seq, mp):
        copy = pltpu.make_async_remote_copy(
            src_ref=src,
            dst_ref=dst,
            send_sem=ssem.at[len(sends)],
            recv_sem=rsem,
            device_id={"seq": seq, "mp": mp},
            device_id_type=MESH,
        )
        copy.start()
        sends.append(copy)

    def arrive(dst, rsem):
        pltpu.make_async_remote_copy(
            src_ref=dst,
            dst_ref=dst,
            send_sem=ssem.at[0],
            recv_sem=rsem,
            device_id={"seq": nxt, "mp": e},
            device_id_type=MESH,
        ).wait_recv()

    def swap_blocks(src, dst, phase):
        for d in range(1, M):
            to = lax.rem(e + d, M)
            send(src.at[to], dst.at[e], mpsem.at[phase, e], r, to)
        dst[pl.ds(e, 1)] = src[pl.ds(e, 1)]

    def blocks_arrive(dst, phase):
        for d in range(1, M):
            b = lax.rem(e + M - d, M)
            arrive(dst.at[b], mpsem.at[phase, b])

    def swap_seq(src, dst, phase):
        for d in range(1, Q):
            to = lax.rem(r + d, Q)
            send(src.at[to], dst.at[r], seqsem.at[phase, r], to, e)
        dst[pl.ds(r, 1)] = src[pl.ds(r, 1)]

    def seq_arrive(dst, phase):
        for d in range(1, Q):
            b = lax.rem(r + Q - d, Q)
            arrive(dst.at[b], seqsem.at[phase, b])

    def pieces(dst, values, width):
        for b in range(M):
            dst[b, 0:width] = values[width * b : width * (b + 1)]

    def joined(src, width):
        return jnp.concatenate([src[b, 0:width] for b in range(M)], axis=0)

    def extra(src):
        total = src[0, PW : PW + 8]
        for b in range(1, M):
            total = total + src[b, PW : PW + 8]
        return total[0:1]

    def by_channel(dst, values):
        if CP == cpd:
            dst[...] = values.reshape(Q, CP, values.shape[1])
        else:
            dst[...] = jnp.zeros(dst.shape, jnp.float32)
            for q in range(Q):
                dst[q, 0:cpd] = values[q * cpd : (q + 1) * cpd]

    def from_channels(src):
        if CP == cpd:
            return src[...].reshape(Q * CP, R)
        return jnp.concatenate([src[q, 0:cpd] for q in range(Q)], axis=0)

    copies = [
        pltpu.make_async_copy(src, dst, wsem.at[i])
        for i, (src, dst) in enumerate(
            ((sq_hbm, sq_v), (dl_hbm, dl_v), (inl_hbm, inl_v), (ul_hbm, ul_v), (dr_hbm, dr_v))
        )
    ]
    for copy in copies:
        copy.start()
    barrier = pltpu.get_barrier_semaphore()
    partners = [(lax.rem(r + d, Q), e) for d in range(1, Q)]
    partners += [(r, lax.rem(e + d, M)) for d in range(1, M)]
    partners += [(s, lax.rem(e + d, M)) for s in (nxt, prv) for d in range(1, M)]
    for seq, mp in partners:
        pl.semaphore_signal(
            barrier, inc=1, device_id={"seq": seq, "mp": mp}, device_id_type=MESH
        )

    lane = lax.broadcasted_iota(jnp.int32, (1, R), 1)
    spot = lax.rem(lane, GL)
    first_bin = spot == 0
    flip = jnp.where(lax.rem(spot, 2) == 0, 1.0, -1.0).astype(jnp.float32)
    keep_bin = jnp.where(first_bin, 0.0, 1.0).astype(jnp.float32)
    length_of = jnp.where(lane < GL, len_ref[0], len_ref[1])
    position = r * GL + spot
    valid = (position < length_of).astype(jnp.float32)
    valid_next = (position + GL < length_of).astype(jnp.float32)
    has_prev = (r > 0).astype(jnp.float32)
    has_next = (r < Q - 1).astype(jnp.float32)
    tail = spot >= GL - 2
    head = spot < 2
    halo_mask = jnp.where(tail, has_prev, jnp.where(head, has_next, 0.0))

    xt_v[...] = x_ref[...].T
    vecp_v[...] = jnp.zeros(vecp_v.shape, jnp.float32)
    vecp_v[0 : 4 + 3 * KS] = vec_ref[...]
    vt_v[...] = vecp_v[...].T

    def column(k):
        return vt_v[:, k : k + 1]

    xt = xt_v[...]
    u0 = xt * column(0)
    u0_v[...] = u0
    copies[0].wait()
    pieces(s0, tn(sq_v[0], u0), PW)
    squares = jnp.broadcast_to(jnp.sum(xt * xt, axis=0, keepdims=True), (8, R))
    for b in range(M):
        s0[b, PW : PW + 8] = squares
    pl.semaphore_wait(barrier, len(partners))
    swap_blocks(s0, r0, 0)
    for d in range(M):
        to = lax.rem(e + d, M)
        send(s0.at[to], hp0.at[e], hpsem.at[e], nxt, to)
        send(s0.at[to], hn0.at[e], hnsem.at[e], prv, to)

    ogt_v[...] = og_ref[...].T
    copies[1].wait()
    pieces(s4, nn(dl_v[...], ogt_v[...]), FW)
    swap_blocks(s4, r4, 4)
    by_channel(vtc_v, vt_v[...])
    by_channel(foc_v, fo_ref[...].T)
    copies[2].wait()

    blocks_arrive(r0, 0)
    for d in range(M):
        b = lax.rem(e + d, M)
        arrive(hp0.at[b], hpsem.at[b])
        arrive(hn0.at[b], hnsem.at[b])
    scale_one = lax.rsqrt(extra(r0) / D + norm_epsilon)
    w0 = joined(r0, PW)
    w0_v[...] = w0
    z = tn(inl_v[...], w0) * scale_one
    w0h = jnp.where(tail, joined(hp0, PW), joined(hn0, PW))
    scale_halo = lax.rsqrt(jnp.where(tail, extra(hp0), extra(hn0)) / D + norm_epsilon) * halo_mask
    zh = tn(inl_v[...], w0h) * scale_halo
    zh_far = pltpu.roll(zh, GL, 1)
    z_v[...] = z
    z1_v[...] = pltpu.roll(jnp.where(spot >= GL - 1, zh_far, z), 1, 1)
    z2_v[...] = pltpu.roll(jnp.where(tail, zh_far, z), 2, 1)
    for s in range(3):
        part = slice(s * C, (s + 1) * C)
        conv_v[part] = (
            column(4 + KS * s) * z_v[part]
            + column(5 + KS * s) * z1_v[part]
            + column(6 + KS * s) * z2_v[part]
        )
    product = conv_v[0:C] * conv_v[2 * C : 3 * C] * valid
    prod_v[...] = product
    by_channel(ps, product)
    swap_seq(ps, ur, 0)

    z_far = pltpu.roll(z, GL, 1)
    ahead_one = pltpu.roll(jnp.where(spot >= GL - 1, z_far, zh), 1, 1)
    ahead_two = pltpu.roll(jnp.where(tail, z_far, zh), 2, 1)
    for s in (0, 2):
        part = slice(s * C, (s + 1) * C)
        convh_v[part] = (
            column(4 + KS * s) * zh[part]
            + column(5 + KS * s) * ahead_one[part]
            + column(6 + KS * s) * ahead_two[part]
        )

    pre = filter_frequency * nn(feat_ref[...], fh_ref[0:8], HIGHEST)
    l1_v[...] = jnp.sin(pre)
    c1_v[...] = filter_frequency * jnp.cos(pre)
    pre = filter_frequency * nn(l1_v[...], fh_ref[EMB : EMB + 128], HIGHEST)
    l2_v[...] = jnp.sin(pre)
    c2_v[...] = filter_frequency * jnp.cos(pre)
    foc = foc_v[pl.ds(r, 1)].reshape(CP, 128)
    vtc = vtc_v[pl.ds(r, 1)].reshape(CP, 128)
    rate = vtc[:, 2:3]
    skip_channel = vtc[:, 3:4]
    shaped = nt(foc, l2_v[...], HIGHEST)
    part_lane = lax.broadcasted_iota(jnp.int32, (1, GL), 1)
    for q in range(Q):
        fraction = (part_lane + q * GL).astype(jnp.float32) / LEN
        decay = jnp.exp(-fraction * rate) * (LEN ** (-0.5))
        decay_v[q] = decay
        taps_v[q] = shaped[:, q * GL : (q + 1) * GL] * decay
    spectrum = nn(taps_v[...].reshape(Q * CP, GL), ttap_ref[...]).reshape(Q, CP, 2 * R)
    for q in range(Q):
        real = spectrum[q, :, 0:R]
        imag = spectrum[q, :, R : 2 * R]
        if q > 0:
            real = real + flip * spectrum[q - 1, :, 0:R]
            imag = imag + flip * spectrum[q - 1, :, R : 2 * R]
        kr_v[q] = real
        km_v[q] = imag * keep_bin
        k4_v[q] = jnp.where(first_bin, imag, real)

    def total_pairs(count, first, term):
        zero = jnp.zeros((CP, R), jnp.float32)
        if Q <= 8:
            real, imag = zero, zero
            for i in range(count):
                add_real, add_imag = term(first + i)
                real, imag = real + add_real, imag + add_imag
            return real, imag

        def body(i, kept):
            add_real, add_imag = term(first + i)
            return (kept[0] + add_real, kept[1] + add_imag)

        return lax.fori_loop(0, count, body, (zero, zero))

    def each_block(body):
        if Q <= 8:
            for q in range(Q):
                body(q)
        else:

            @pl.loop(0, Q)
            def _(q):
                body(q)

    seq_arrive(ur, 0)
    us_v[...] = nn(ur[...].reshape(Q * CP, R), tfwd_ref[...]).reshape(Q, CP, 2 * R)

    def forward_block(p):
        def term(q):
            real = us_v[q, :, 0:R]
            imag = us_v[q, :, R : 2 * R]
            lag = p - q
            return (
                kr_v[lag] * real - km_v[lag] * imag,
                km_v[lag] * real + k4_v[lag] * imag,
            )

        real, imag = total_pairs(p + 1, 0, term)
        zs_v[p, :, 0:R] = real
        zs_v[p, :, R : 2 * R] = imag

    each_block(forward_block)
    ys[...] = nn(zs_v[...].reshape(Q * CP, 2 * R), tinv_ref[...]).reshape(Q, CP, R)
    swap_seq(ys, yr, 1)
    for q in range(Q):
        real = us_v[q, :, 0:R]
        imag = us_v[q, :, R : 2 * R]
        um_v[q] = imag * keep_bin
        u4_v[q] = jnp.where(first_bin, imag, real)

    seq_arrive(yr, 1)
    inner_sum = from_channels(yr) + column(3) * prod_v[...]
    insum_v[...] = inner_sum
    gated = conv_v[C : 2 * C] * inner_sum
    gated_v[...] = gated
    pieces(s1, tn(sq_v[1], gated), PW)
    swap_blocks(s1, r1, 1)

    copies[4].wait()
    blocks_arrive(r4, 4)
    dact_v[...] = nn(dr_v[...], r4[...].reshape(F, R))
    copies[3].wait()

    blocks_arrive(r1, 1)
    w1 = r1[...].reshape(C, R)
    w1_v[...] = w1
    h = xt_v[...] + tn(sq_v[2], w1)
    h_v[...] = h
    u3 = h * column(1)
    pieces(s2, tn(sq_v[3], u3), PW)
    squares = jnp.broadcast_to(jnp.sum(h * h, axis=0, keepdims=True), (8, R))
    for b in range(M):
        s2[b, PW : PW + 8] = squares
    swap_blocks(s2, r2, 2)

    blocks_arrive(r2, 2)
    scale_two = lax.rsqrt(extra(r2) / D + norm_epsilon)
    n2_v[...] = h_v[...] * scale_two
    w3 = joined(r2, PW)
    w3_v[...] = w3
    gu_v[...] = tn(ul_v[...], w3) * scale_two
    gate = gu_v[0:F]
    up = gu_v[F : 2 * F]
    bend = jnp.tanh(gelu_scale * (gate + gelu_cubic * gate * gate * gate))
    gelu = 0.5 * gate * (1.0 + bend)
    slope = 0.5 * (1.0 + bend) + 0.5 * gate * (1.0 - bend * bend) * gelu_scale * (
        1.0 + 3.0 * gelu_cubic * gate * gate
    )
    dact = dact_v[...]
    act_v[...] = gelu * up
    dgu_v[0:F] = dact * up * slope
    dgu_v[F : 2 * F] = dact * gelu
    back = nn(ul_v[...], dgu_v[...])
    pieces(s5, back, PW)
    inner = jnp.broadcast_to(jnp.sum(back * w3_v[...], axis=0, keepdims=True), (8, R))
    for b in range(M):
        s5[b, PW : PW + 8] = inner
    swap_blocks(s5, r5, 5)
    pieces(s3, tn(dr_v[...], act_v[...]), FW)
    swap_blocks(s3, r3, 3)

    blocks_arrive(r5, 5)
    back = joined(r5, PW)
    inner = extra(r5)
    grad_two = nn(sq_v[3], back)
    hidden_grad = (
        ogt_v[...]
        + scale_two * (grad_two * column(1))
        - h_v[...] * (scale_two * scale_two * scale_two * inner / D)
    )
    hg_v[...] = hidden_grad
    pieces(s6, nn(sq_v[2], hidden_grad), PW)
    swap_blocks(s6, r6, 6)
    gsq_ref[3] = nt(n2_v[...] * column(1), back)
    gain_two = jnp.sum(grad_two * n2_v[...], axis=1, keepdims=True)
    gsq_ref[2] = nt(w1_v[...], hg_v[...])

    blocks_arrive(r6, 6)
    back = r6[...].reshape(C, R)
    gated_grad = nn(sq_v[1], back)
    inner_grad = gated_grad * conv_v[C : 2 * C]
    inner_v[...] = inner_grad
    d1_v[...] = gated_grad * insum_v[...]
    by_channel(is_, inner_grad)
    swap_seq(is_, vr, 2)
    send(d1_v, d1h_v, d1sem, prv, e)
    gsq_ref[1] = nt(gated_v[...], back)
    skip_total = jnp.sum(inner_grad * prod_v[...], axis=1, keepdims=True)
    gdr_ref[...] = nt(act_v[...], r4[...].reshape(F, R))

    seq_arrive(vr, 2)
    vs_v[...] = nn(vr[...].reshape(Q * CP, R), tfwd_ref[...]).reshape(Q, CP, 2 * R)

    def back_block(q):
        def term(p):
            real = vs_v[p, :, 0:R]
            imag = vs_v[p, :, R : 2 * R]
            lag = p - q
            return (
                kr_v[lag] * real + km_v[lag] * imag,
                k4_v[lag] * imag - km_v[lag] * real,
            )

        real, imag = total_pairs(Q - q, q, term)
        zs_v[q, :, 0:R] = real
        zs_v[q, :, R : 2 * R] = imag

    each_block(back_block)
    ds_[...] = (
        nn(zs_v[...].reshape(Q * CP, 2 * R), tinv_ref[...]).reshape(Q, CP, R)
        + skip_channel[None] * vr[...]
    )
    swap_seq(ds_, dmain, 3)
    for d in range(Q):
        p = lax.rem(r + d, Q)
        to = lax.rem(r + d + Q - 1, Q)
        if d == 1:
            dhalo[pl.ds(r, 1)] = ds_[pl.ds(p, 1)]
        else:
            send(ds_.at[p], dhalo.at[r], seqsem.at[4, r], to, e)

    def lag_block(j):
        def term(p):
            real = vs_v[p, :, 0:R]
            imag = vs_v[p, :, R : 2 * R]
            q = p - j
            return (
                us_v[q, :, 0:R] * real + um_v[q] * imag,
                u4_v[q] * imag - um_v[q] * real,
            )

        real, imag = total_pairs(Q - j, j, term)
        zs_v[j, :, 0:R] = real
        zs_v[j, :, R : 2 * R] = imag

    each_block(lag_block)
    cross = zs_v[...].reshape(Q * CP, 2 * R)
    near = nn(cross, tw1_ref[...]).reshape(Q, CP, GL)
    far = nn(cross, tw2_ref[...]).reshape(Q, CP, GL)
    decay_total = jnp.zeros((CP, 1), jnp.float32)
    for q in range(Q):
        grad = near[q]
        if q < Q - 1:
            grad = grad + far[q + 1]
        fraction = (part_lane + q * GL).astype(jnp.float32) / LEN
        decay_total = decay_total - jnp.sum(
            grad * taps_v[q] * fraction, axis=1, keepdims=True
        )
        draw_v[:, q * GL : (q + 1) * GL] = grad * decay_v[q]
    raw = draw_v[...]
    gfo_ref[...] = jnp.zeros(gfo_ref.shape, jnp.float32)
    gdec_ref[...] = jnp.zeros(gdec_ref.shape, jnp.float32)
    gfo_ref[pl.ds(r, 1)] = nn(raw, l2_v[...]).reshape(1, CP, 128)
    gdec_ref[pl.ds(r, 1)] = jnp.broadcast_to(decay_total, (CP, 128)).reshape(1, CP, 128)
    back = tn(raw, foc) * c2_v[...]
    gw2_ref[...] = tn(l1_v[...], back)
    back = nt(back, fh_ref[EMB : EMB + 128]) * c1_v[...]
    gw1_ref[...] = tn(feat_ref[...], back)

    blocks_arrive(r3, 3)
    w4 = r3[...].reshape(F, R)
    bo_ref[...] = (h_v[...] + tn(dl_v[...], w4)).T
    gdl_ref[...] = nt(w4, ogt_v[...])
    gul_ref[...] = nt(w3_v[...] * scale_two, dgu_v[...])

    seq_arrive(dmain, 3)
    for d in range(1, Q):
        b = lax.rem(r + Q - d, Q)
        arrive(dhalo.at[b], seqsem.at[4, b])
    arrive(d1h_v, d1sem)
    product_grad = from_channels(dmain) * valid
    product_next = from_channels(dhalo) * valid_next
    grads = (product_grad * conv_v[2 * C : 3 * C], d1_v[...], product_grad * conv_v[0:C])
    nexts = (
        product_next * convh_v[2 * C : 3 * C],
        d1h_v[...] * has_next,
        product_next * convh_v[0:C],
    )
    tap_totals = []
    for s in range(3):
        part = slice(s * C, (s + 1) * C)
        grad = grads[s]
        following = pltpu.roll(nexts[s], GL, 1)
        one = pltpu.roll(jnp.where(spot == 0, following, grad), R - 1, 1)
        two = pltpu.roll(jnp.where(head, following, grad), R - 2, 1)
        dz_v[part] = (
            column(4 + KS * s) * grad + column(5 + KS * s) * one + column(6 + KS * s) * two
        )
        for shifted in (z_v, z1_v, z2_v):
            tap_totals.append(jnp.sum(grad * shifted[part], axis=1, keepdims=True))
    back = nn(inl_v[...], dz_v[...])
    pieces(s7, back, PW)
    inner = jnp.broadcast_to(jnp.sum(back * w0_v[...], axis=0, keepdims=True), (8, R))
    for b in range(M):
        s7[b, PW : PW + 8] = inner
    swap_blocks(s7, r7, 7)
    ginl_ref[...] = nt(w0_v[...] * scale_one, dz_v[...])

    blocks_arrive(r7, 7)
    back = joined(r7, PW)
    inner = extra(r7)
    grad_one = nn(sq_v[0], back)
    xt = xt_v[...]
    ig_ref[...] = (
        hg_v[...]
        + scale_one * (grad_one * column(0))
        - xt * (scale_one * scale_one * scale_one * inner / D)
    ).T
    gsq_ref[0] = nt(u0_v[...] * scale_one, back)
    gain_one = jnp.sum(grad_one * xt * scale_one, axis=1, keepdims=True)
    slot = lax.broadcasted_iota(jnp.int32, (1, 128), 1)
    rows = {0: gain_one, 1: gain_two, 3: skip_total}
    rows.update({4 + k: total for k, total in enumerate(tap_totals)})
    stacked = jnp.zeros((C, 128), jnp.float32)
    for k, total in rows.items():
        stacked = jnp.where(slot == k, total, stacked)
    gvec_ref[...] = stacked.T[0:16]
    for copy in sends:
        copy.wait_send()


def run_chain(x, og, lengths, sq, inl, ul, dr, dl, vectors, fh, fo):
    M, Q = lax.axis_size("mp"), lax.axis_size("seq")
    _, GL, C = x.shape
    R = SEQS * GL
    F = dr.shape[0]
    LEN = GL * Q
    cpd = C // Q
    CP = -(-cpd // 8) * 8
    PW, FW = C // M, F // M
    dims = (C, M, Q, GL, CP, cpd, F, LEN)
    tables = spectrum_tables(GL)
    feat = feature_table(LEN)
    sds = lambda *shape: jax.ShapeDtypeStruct(shape, jnp.float32)
    v = lambda *shape: pltpu.VMEM(shape, jnp.float32)
    outs = (
        sds(R, C),
        sds(R, C),
        sds(4, C, C),
        sds(C, 3 * C),
        sds(C, 2 * F),
        sds(F, F),
        sds(F, C),
        sds(16, C),
        sds(Q, CP, 128),
        sds(Q, CP, 128),
        sds(8, 128),
        sds(128, 128),
    )
    scratch = [
        v(4, C, C),
        v(C, 3 * C),
        v(C, 2 * F),
        v(F, F),
        v(F, C),
        v(128, C),
        v(C, 128),
        v(Q, CP, 128),
        v(Q, CP, 128),
        v(C, R),
        v(C, R),
        v(C, R),
        v(3 * C, R),
        v(3 * C, R),
        v(3 * C, R),
        v(3 * C, R),
        v(3 * C, R),
        v(C, R),
        v(C, R),
        v(C, R),
        v(C, R),
        v(C, R),
        v(C, R),
        v(C, R),
        v(C, R),
        v(2 * F, R),
        v(F, R),
        v(F, R),
        v(2 * F, R),
        v(C, R),
        v(C, R),
        v(C, R),
        v(C, R),
        v(3 * C, R),
        v(LEN, 128),
        v(LEN, 128),
        v(LEN, 128),
        v(LEN, 128),
        v(Q, CP, GL),
        v(Q, CP, GL),
        v(CP, LEN),
        v(Q, CP, R),
        v(Q, CP, R),
        v(Q, CP, R),
        v(Q, CP, 2 * R),
        v(Q, CP, R),
        v(Q, CP, R),
        v(Q, CP, 2 * R),
        v(Q, CP, 2 * R),
    ]
    scratch += [v(M, PW + 8, R)] * 4
    scratch += [v(M, PW, R)] * 2
    scratch += [v(M, PW + 8, R)] * 2
    scratch += [v(M, FW, R)] * 4
    scratch += [v(M, PW + 8, R)] * 2
    scratch += [v(M, PW, R)] * 2
    scratch += [v(M, PW + 8, R)] * 2
    scratch += [v(Q, CP, R)] * 9
    sends = 8 * (M - 1) + 2 * M + 5 * (Q - 1) + 1
    scratch += [
        pltpu.SemaphoreType.DMA((5,)),
        pltpu.SemaphoreType.DMA((sends,)),
        pltpu.SemaphoreType.DMA((8, M)),
        pltpu.SemaphoreType.DMA((M,)),
        pltpu.SemaphoreType.DMA((M,)),
        pltpu.SemaphoreType.DMA((5, Q)),
        pltpu.SemaphoreType.DMA,
    ]
    vmem = pl.BlockSpec(memory_space=pltpu.VMEM)
    smem = pl.BlockSpec(memory_space=pltpu.SMEM)
    hbm = pl.BlockSpec(memory_space=pl.ANY)
    return pl.pallas_call(
        functools.partial(chain_kernel, dims),
        out_shape=outs,
        in_specs=[vmem, vmem, smem] + [vmem] * 9 + [hbm] * 5,
        out_specs=[vmem] * len(outs),
        scratch_shapes=scratch,
        compiler_params=pltpu.CompilerParams(
            collective_id=0, has_side_effects=True, vmem_limit_bytes=58 * 2**20
        ),
        name="chain",
    )(
        x.reshape(R, C),
        og.reshape(R, C),
        lengths,
        vectors,
        fh,
        fo,
        feat,
        *tables,
        sq,
        inl,
        ul,
        dr,
        dl,
    )


def halves(values):
    high = values.astype(jnp.bfloat16)
    return high, (values - high.astype(jnp.float32)).astype(jnp.bfloat16)


def thrice(left, right, product):
    a, b = left
    c, d = right
    plain = lambda m, n: product(m, n, None)
    return plain(a, c) + plain(a, d) + plain(b, c)


def unit_scale(values):
    return 1.0 / (jnp.sqrt(jnp.sum(values * values)) + 1e-07)


def polynomial(gram, precision):
    return schulz_second * gram + schulz_third * nn(gram, gram, precision)


def square_schulz(current):
    for _ in range(5):
        gram = nt(current, current)
        current = schulz_first * current + nn(polynomial(gram, HIGH), current)
    return current


def gram_schulz(gram):
    size = gram.shape[0]
    eye = (
        lax.broadcasted_iota(jnp.int32, (size, size), 0)
        == lax.broadcasted_iota(jnp.int32, (size, size), 1)
    ).astype(jnp.float32)
    total = None
    for step in range(5):
        factor = schulz_first * eye + polynomial(gram, HIGHEST)
        total = factor if total is None else nn(total, factor, HIGHEST)
        if step < 4:
            gram = nn(nn(gram, factor, HIGHEST), factor, HIGHEST)
    return total


def muon_kernel(
    gsq,
    ginl,
    gul,
    gdr,
    gdl,
    psq,
    pinl,
    pul,
    pdr,
    pdl,
    wsq,
    winl,
    wul,
    wdr,
    wdl,
    msq,
    nsq,
    csq,
    minl,
    ninl,
    cinl,
    mul,
    nul,
    cul,
    mdr,
    ndr,
    cdr,
    mdl,
    ndl,
    cdl,
    x_v,
    xh,
    xl,
    a_v,
    ah,
    al,
    ph,
    pl_,
):
    def finish(weights, orthogonal, rows, cols, new_ref, copy_ref, index=...):
        new = weights - muon_rate * math.sqrt(max(rows, cols) / rows) * orthogonal
        new_ref[index] = new
        copy_ref[index] = new.astype(jnp.bfloat16)

    for k in range(4):
        moment = momentum_decay * psq[k] + gsq[k]
        msq[k] = moment
        size = moment.shape[0]
        finish(wsq[k], square_schulz(moment * unit_scale(moment)), size, size, nsq, csq, k)
    for p_ref, g_ref, w_ref, m_ref, n_ref, c_ref in (
        (pinl, ginl, winl, minl, ninl, cinl),
        (pul, gul, wul, mul, nul, cul),
        (pdl, gdl, wdl, mdl, ndl, cdl),
    ):
        moment = momentum_decay * p_ref[...] + g_ref[...]
        m_ref[...] = moment
        start = moment * unit_scale(moment)
        rows, cols = moment.shape
        if rows > cols:
            orthogonal = nn(start, gram_schulz(tn(start, start, HIGHEST)))
        else:
            orthogonal = nn(gram_schulz(nt(start, start, HIGHEST)), start)
        finish(w_ref[...], orthogonal, rows, cols, n_ref, c_ref)

    moment = momentum_decay * pdr[...] + gdr[...]
    mdr[...] = moment
    x_v[...] = moment * unit_scale(moment)
    size = x_v.shape[0]
    tile = 256
    tiles = size // tile

    def spread(i):
        rows = pl.ds(pl.multiple_of(i * tile, tile), tile)
        xh[rows], xl[rows] = halves(x_v[rows])

    pl.loop(0, tiles)(spread)

    @pl.loop(0, 5)
    def _(step):
        @pl.loop(0, tiles)
        def _(i):
            rows = pl.ds(pl.multiple_of(i * tile, tile), tile)
            gram = thrice((xh[rows], xl[rows]), (xh[...], xl[...]), nt)
            a_v[rows] = gram
            ah[rows], al[rows] = halves(gram)

        @pl.loop(0, tiles)
        def _(i):
            rows = pl.ds(pl.multiple_of(i * tile, tile), tile)
            squared = thrice((ah[rows], al[rows]), (ah[...], al[...]), nn)
            ph[rows], pl_[rows] = halves(schulz_second * a_v[rows] + schulz_third * squared)

        @pl.loop(0, tiles)
        def _(i):
            rows = pl.ds(pl.multiple_of(i * tile, tile), tile)
            x_v[rows] = schulz_first * x_v[rows] + thrice(
                (ph[rows], pl_[rows]), (xh[...], xl[...]), nn
            )

        pl.loop(0, tiles)(spread)

    finish(wdr[...], x_v[...], size, size, ndr, cdr)


def run_muon(gradients, moments, weights):
    shapes = [g.shape for g in gradients]
    outs = []
    for shape in shapes:
        outs += [
            jax.ShapeDtypeStruct(shape, jnp.float32),
            jax.ShapeDtypeStruct(shape, jnp.float32),
            jax.ShapeDtypeStruct(shape, jnp.bfloat16),
        ]
    big = shapes[3]
    wide = pltpu.VMEM(big, jnp.float32)
    half = pltpu.VMEM(big, jnp.bfloat16)
    vmem = pl.BlockSpec(memory_space=pltpu.VMEM)
    return pl.pallas_call(
        muon_kernel,
        out_shape=outs,
        in_specs=[vmem] * 15,
        out_specs=[vmem] * 15,
        scratch_shapes=[wide, half, half, wide, half, half, half, half],
        compiler_params=pltpu.CompilerParams(vmem_limit_bytes=58 * 2**20),
        name="muon",
    )(*gradients, *moments, *weights)


def adam_update(weights, first, second, gradient, rate):
    first_new = beta_first * first + (1.0 - beta_first) * gradient
    second_new = beta_second * second + (1.0 - beta_second) * gradient * gradient
    corrected_first = first_new / (1.0 - beta_first**STEP)
    corrected_second = second_new / (1.0 - beta_second**STEP)
    new_weights = weights - rate * (
        corrected_first / (jnp.sqrt(corrected_second) + adam_epsilon) + weight_decay * weights
    )
    return (first_new, second_new, new_weights, new_weights.astype(jnp.bfloat16))


def per_device(
    block_input,
    out_grad,
    lengths,
    square_factors,
    square_moment,
    input_left,
    input_left_moment,
    up_left,
    up_left_moment,
    down_right,
    down_right_moment,
    down_left,
    down_left_moment,
    vectors,
    vectors_first,
    vectors_second,
    filter_hidden,
    hidden_first,
    hidden_second,
    filter_out,
    filter_out_first,
    filter_out_second,
):
    C = block_input.shape[2]
    Q = lax.axis_size("seq")
    cpd = C // Q
    weights = (square_factors[:, 0], input_left[0], up_left[0], down_right[0], down_left[0])
    moments = (
        square_moment[:, 0],
        input_left_moment[0],
        up_left_moment[0],
        down_right_moment[0],
        down_left_moment[0],
    )
    block_output, input_grad, *rest = run_chain(
        block_input, out_grad, lengths, *weights, vectors, filter_hidden, filter_out
    )
    gradients = rest[:5]
    gvec, gfo, gdec, gw1, gw2 = rest[5:]
    gradients, gvec, gfo, gdec = lax.psum((gradients, gvec, gfo, gdec), "seq")
    gw1, gw2 = lax.psum((gw1, gw2), ("seq", "mp"))
    hidden_total = jnp.concatenate([gw1[:EMB], gw2], axis=0)
    filter_out_total = gfo[:, :cpd].reshape(C, 128).T
    decay = gdec[:, :cpd, 0].reshape(C)
    vector_total = jnp.concatenate([gvec[:2], decay[None], gvec[3 : 4 + 3 * KS]], axis=0)
    updated = run_muon(gradients, moments, weights)
    vector_new = adam_update(vectors, vectors_first, vectors_second, vector_total, rate_vectors)
    hidden_new = adam_update(filter_hidden, hidden_first, hidden_second, hidden_total, rate_hidden)
    filter_new = adam_update(
        filter_out, filter_out_first, filter_out_second, filter_out_total, rate_output
    )
    return (
        block_output.reshape(block_input.shape),
        input_grad.reshape(block_input.shape),
        *[v[:, None] for v in updated[:3]],
        *[v[None] for v in updated[3:]],
        *vector_new,
        *hidden_new,
        *filter_new,
    )


def solution(mesh):
    tokens = P(None, "seq", "mp")
    square = P(None, "mp", None, None)
    block = P("mp", None, None)
    row = P(None, "mp")
    return jax.shard_map(
        per_device,
        mesh=mesh,
        in_specs=(tokens, tokens, P(), square, square)
        + (block,) * 8
        + (row,) * 3
        + (P(),) * 3
        + (row,) * 3,
        out_specs=(tokens, tokens)
        + (square,) * 3
        + (block,) * 12
        + (row,) * 4
        + (P(),) * 4
        + (row,) * 4,
        check_vma=False,
    )
```

```python
import functools
import math
import types

import jax
import jax.numpy as jnp
import numpy as np
from jax import lax
from jax.experimental import pallas as pl
from jax.experimental.pallas import tpu as pltpu
from jax.sharding import PartitionSpec as P

EMB = 5
KS = 3
STEP = 10
SEQS = 2

HIGH = lax.Precision.HIGH
HIGHEST = lax.Precision.HIGHEST
MESH = pl.DeviceIdType.MESH
norm_epsilon = 1e-05
beta_first = 0.9
beta_second = 0.95
adam_epsilon = 1e-08
weight_decay = 0.01
rate_vectors = 0.2
rate_hidden = 0.05
rate_output = 0.05
muon_rate = 0.5
momentum_decay = 0.5
schulz_first = 3.4445
schulz_second = -4.775
schulz_third = 2.0315
filter_frequency = 10.0
gelu_scale = math.sqrt(2.0 / math.pi)
gelu_cubic = 0.044715


def contract(a, b, dim_a, dim_b, precision=HIGH):
    return lax.dot_general(
        a,
        b,
        (((dim_a,), (dim_b,)), ((), ())),
        precision=precision,
        preferred_element_type=jnp.float32,
    )


def nn(a, b, precision=HIGH):
    return contract(a, b, 1, 0, precision)


def nt(a, b, precision=HIGH):
    return contract(a, b, 1, 1, precision)


def tn(a, b, precision=HIGH):
    return contract(a, b, 0, 0, precision)


def spectrum_tables(group_len):
    rows = SEQS * group_len
    period = 2 * group_len
    time = np.arange(group_len)
    lags = np.arange(period)
    bins = np.arange(group_len)
    angle = 2.0 * np.pi * (np.outer(time, bins) % period) / period
    real = np.cos(angle)
    imag = -np.sin(angle)
    imag[:, 0] = (-1.0) ** time
    forward = np.zeros((rows, 2 * rows))
    for s in range(SEQS):
        part = slice(s * group_len, (s + 1) * group_len)
        forward[part, part] = real
        forward[part, rows + s * group_len : rows + (s + 1) * group_len] = imag
    of_taps = np.concatenate([real] * SEQS + [imag] * SEQS, axis=1)
    angle = 2.0 * np.pi * (np.outer(bins, lags) % period) / period
    back_real = 2.0 * np.cos(angle) / period
    back_real[0] = 1.0 / period
    back_imag = -2.0 * np.sin(angle) / period
    back_imag[0] = (-1.0) ** lags / period
    inverse = np.zeros((2 * rows, rows))
    for s in range(SEQS):
        part = slice(s * group_len, (s + 1) * group_len)
        inverse[part, part] = back_real[:, :group_len]
        inverse[rows + s * group_len : rows + (s + 1) * group_len, part] = back_imag[:, :group_len]
    window = np.concatenate([back_real] * SEQS + [back_imag] * SEQS, axis=0)
    return tuple(
        v.astype(np.float32)
        for v in (forward, of_taps, inverse, window[:, :group_len], window[:, group_len:])
    )


def feature_table(length):
    fraction = np.arange(length).astype(np.float32) / np.float32(length)
    angle = np.float32(2.0 * math.pi) * fraction
    wide = angle.astype(np.float64)
    twice = (np.float32(2.0) * angle).astype(np.float64)
    columns = [fraction, np.cos(wide), np.sin(wide), np.cos(twice), np.sin(twice)]
    table = np.zeros((length, 8), np.float32)
    for i, column in enumerate(columns):
        table[:, i] = column.astype(np.float32)
    return table


LATE = dict(sq=0, inl=1, vec=2, fo=3, hid=4)


def late_columns(C):
    start = [0, 4 * C, 7 * C, 7 * C + C // 3, 7 * C + C // 3 + 128]
    return start, 7 * C + C // 3 + 256


def when(condition, body):
    if isinstance(condition, bool):
        if condition:
            body()
    else:
        pl.when(condition)(body)


MID_EARLY = 3


class Ring:
    def __init__(self, grad, total, far_slot, near_slot, ssem, rsem, rows, columns, way, place, count, ids):
        self.grad, self.total = grad, total
        self.far_slot, self.near_slot = far_slot, near_slot
        self.ssem, self.rsem = ssem, rsem
        self.stride, self.offset, self.height = rows
        self.columns = columns
        self.sign = 1 if way == 0 else -1
        self.place, self.count = place, count
        self.ahead, self.behind = ids if way == 0 else ids[::-1]

    def part(self, ref, ahead):
        chunk = lax.rem(self.place + self.sign * ahead + 4 * self.count, self.count)
        start = pl.multiple_of(chunk * self.stride + self.offset, 8)
        return ref.at[pl.ds(start, self.height), self.columns]

    def copy(self, source, target, index, to):
        return pltpu.make_async_remote_copy(
            src_ref=source,
            dst_ref=target,
            send_sem=self.ssem.at[index],
            recv_sem=self.rsem.at[index],
            device_id=to,
            device_id_type=MESH,
        )

    def far_sum(self, i):
        n = self.count // 2
        return self.copy(self.part(self.grad, n - i), self.far_slot.at[i], i, self.ahead)

    def near_sum(self, i):
        n = self.count // 2
        source = self.part(self.grad, i - (n - 1))
        return self.copy(source, self.near_slot.at[i], n + i, self.behind)

    def far_total(self, i, hops=0):
        n = self.count // 2
        whole = self.part(self.total, i + hops)
        return self.copy(whole, whole, 2 * n - 1 + i, self.behind)

    def near_total(self, i, hops=0):
        n = self.count // 2
        whole = self.part(self.total, -i - hops)
        return self.copy(whole, whole, 3 * n - 1 + i, self.ahead)

    def begin(self):
        self.far_sum(0).start()
        self.near_sum(0).start()

    def event(self, s):
        n = self.count // 2

        def add_far():
            mine = self.part(self.grad, n - 1 - s)
            mine[...] = mine[...] + self.far_slot[s]
            self.far_sum(s + 1).start()

        def add_near():
            mine = self.part(self.grad, s - (n - 2))
            mine[...] = mine[...] + self.near_slot[s]
            self.near_sum(s + 1).start()

        def turn():
            own = self.part(self.total, 0)
            mine = self.part(self.grad, 0)
            own[...] = mine[...] + self.far_slot[n - 1] + self.near_slot[n - 2]
            self.far_total(0).start()
            self.near_total(0).start()

        both = lambda p, q: p and q if isinstance(p, bool) else p & q
        i = s - n
        when(s < n, lambda: self.far_sum(s).wait_recv())
        when(s < n - 1, add_far)
        when(s < n - 1, lambda: self.near_sum(s).wait_recv())
        when(s < n - 2, add_near)
        when(s == n - 1, turn)
        when(both(s >= n, s < 2 * n), lambda: self.far_total(i, 1).wait_recv())
        when(both(s >= n, s < 2 * n - 1), lambda: self.far_total(i + 1).start())
        when(both(s >= n, s < 2 * n - 1), lambda: self.near_total(i, 1).wait_recv())
        when(both(s >= n, s < 2 * n - 2), lambda: self.near_total(i + 1).start())

    def end(self):
        n = self.count // 2
        for i in range(n):
            self.far_sum(i).wait_send()
            self.far_total(i).wait_send()
        for i in range(n - 1):
            self.near_sum(i).wait_send()
            self.near_total(i).wait_send()


def unit_scale(values):
    return 1.0 / (jnp.sqrt(jnp.sum(values * values)) + 1e-07)


def halves(values):
    high = values.astype(jnp.bfloat16)
    return high, (values - high.astype(jnp.float32)).astype(jnp.bfloat16)


def thrice(left, right, product):
    a, b = left
    c, d = right
    plain = lambda m, n: product(m, n, None)
    return plain(a, c) + plain(a, d) + plain(b, c)


def idle(product):
    pass


def large_schulz(k, between):
    size = k.x.shape[0]
    tile = 256
    strips = [
        (slice(i * tile, (i + 1) * tile), slice(0, (i + 1) * tile)) for i in range(size // tile)
    ]

    def keep(high, low, rows, columns, values):
        high[rows, columns], low[rows, columns] = halves(values)
        if rows.start:
            turned = values[:, 0 : rows.start].T
            high[0 : rows.start, rows], low[0 : rows.start, rows] = halves(turned)

    def newton_step(step):
        k.xh[...], k.xl[...] = halves(k.x[...])
        for i, (rows, columns) in enumerate(strips):
            gram = thrice((k.xh[rows], k.xl[rows]), (k.xh[columns], k.xl[columns]), nt)
            k.a[rows, columns] = gram
            keep(k.ah, k.al, rows, columns, gram)
        between(3 * step)
        for i, (rows, columns) in enumerate(strips):
            squared = thrice(
                (k.ah[rows], k.al[rows]), (k.ah[:, columns], k.al[:, columns]), nn
            )
            values = schulz_second * k.a[rows, columns] + schulz_third * squared
            keep(k.ph, k.pl, rows, columns, values)
        between(3 * step + 1)
        for i in range(2):
            rows = slice(i * size // 2, (i + 1) * size // 2)
            k.x[rows] = schulz_first * k.x[rows] + thrice(
                (k.ph[rows], k.pl[rows]), (k.xh[...], k.xl[...]), nn
            )
        between(3 * step + 2)

    if between is idle:
        pl.loop(0, 5)(newton_step)
    else:
        for step in range(5):
            newton_step(step)


def chain_kernel(dims, names, *refs):
    k = types.SimpleNamespace(**dict(zip(names, refs, strict=True)))
    C, M, Q, GL, CP, cpd, F, LEN, ringed = dims
    R = SEQS * GL
    PW = C // M
    FW = F // M
    D = C * M
    r = lax.axis_index("seq")
    e = lax.axis_index("mp")
    nxt = lax.rem(r + 1, Q)
    prv = lax.rem(r + Q - 1, Q)
    sends = []

    def remote(src, dst, ssem, rsem, seq, mp):
        return pltpu.make_async_remote_copy(
            src_ref=src,
            dst_ref=dst,
            send_sem=ssem,
            recv_sem=rsem,
            device_id={"seq": seq, "mp": mp},
            device_id_type=MESH,
        )

    def send(src, dst, rsem, seq, mp):
        copy = remote(src, dst, k.ssem.at[len(sends)], rsem, seq, mp)
        copy.start()
        sends.append(copy)

    def arrive(dst, rsem):
        pltpu.make_async_remote_copy(
            src_ref=dst,
            dst_ref=dst,
            send_sem=k.ssem.at[0],
            recv_sem=rsem,
            device_id={"seq": nxt, "mp": e},
            device_id_type=MESH,
        ).wait_recv()

    def swap_blocks(src, dst, phase):
        for d in range(1, M):
            to = lax.rem(e + d, M)
            send(src.at[to], dst.at[e], k.mpsem.at[phase, e], r, to)
        dst[pl.ds(e, 1)] = src[pl.ds(e, 1)]

    def blocks_arrive(dst, phase):
        for d in range(1, M):
            b = lax.rem(e + M - d, M)
            arrive(dst.at[b], k.mpsem.at[phase, b])

    def swap_seq(src, dst, phase):
        for d in range(1, Q):
            to = lax.rem(r + d, Q)
            send(src.at[to], dst.at[r], k.seqsem.at[phase, r], to, e)
        dst[pl.ds(r, 1)] = src[pl.ds(r, 1)]

    def seq_arrive(dst, phase):
        for d in range(1, Q):
            b = lax.rem(r + Q - d, Q)
            arrive(dst.at[b], k.seqsem.at[phase, b])

    def pieces(dst, values, width):
        for b in range(M):
            dst[b, 0:width] = values[width * b : width * (b + 1)]

    def joined(src, width):
        return jnp.concatenate([src[b, 0:width] for b in range(M)], axis=0)

    def extra(src):
        total = src[0, PW : PW + 8]
        for b in range(1, M):
            total = total + src[b, PW : PW + 8]
        return total[0:1]

    def by_channel(dst, values):
        if CP == cpd:
            dst[...] = values.reshape(Q, CP, values.shape[1])
        else:
            dst[...] = jnp.zeros(dst.shape, jnp.float32)
            for q in range(Q):
                dst[q, 0:cpd] = values[q * cpd : (q + 1) * cpd]

    def from_channels(src):
        if CP == cpd:
            return src[...].reshape(Q * CP, src.shape[2])
        return jnp.concatenate([src[q, 0:cpd] for q in range(Q)], axis=0)

    copies = [
        pltpu.make_async_copy(src, dst, k.wsem.at[i])
        for i, (src, dst) in enumerate(
            (
                (k.sq_hbm, k.sq),
                (k.dl_hbm, k.dl),
                (k.inl_hbm, k.inl),
                (k.ul_hbm, k.ul),
                (k.dr_hbm, k.dr),
            )
        )
    ]
    if ringed:
        copies.append(pltpu.make_async_copy(k.pdr_hbm, k.x, k.wsem.at[5]))
    for copy in copies:
        copy.start()

    odd = lax.rem(r, 2)
    place = (1 - odd) * (r // 2) + odd * (Q - 1 - r // 2)

    def at_place(p):
        back = p // (Q // 2)
        return (1 - back) * 2 * p + back * (2 * (Q - 1 - p) + 1)

    ring_ids = tuple(
        {"seq": at_place(lax.rem(place + d, Q)), "mp": e} for d in (1, Q - 1)
    )

    barrier = pltpu.get_barrier_semaphore()
    partners = [(lax.rem(r + d, Q), e) for d in range(1, Q)]
    partners += [(r, lax.rem(e + d, M)) for d in range(1, M)]
    partners += [(s, lax.rem(e + d, M)) for s in (nxt, prv) for d in range(1, M)]
    for seq, mp in partners:
        pl.semaphore_signal(
            barrier, inc=1, device_id={"seq": seq, "mp": mp}, device_id_type=MESH
        )

    first_rings, other_rings, late_rings = [], [], []
    if ringed:

        def ring(grad, total, slots, rows, columns, way, index):
            return Ring(
                grad,
                total,
                *slots,
                k.ring_ssem.at[index],
                k.ring_rsem.at[index],
                rows,
                columns,
                way,
                place,
                Q,
                ring_ids,
            )

        tall, low = F // Q, C // Q
        for way in range(2):
            rows = (tall, way * (tall // 2), tall // 2)
            slots = (k.far_dr.at[way], k.near_dr.at[way])
            first_rings.append(ring(k.gdr, k.tdr, slots, rows, slice(0, F), way, way))
        for rings, grad, total, slots, index in (
            (
                other_rings,
                k.gmid,
                k.tmid,
                ((k.far_mid0, k.near_mid0), (k.far_mid1, k.near_mid1)),
                2,
            ),
            (
                late_rings,
                k.glate,
                k.tlate,
                ((k.far_late0, k.near_late0), (k.far_late1, k.near_late1)),
                4,
            ),
        ):
            width = grad.shape[1]
            cut = width // 256 * 128
            for way, columns in enumerate((slice(0, cut), slice(cut, width))):
                rows = (low, 0, low)
                rings.append(ring(grad, total, slots[way], rows, columns, way, index + way))

    def go(rings, s):
        for one in rings:
            one.event(s)

    halves_done = [0, 0]

    def first_halves(count):
        if ringed:
            for _ in range(count):
                i = halves_done[0]
                first_rings[i % 2].event(i // 2)
                halves_done[0] += 1

    def mid_half():
        if ringed:
            i = halves_done[1]
            other_rings[i % 2].event(i // 2)
            halves_done[1] += 1

    lane = lax.broadcasted_iota(jnp.int32, (1, R), 1)
    spot = lax.rem(lane, GL)
    first_bin = spot == 0
    flip = jnp.where(lax.rem(spot, 2) == 0, 1.0, -1.0).astype(jnp.float32)
    keep_bin = jnp.where(first_bin, 0.0, 1.0).astype(jnp.float32)
    length_of = jnp.where(lane < GL, k.lengths[0], k.lengths[1])
    position = r * GL + spot
    valid = (position < length_of).astype(jnp.float32)
    has_prev = (r > 0).astype(jnp.float32)
    has_next = (r < Q - 1).astype(jnp.float32)
    tail = spot >= GL - 2
    head = spot < 2
    halo_mask = jnp.where(tail, has_prev, jnp.where(head, has_next, 0.0))
    end_row = lax.broadcasted_iota(jnp.int32, (8, R), 0)
    end_lane = lax.rem(end_row, 4) // 2 * GL + lax.rem(end_row, 2)
    end_lane = end_lane + jnp.where(end_row < 4, 0, GL - 2)
    ends = (lax.broadcasted_iota(jnp.int32, (8, R), 1) == end_lane).astype(jnp.float32)

    k.xt[...] = k.block_in[...].T
    k.vecp[...] = jnp.zeros(k.vecp.shape, jnp.float32)
    k.vecp[0 : 4 + 3 * KS] = k.vec[...]
    k.vt[...] = k.vecp[...].T

    def column(i):
        return k.vt[:, i : i + 1]

    xt = k.xt[...]
    u0 = xt * column(0)
    k.u0[...] = u0
    copies[0].wait()
    pieces(k.s0, tn(k.sq[0], u0), PW)
    squares = jnp.broadcast_to(jnp.sum(xt * xt, axis=0, keepdims=True), (8, R))
    for b in range(M):
        k.s0[b, PW : PW + 8] = squares
    pl.semaphore_wait(barrier, len(partners))
    swap_blocks(k.s0, k.r0, 0)
    for b in range(M):
        k.hs0[b, :, 0 : PW + 8] = nt(ends, k.s0[b], HIGHEST)
    halo_after, halo_before = [], []
    for d in range(M):
        to = lax.rem(e + d, M)
        halo_after.append(
            remote(k.hs0.at[to], k.hp0.at[e], k.hsem.at[0, d], k.hpsem.at[e], nxt, to)
        )
        halo_before.append(
            remote(k.hs0.at[to], k.hn0.at[e], k.hsem.at[1, d], k.hnsem.at[e], prv, to)
        )

    @pl.when(r < Q - 1)
    def _():
        for copy in halo_after:
            copy.start()

    @pl.when(r > 0)
    def _():
        for copy in halo_before:
            copy.start()

    @pl.when(r == 0)
    def _():
        k.hp0[...] = jnp.zeros(k.hp0.shape, jnp.float32)

    @pl.when(r == Q - 1)
    def _():
        k.hn0[...] = jnp.zeros(k.hn0.shape, jnp.float32)

    k.ogt[...] = k.out_grad[...].T
    copies[1].wait()
    pieces(k.s4, tn(k.dl[...], k.ogt[...]), FW)
    swap_blocks(k.s4, k.r4, 4)
    by_channel(k.vtc, k.vt[...])
    by_channel(k.foc, k.fo[...])
    copies[2].wait()

    blocks_arrive(k.r0, 0)

    @pl.when(r > 0)
    def _():
        for d in range(M):
            b = lax.rem(e + d, M)
            arrive(k.hp0.at[b], k.hpsem.at[b])

    @pl.when(r < Q - 1)
    def _():
        for d in range(M):
            b = lax.rem(e + d, M)
            arrive(k.hn0.at[b], k.hnsem.at[b])

    scale_one = lax.rsqrt(extra(k.r0) / D + norm_epsilon)
    w0 = joined(k.r0, PW)
    k.w0[...] = w0
    z = tn(k.inl[...], w0) * scale_one
    first_half = lax.broadcasted_iota(jnp.int32, (8, 128), 0) < 4
    spread = [
        tn(jnp.where(first_half, k.hn0[b], k.hp0[b]), ends, HIGHEST) for b in range(M)
    ]
    w0h = jnp.concatenate([one[0:PW] for one in spread], axis=0)
    squares = spread[0][PW : PW + 1]
    for b in range(1, M):
        squares = squares + spread[b][PW : PW + 1]
    zh = tn(k.inl[...], w0h) * (lax.rsqrt(squares / D + norm_epsilon) * halo_mask)
    zh_far = pltpu.roll(zh, GL, 1)
    k.z[...] = z
    k.z1[...] = pltpu.roll(jnp.where(spot >= GL - 1, zh_far, z), 1, 1)
    k.z2[...] = pltpu.roll(jnp.where(tail, zh_far, z), 2, 1)
    for s in range(3):
        part = slice(s * C, (s + 1) * C)
        k.conv[part] = (
            column(4 + KS * s) * k.z[part]
            + column(5 + KS * s) * k.z1[part]
            + column(6 + KS * s) * k.z2[part]
        )
    product = k.conv[0:C] * k.conv[2 * C : 3 * C] * valid
    k.prod[...] = product
    by_channel(k.ps, product)
    swap_seq(k.ps, k.ur, 0)

    pre = filter_frequency * nn(k.feat[...], k.fh[0:8], HIGHEST)
    k.l1[...] = jnp.sin(pre)
    k.c1[...] = filter_frequency * jnp.cos(pre)
    pre = filter_frequency * nn(k.l1[...], k.fh[EMB : EMB + 128], HIGHEST)
    k.l2[...] = jnp.sin(pre)
    k.c2[...] = filter_frequency * jnp.cos(pre)
    foc = k.foc[pl.ds(r, 1)].reshape(CP, 128)
    vtc = k.vtc[pl.ds(r, 1)].reshape(CP, 128)
    rate = vtc[:, 2:3]
    skip_channel = vtc[:, 3:4]
    shaped = nt(foc, k.l2[...], HIGHEST)
    part_lane = lax.broadcasted_iota(jnp.int32, (1, GL), 1)
    for q in range(Q):
        fraction = (part_lane + q * GL).astype(jnp.float32) / LEN
        decay = jnp.exp(-fraction * rate) * (LEN ** (-0.5))
        k.decay[q] = decay
        k.taps[q] = shaped[:, q * GL : (q + 1) * GL] * decay
    spectrum = nn(k.taps[...].reshape(Q * CP, GL), k.ttap[...]).reshape(Q, CP, 2 * R)
    for q in range(Q):
        real = spectrum[q, :, 0:R]
        imag = spectrum[q, :, R : 2 * R]
        if q > 0:
            real = real + flip * spectrum[q - 1, :, 0:R]
            imag = imag + flip * spectrum[q - 1, :, R : 2 * R]
        k.kr[q] = real
        k.km[q] = imag * keep_bin
        k.k4[q] = jnp.where(first_bin, imag, real)

    def total_pairs(count, first, term):
        zero = jnp.zeros((CP, R), jnp.float32)
        if Q <= 8:
            real, imag = zero, zero
            for i in range(count):
                add_real, add_imag = term(first + i)
                real, imag = real + add_real, imag + add_imag
            return real, imag

        def body(i, kept):
            add_real, add_imag = term(first + i)
            return (kept[0] + add_real, kept[1] + add_imag)

        return lax.fori_loop(0, count, body, (zero, zero))

    def each_block(body):
        if Q <= 8:
            for q in range(Q):
                body(q)
        else:
            pl.loop(0, Q)(body)

    seq_arrive(k.ur, 0)
    k.us[...] = nn(k.ur[...].reshape(Q * CP, R), k.tfwd[...]).reshape(Q, CP, 2 * R)

    def forward_block(p):
        def term(q):
            real = k.us[q, :, 0:R]
            imag = k.us[q, :, R : 2 * R]
            lag = p - q
            return (
                k.kr[lag] * real - k.km[lag] * imag,
                k.km[lag] * real + k.k4[lag] * imag,
            )

        real, imag = total_pairs(p + 1, 0, term)
        k.zs[p, :, 0:R] = real
        k.zs[p, :, R : 2 * R] = imag

    each_block(forward_block)
    k.ys[...] = nn(k.zs[...].reshape(Q * CP, 2 * R), k.tinv[...]).reshape(Q, CP, R)
    swap_seq(k.ys, k.yr, 1)
    for q in range(Q):
        real = k.us[q, :, 0:R]
        imag = k.us[q, :, R : 2 * R]
        k.um[q] = imag * keep_bin
        k.u4[q] = jnp.where(first_bin, imag, real)

    seq_arrive(k.yr, 1)
    inner_sum = from_channels(k.yr) + column(3) * k.prod[...]
    k.insum[...] = inner_sum
    gated = k.conv[C : 2 * C] * inner_sum
    k.gated[...] = gated
    pieces(k.s1, tn(k.sq[1], gated), PW)
    swap_blocks(k.s1, k.r1, 1)

    copies[4].wait()
    blocks_arrive(k.r4, 4)
    k.dact[...] = nn(k.dr[...], k.r4[...].reshape(F, R))
    copies[3].wait()

    blocks_arrive(k.r1, 1)
    w1 = k.r1[...].reshape(C, R)
    k.w1[...] = w1
    h = k.xt[...] + tn(k.sq[2], w1)
    k.h[...] = h
    u3 = h * column(1)
    pieces(k.s2, tn(k.sq[3], u3), PW)
    squares = jnp.broadcast_to(jnp.sum(h * h, axis=0, keepdims=True), (8, R))
    for b in range(M):
        k.s2[b, PW : PW + 8] = squares
    swap_blocks(k.s2, k.r2, 2)

    blocks_arrive(k.r2, 2)
    scale_two = lax.rsqrt(extra(k.r2) / D + norm_epsilon)
    k.n2[...] = k.h[...] * scale_two
    w3 = joined(k.r2, PW)
    k.w3[...] = w3
    k.gu[...] = tn(k.ul[...], w3) * scale_two
    gate = k.gu[0:F]
    up = k.gu[F : 2 * F]
    bend = jnp.tanh(gelu_scale * (gate + gelu_cubic * gate * gate * gate))
    gelu = 0.5 * gate * (1.0 + bend)
    slope = 0.5 * (1.0 + bend) + 0.5 * gate * (1.0 - bend * bend) * gelu_scale * (
        1.0 + 3.0 * gelu_cubic * gate * gate
    )
    dact = k.dact[...]
    k.act[...] = gelu * up
    k.dgu[0:F] = dact * up * slope
    k.dgu[F : 2 * F] = dact * gelu
    back = nn(k.ul[...], k.dgu[...])
    pieces(k.s5, back, PW)
    inner = jnp.broadcast_to(jnp.sum(back * k.w3[...], axis=0, keepdims=True), (8, R))
    for b in range(M):
        k.s5[b, PW : PW + 8] = inner
    swap_blocks(k.s5, k.r5, 5)
    pieces(k.s3, tn(k.dr[...], k.act[...]), FW)
    swap_blocks(k.s3, k.r3, 3)
    k.gdr[...] = nt(k.act[...], k.r4[...].reshape(F, R))
    for one in first_rings:
        one.begin()

    k.gmid[:, 0 : 2 * F] = nt(k.w3[...] * scale_two, k.dgu[...])
    blocks_arrive(k.r3, 3)
    w4 = k.r3[...].reshape(F, R)
    k.block_out[...] = (k.h[...] + nn(k.dl[...], w4)).T
    k.gmid[:, 2 * F : 3 * F] = nt(k.ogt[...], w4)
    for one in other_rings:
        one.begin()
    blocks_arrive(k.r5, 5)
    back = joined(k.r5, PW)
    inner = extra(k.r5)
    grad_two = nn(k.sq[3], back)
    hidden_grad = (
        k.ogt[...]
        + scale_two * (grad_two * column(1))
        - k.h[...] * (scale_two * scale_two * scale_two * inner / D)
    )
    k.hg[...] = hidden_grad
    pieces(k.s6, nn(k.sq[2], hidden_grad), PW)
    swap_blocks(k.s6, k.r6, 6)
    first_halves(1)
    k.glate[:, 3 * C : 4 * C] = nt(k.n2[...] * column(1), back)
    gain_two = jnp.sum(grad_two * k.n2[...], axis=1, keepdims=True)
    k.glate[:, 2 * C : 3 * C] = nt(k.w1[...], k.hg[...])

    first_halves(1)
    blocks_arrive(k.r6, 6)
    back = k.r6[...].reshape(C, R)
    gated_grad = nn(k.sq[1], back)
    inner_grad = gated_grad * k.conv[C : 2 * C]
    k.inner[...] = inner_grad
    k.d1[...] = gated_grad * k.insum[...]
    by_channel(k.inner_s, inner_grad)
    swap_seq(k.inner_s, k.vr, 2)
    k.glate[:, C : 2 * C] = nt(k.gated[...], back)
    skip_total = jnp.sum(inner_grad * k.prod[...], axis=1, keepdims=True)

    first_halves(2)
    mid_half()
    seq_arrive(k.vr, 2)
    k.vs[...] = nn(k.vr[...].reshape(Q * CP, R), k.tfwd[...]).reshape(Q, CP, 2 * R)

    def back_block(q):
        def term(p):
            real = k.vs[p, :, 0:R]
            imag = k.vs[p, :, R : 2 * R]
            lag = p - q
            return (
                k.kr[lag] * real + k.km[lag] * imag,
                k.k4[lag] * imag - k.km[lag] * real,
            )

        real, imag = total_pairs(Q - q, q, term)
        k.zs[q, :, 0:R] = real
        k.zs[q, :, R : 2 * R] = imag

    each_block(back_block)
    k.ds[...] = (
        nn(k.zs[...].reshape(Q * CP, 2 * R), k.tinv[...]).reshape(Q, CP, R)
        + skip_channel[None] * k.vr[...]
    )
    swap_seq(k.ds, k.dmain, 3)
    first_halves(1)
    def lag_block(j):
        def term(p):
            real = k.vs[p, :, 0:R]
            imag = k.vs[p, :, R : 2 * R]
            q = p - j
            return (
                k.us[q, :, 0:R] * real + k.um[q] * imag,
                k.u4[q] * imag - k.um[q] * real,
            )

        real, imag = total_pairs(Q - j, j, term)
        k.zs[j, :, 0:R] = real
        k.zs[j, :, R : 2 * R] = imag

    each_block(lag_block)
    cross = k.zs[...].reshape(Q * CP, 2 * R)
    near = nn(cross, k.tw1[...]).reshape(Q, CP, GL)
    far = nn(cross, k.tw2[...]).reshape(Q, CP, GL)
    decay_total = jnp.zeros((CP, 1), jnp.float32)
    for q in range(Q):
        grad = near[q]
        if q < Q - 1:
            grad = grad + far[q + 1]
        fraction = (part_lane + q * GL).astype(jnp.float32) / LEN
        decay_total = decay_total - jnp.sum(
            grad * k.taps[q] * fraction, axis=1, keepdims=True
        )
        k.draw[:, q * GL : (q + 1) * GL] = grad * k.decay[q]
    raw = k.draw[...]
    k.gfo[...] = jnp.zeros(k.gfo.shape, jnp.float32)
    k.gdec[...] = jnp.zeros(k.gdec.shape, jnp.float32)
    k.gfo[pl.ds(r, 1)] = nn(raw, k.l2[...]).reshape(1, CP, 128)
    k.gdec[pl.ds(r, 1)] = jnp.broadcast_to(decay_total, (CP, 128)).reshape(1, CP, 128)
    first_halves(1)
    mid_half()
    back = tn(raw, foc) * k.c2[...]
    k.hid[8:136] = tn(k.l1[...], back)
    back = nt(back, k.fh[EMB : EMB + 128]) * k.c1[...]
    k.hid[0:8] = tn(k.feat[...], back)
    for d in range(1, M):
        send(k.hid, k.hids.at[e], k.mpsem.at[8, e], r, lax.rem(e + d, M))
    k.hids[pl.ds(e, 1)] = k.hid[...].reshape(1, 136, 128)


    first_halves(1)
    seq_arrive(k.dmain, 3)
    product_grad = from_channels(k.dmain) * valid
    k.d3[0:C] = product_grad * k.conv[2 * C : 3 * C]
    k.d3[C : 2 * C] = k.d1[...]
    k.d3[2 * C : 3 * C] = product_grad * k.conv[0:C]
    k.hs1[...] = nt(ends, k.d3[...], HIGHEST)
    edge = remote(k.hs1, k.hr1, k.hsem.at[2, 0], k.d1sem, prv, e)

    @pl.when(r > 0)
    def _():
        edge.start()

    @pl.when(r == Q - 1)
    def _():
        k.hr1[...] = jnp.zeros(k.hr1.shape, jnp.float32)

    first_halves(1)
    mid_half()

    @pl.when(r < Q - 1)
    def _():
        arrive(k.hr1, k.d1sem)

    following = pltpu.roll(tn(k.hr1[...], ends, HIGHEST), GL, 1)
    tap_totals = []
    for s in range(3):
        part = slice(s * C, (s + 1) * C)
        grad = k.d3[part]
        one = pltpu.roll(jnp.where(spot == 0, following[part], grad), R - 1, 1)
        two = pltpu.roll(jnp.where(head, following[part], grad), R - 2, 1)
        k.dz[part] = (
            column(4 + KS * s) * grad + column(5 + KS * s) * one + column(6 + KS * s) * two
        )
        for shifted in (k.z, k.z1, k.z2):
            tap_totals.append(jnp.sum(grad * shifted[part], axis=1, keepdims=True))
    back = nn(k.inl[...], k.dz[...])
    pieces(k.s7, back, PW)
    inner = jnp.broadcast_to(jnp.sum(back * k.w0[...], axis=0, keepdims=True), (8, R))
    for b in range(M):
        k.s7[b, PW : PW + 8] = inner
    swap_blocks(k.s7, k.r7, 7)
    k.glate[:, 4 * C : 7 * C] = nt(k.w0[...] * scale_one, k.dz[...])

    first_halves(1)
    blocks_arrive(k.r7, 7)
    back = joined(k.r7, PW)
    inner = extra(k.r7)
    grad_one = nn(k.sq[0], back)
    xt = k.xt[...]
    k.input_grad[...] = (
        k.hg[...]
        + scale_one * (grad_one * column(0))
        - xt * (scale_one * scale_one * scale_one * inner / D)
    ).T
    k.glate[:, 0:C] = nt(k.u0[...] * scale_one, back)
    gain_one = jnp.sum(grad_one * xt * scale_one, axis=1, keepdims=True)
    starts, width = late_columns(C)
    slot = lax.broadcasted_iota(jnp.int32, (1, 16), 1)
    rows = {0: gain_one, 1: gain_two, 2: from_channels(k.gdec)[:, 0:1], 3: skip_total}
    rows.update({4 + i: total for i, total in enumerate(tap_totals)})
    stacked = jnp.zeros((C, 16), jnp.float32)
    for i, total in rows.items():
        stacked = jnp.where(slot == i, total, stacked)
    k.glate[:, starts[2] : starts[3]] = jnp.zeros((C, starts[3] - starts[2]), jnp.float32)
    k.glate[:, starts[2] : starts[2] + 16] = stacked
    k.glate[:, starts[3] : starts[4]] = from_channels(k.gfo)
    first_halves(1)
    mid_half()
    blocks_arrive(k.hids, 8)
    hidden_sum = k.hids[0]
    for b in range(1, M):
        hidden_sum = hidden_sum + k.hids[b]
    k.glate[0:136, starts[4] : width] = hidden_sum
    k.glate[136:C, starts[4] : width] = jnp.zeros((C - 136, 128), jnp.float32)

    if ringed:
        for one in late_rings:
            one.begin()
        rest = other_rings + late_rings
        for _ in range(2 * Q - halves_done[0]):
            first_halves(1)
            if halves_done[1] < 2 * MID_EARLY:
                mid_half()
        copies[5].wait()
        moment = momentum_decay * k.x[...] + k.tdr[...]
        k.moment[...] = moment
        outs = [pltpu.make_async_copy(k.moment, k.out_dr, k.wsem.at[6])]
        outs[0].start()
        k.x[...] = moment * unit_scale(moment)

        late_turns, mid_turns = iter(range(Q)), iter(range(MID_EARLY, Q))

        def between(product):
            rings, turns = ((late_rings, late_turns), (other_rings, mid_turns))[product % 3 == 1]
            turn = next(turns, None)
            if turn is not None:
                go(rings, turn)

        large_schulz(k, between)
        outs.append(pltpu.make_async_copy(k.x, k.out_ortho, k.wsem.at[7]))
        outs.append(pltpu.make_async_copy(k.tmid, k.out_mid, k.wsem.at[8]))
        for copy in outs[1:]:
            copy.start()
        outs.append(pltpu.make_async_copy(k.tlate, k.out_late, k.wsem.at[9]))
        outs[-1].start()
        for one in first_rings + rest:
            one.end()
    else:
        outs = [
            pltpu.make_async_copy(k.gdr, k.out_dr, k.wsem.at[6]),
            pltpu.make_async_copy(k.gmid, k.out_mid, k.wsem.at[8]),
            pltpu.make_async_copy(k.glate, k.out_late, k.wsem.at[9]),
        ]
        for copy in outs:
            copy.start()
    for copy in outs:
        copy.wait()
    for copy in sends:
        copy.wait_send()

    @pl.when(r < Q - 1)
    def _():
        for copy in halo_after:
            copy.wait_send()

    @pl.when(r > 0)
    def _():
        for copy in halo_before + [edge]:
            copy.wait_send()


def run_chain(x, og, lengths, sq, inl, ul, dr, dl, pdr, vectors, fh, fo):
    M, Q = lax.axis_size("mp"), lax.axis_size("seq")
    _, GL, C = x.shape
    R = SEQS * GL
    F = dr.shape[0]
    LEN = GL * Q
    cpd = C // Q
    CP = -(-cpd // 8) * 8
    PW, FW = C // M, F // M
    ringed = cpd % 8 == 0 and F % (32 * Q) == 0
    dims = (C, M, Q, GL, CP, cpd, F, LEN, ringed)
    tables = spectrum_tables(GL)
    feat = feature_table(LEN)
    width = late_columns(C)[1]
    sds = lambda *shape: jax.ShapeDtypeStruct(shape, jnp.float32)
    v = lambda *shape: pltpu.VMEM(shape, jnp.float32)
    dma = lambda *shape: pltpu.SemaphoreType.DMA(shape)
    in_vmem = dict(
        block_in=x.reshape(R, C),
        out_grad=og.reshape(R, C),
        vec=vectors,
        fh=fh,
        fo=fo,
        feat=feat,
        **dict(zip(("tfwd", "ttap", "tinv", "tw1", "tw2"), tables)),
    )
    in_hbm = dict(sq_hbm=sq, inl_hbm=inl, ul_hbm=ul, dr_hbm=dr, dl_hbm=dl)
    if ringed:
        in_hbm["pdr_hbm"] = pdr
    out_vmem = dict(block_out=sds(R, C), input_grad=sds(R, C))
    out_hbm = dict(out_dr=sds(F, F), out_mid=sds(C, 3 * F), out_late=sds(C, width))
    if ringed:
        out_hbm["out_ortho"] = sds(F, F)
    scratch = dict(
        sq=v(4, C, C),
        inl=v(C, 3 * C),
        ul=v(C, 2 * F),
        dr=v(F, F),
        dl=v(C, F),
        vecp=v(128, C),
        vt=v(C, 128),
        vtc=v(Q, CP, 128),
        foc=v(Q, CP, 128),
        gfo=v(Q, CP, 128),
        gdec=v(Q, CP, 128),
        gu=v(2 * F, R),
        act=v(F, R),
        dact=v(F, R),
        dgu=v(2 * F, R),
        hid=v(136, 128),
        hs0=v(M, 8, 128),
        hp0=v(M, 8, 128),
        hn0=v(M, 8, 128),
        hs1=v(8, 3 * C),
        hr1=v(8, 3 * C),
        hids=v(M, 136, 128),
        taps=v(Q, CP, GL),
        decay=v(Q, CP, GL),
        draw=v(CP, LEN),
        gdr=v(F, F),
        gmid=v(C, 3 * F),
        glate=v(C, width),
    )
    for name in ("xt", "ogt", "u0", "prod", "insum", "gated", "w0", "w1", "w3", "h", "n2", "hg", "inner", "d1"):
        scratch[name] = v(C, R)
    for name in ("z", "z1", "z2", "conv", "dz", "d3"):
        scratch[name] = v(3 * C, R)
    for name in ("l1", "c1", "l2", "c2"):
        scratch[name] = v(LEN, 128)
    for name in ("kr", "km", "k4", "um", "u4", "ps", "ur", "ys", "yr", "inner_s", "vr", "ds", "dmain"):
        scratch[name] = v(Q, CP, R)
    for name in ("us", "vs", "zs"):
        scratch[name] = v(Q, CP, 2 * R)
    for name in ("s0", "r0", "s2", "r2", "s5", "r5", "s7", "r7"):
        scratch[name] = v(M, PW + 8, R)
    for name in ("s1", "r1", "s6", "r6"):
        scratch[name] = v(M, PW, R)
    for name in ("s3", "r3", "s4", "r4"):
        scratch[name] = v(M, FW, R)
    sends = 9 * (M - 1) + 4 * (Q - 1)
    scratch.update(
        wsem=dma(10),
        ssem=dma(sends),
        mpsem=dma(9, M),
        hsem=dma(3, M),
        hpsem=dma(M),
        hnsem=dma(M),
        seqsem=dma(4, Q),
        d1sem=pltpu.SemaphoreType.DMA,
    )
    if ringed:
        scratch.update(
            tdr=v(F, F),
            tmid=v(C, 3 * F),
            tlate=v(C, width),
            far_dr=v(2, Q // 2, F // Q // 2, F),
            near_dr=v(2, Q // 2 - 1, F // Q // 2, F),
            ring_ssem=dma(6, 2 * Q - 2),
            ring_rsem=dma(6, 2 * Q - 2),
            x=v(F, F),
            a=v(F, F),
            moment=v(F, F),
        )
        for name in ("xh", "xl", "ah", "al", "ph", "pl"):
            scratch[name] = pltpu.VMEM((F, F), jnp.bfloat16)
        for name, columns in (("mid", 3 * F), ("late", width)):
            cut = columns // 256 * 128
            for i, part in enumerate((cut, columns - cut)):
                scratch[f"far_{name}{i}"] = v(Q // 2, C // Q, part)
                scratch[f"near_{name}{i}"] = v(Q // 2 - 1, C // Q, part)
    vmem = pl.BlockSpec(memory_space=pltpu.VMEM)
    smem = pl.BlockSpec(memory_space=pltpu.SMEM)
    hbm = pl.BlockSpec(memory_space=pl.ANY)
    names = ["lengths", *in_vmem, *in_hbm, *out_vmem, *out_hbm, *scratch]
    outs = pl.pallas_call(
        functools.partial(chain_kernel, dims, names),
        out_shape=[*out_vmem.values(), *out_hbm.values()],
        in_specs=[smem] + [vmem] * len(in_vmem) + [hbm] * len(in_hbm),
        out_specs=[vmem] * len(out_vmem) + [hbm] * len(out_hbm),
        scratch_shapes=list(scratch.values()),
        compiler_params=pltpu.CompilerParams(
            collective_id=0, has_side_effects=True, vmem_limit_bytes=58 * 2**20
        ),
        name="chain",
    )(lengths, *in_vmem.values(), *in_hbm.values())
    block_out, input_grad, out_dr, out_mid, out_late = outs[:5]
    if ringed:
        return block_out, input_grad, (out_dr, out_mid, out_late), outs[5]
    return block_out, input_grad, lax.psum((out_dr, out_mid, out_late), "seq"), None


def polynomial(gram):
    return schulz_second * gram + schulz_third * nn(gram, gram)


def gram_step(gram, total, eye, last):
    factor = schulz_first * eye + (
        schulz_second * gram + schulz_third * nn(gram, gram, HIGHEST)
    )
    total = factor if total is None else nn(total, factor)
    if not last:
        gram = nn(nn(gram, factor, HIGHEST), factor, HIGHEST)
    return gram, total


def schulz_step(current):
    return schulz_first * current + nn(polynomial(nt(current, current)), current)


def adam(refs, gradient, rate):
    weights, first, second, first_out, second_out, weights_out, copy_out = refs
    first_new = beta_first * first[...] + (1.0 - beta_first) * gradient
    second_new = beta_second * second[...] + (1.0 - beta_second) * gradient * gradient
    corrected_first = first_new / (1.0 - beta_first**STEP)
    corrected_second = second_new / (1.0 - beta_second**STEP)
    old = weights[...]
    new = old - rate * (
        corrected_first / (jnp.sqrt(corrected_second) + adam_epsilon) + weight_decay * old
    )
    first_out[...] = first_new
    second_out[...] = second_new
    weights_out[...] = new
    copy_out[...] = new.astype(jnp.bfloat16)


def muon_kernel(names, loaded, stored, ringed, *refs):
    k = types.SimpleNamespace(**dict(zip(names, refs, strict=True)))
    C = k.wsq.shape[1]
    F = k.wdr.shape[0]
    starts, width = late_columns(C)
    reads = {
        name: pltpu.make_async_copy(
            getattr(k, "hbm_" + name), getattr(k, name), k.read_sem.at[i]
        )
        for i, name in enumerate(loaded)
    }
    writes = {
        name: pltpu.make_async_copy(
            getattr(k, name), getattr(k, "hbm_" + name), k.write_sem.at[i]
        )
        for i, name in enumerate(stored)
    }
    if ringed:
        writes["mdr"] = pltpu.make_async_copy(k.gdr, k.hbm_mdr, k.write_sem.at[len(stored)])
    for copy in reads.values():
        copy.start()

    def need(*wanted):
        for name in wanted:
            reads[name].wait()

    def put(*done):
        for name in done:
            writes[name].start()

    def finish(name, orthogonal, scale, index=...):
        new = getattr(k, "w" + name)[index] - muon_rate * math.sqrt(scale) * orthogonal
        getattr(k, "n" + name)[index] = new
        getattr(k, "c" + name)[index] = new.astype(jnp.bfloat16)

    def moved(name, gradient, index=...):
        moment = momentum_decay * getattr(k, "p" + name)[index] + gradient
        getattr(k, "m" + name)[index] = moment
        return moment * unit_scale(moment)

    need("glate", "psq")
    squares = [moved("sq", k.glate[:, i * C : (i + 1) * C], i) for i in range(4)]
    put("msq")
    need("pinl")
    wide = {"inl": moved("inl", k.glate[:, starts[1] : starts[2]])}
    put("minl")
    need("gmid", "pul")
    wide["ul"] = moved("ul", k.gmid[:, 0 : 2 * F])
    put("mul")
    need("pdl")
    wide["dl"] = moved("dl", k.gmid[:, 2 * F : 3 * F])
    put("mdl")
    eye = (
        lax.broadcasted_iota(jnp.int32, (C, C), 0) == lax.broadcasted_iota(jnp.int32, (C, C), 1)
    ).astype(jnp.float32)
    grams = {name: (nt(start, start, HIGHEST), None) for name, start in wide.items()}
    for step in range(5):
        squares = [schulz_step(current) for current in squares]
        grams = {
            name: gram_step(gram, total, eye, step == 4)
            for name, (gram, total) in grams.items()
        }
        if step == 1 and ringed:
            need("gdr", "ortho", "wdr")
            put("mdr")
            finish("dr", k.ortho[...], 1.0)
            put("ndr", "cdr")
    need("wsq")
    for i in range(4):
        finish("sq", squares[i], 1.0, i)
    put("nsq", "csq")
    for name, scale in (("inl", 3.0), ("dl", 1.0), ("ul", 2.0 * F / C)):
        need("w" + name)
        finish(name, nn(grams[name][1], wide[name]), scale)
        put("n" + name, "c" + name)

    turned = k.glate[:, starts[3] - 128 : starts[3]].T
    lead = 128 - (starts[3] - starts[2])
    vector_grad = turned[lead : lead + 16][0 : 4 + 3 * KS]
    hidden_grad = jnp.concatenate(
        [k.glate[0:EMB, starts[4] : width], k.glate[8:136, starts[4] : width]], axis=0
    )
    for name, gradient, rate in (
        ("v", vector_grad, rate_vectors),
        ("h", hidden_grad, rate_hidden),
        ("f", k.glate[:, starts[3] : starts[4]], rate_output),
    ):
        adam(
            [getattr(k, name + kind) for kind in ("w", "1", "2", "1n", "2n", "n", "c")],
            gradient,
            rate,
        )

    if not ringed:
        need("gdr", "pdr", "wdr")
        k.x[...] = moved("dr", k.gdr[...])
        large_schulz(k, idle)
        finish("dr", k.x[...], 1.0)
        put("mdr", "ndr", "cdr")
    for copy in writes.values():
        copy.wait()


def run_muon(totals, ortho, moments, weights, small):
    gdr, gmid, glate = totals
    ringed = ortho is not None
    kinds = ("sq", "inl", "ul", "dr", "dl")
    arrays = dict(glate=glate, gmid=gmid, gdr=gdr)
    arrays.update({"p" + name: moment for name, moment in zip(kinds, moments)})
    arrays.update({"w" + name: weight for name, weight in zip(kinds, weights)})
    if ringed:
        arrays["ortho"] = ortho
    loaded = ["glate", "psq", "pinl", "gmid", "pul", "pdl", "wdr", "wsq", "winl", "wdl", "wul"]
    loaded[6:6] = ["gdr", "ortho"] if ringed else ["gdr", "pdr"]
    in_hbm = {"hbm_" + name: array for name, array in arrays.items()}
    out_hbm = {}
    for name, weight in zip(kinds, weights):
        for kind, dtype in (("m", jnp.float32), ("n", jnp.float32), ("c", jnp.bfloat16)):
            out_hbm["hbm_" + kind + name] = jax.ShapeDtypeStruct(weight.shape, dtype)
    in_vmem, out_vmem = {}, {}
    for name, (weight, first, second) in small.items():
        in_vmem[name + "w"], in_vmem[name + "1"], in_vmem[name + "2"] = weight, first, second
        for suffix in ("1n", "2n", "n"):
            out_vmem[name + suffix] = jax.ShapeDtypeStruct(weight.shape, jnp.float32)
        out_vmem[name + "c"] = jax.ShapeDtypeStruct(weight.shape, jnp.bfloat16)
    scratch = {name: pltpu.VMEM(arrays[name].shape, jnp.float32) for name in loaded}
    stored = [name[4:] for name in out_hbm if not (ringed and name == "hbm_mdr")]
    for name in stored:
        like = out_hbm["hbm_" + name]
        scratch[name] = pltpu.VMEM(like.shape, like.dtype)
    if not ringed:
        scratch.update({n: pltpu.VMEM(gdr.shape, jnp.float32) for n in ("x", "a")})
        for name in ("xh", "xl", "ah", "al", "ph", "pl"):
            scratch[name] = pltpu.VMEM(gdr.shape, jnp.bfloat16)
    scratch["read_sem"] = pltpu.SemaphoreType.DMA((len(loaded),))
    scratch["write_sem"] = pltpu.SemaphoreType.DMA((len(stored) + 1,))
    vmem = pl.BlockSpec(memory_space=pltpu.VMEM)
    hbm = pl.BlockSpec(memory_space=pl.ANY)
    names = [*in_hbm, *in_vmem, *out_hbm, *out_vmem, *scratch]
    results = pl.pallas_call(
        functools.partial(muon_kernel, names, loaded, stored, ringed),
        out_shape=[*out_hbm.values(), *out_vmem.values()],
        in_specs=[hbm] * len(in_hbm) + [vmem] * len(in_vmem),
        out_specs=[hbm] * len(out_hbm) + [vmem] * len(out_vmem),
        scratch_shapes=list(scratch.values()),
        compiler_params=pltpu.CompilerParams(vmem_limit_bytes=60 * 2**20),
        name="muon",
    )(*in_hbm.values(), *in_vmem.values())
    new = dict(zip([*out_hbm, *out_vmem], results))
    return {name.removeprefix("hbm_"): value for name, value in new.items()}


def per_device(
    block_input,
    out_grad,
    lengths,
    square_factors,
    square_moment,
    input_left,
    input_left_moment,
    up_left,
    up_left_moment,
    down_right,
    down_right_moment,
    down_left,
    down_left_moment,
    vectors,
    vectors_first,
    vectors_second,
    filter_hidden,
    hidden_first,
    hidden_second,
    filter_out,
    filter_out_first,
    filter_out_second,
):
    weights = (square_factors[:, 0], input_left[0], up_left[0], down_right[0], down_left[0].T)
    moments = (
        square_moment[:, 0],
        input_left_moment[0],
        up_left_moment[0],
        down_right_moment[0],
        down_left_moment[0].T,
    )
    block_output, input_grad, totals, ortho = run_chain(
        block_input, out_grad, lengths, *weights, moments[3], vectors, filter_hidden, filter_out.T
    )
    small = dict(
        v=(vectors, vectors_first, vectors_second),
        h=(filter_hidden, hidden_first, hidden_second),
        f=(filter_out.T, filter_out_first.T, filter_out_second.T),
    )
    new = run_muon(totals, ortho, moments, weights, small)
    return (
        block_output.reshape(block_input.shape),
        input_grad.reshape(block_input.shape),
        *[new[kind + "sq"][:, None] for kind in "mnc"],
        *[new[kind + name][None] for name in ("inl", "ul", "dr") for kind in "mnc"],
        *[new[kind + "dl"].T[None] for kind in "mnc"],
        *[new[name + suffix] for name in "vh" for suffix in ("1n", "2n", "n", "c")],
        *[new["f" + suffix].T for suffix in ("1n", "2n", "n", "c")],
    )


def solution(mesh):
    tokens = P(None, "seq", "mp")
    square = P(None, "mp", None, None)
    block = P("mp", None, None)
    row = P(None, "mp")
    return jax.shard_map(
        per_device,
        mesh=mesh,
        in_specs=(tokens, tokens, P(), square, square)
        + (block,) * 8
        + (row,) * 3
        + (P(),) * 3
        + (row,) * 3,
        out_specs=(tokens, tokens)
        + (square,) * 3
        + (block,) * 12
        + (row,) * 4
        + (P(),) * 4
        + (row,) * 4,
        check_vma=False,
    )
```

```python
import functools
import math
import types

import jax
import jax.numpy as jnp
import numpy as np
from jax import lax
from jax.experimental import pallas as pl
from jax.experimental.pallas import tpu as pltpu
from jax.sharding import PartitionSpec as P

EMB = 5
KS = 3
STEP = 10
SEQS = 2

HIGH = lax.Precision.HIGH
HIGHEST = lax.Precision.HIGHEST
MESH = pl.DeviceIdType.MESH
norm_epsilon = 1e-05
beta_first = 0.9
beta_second = 0.95
adam_epsilon = 1e-08
weight_decay = 0.01
rate_vectors = 0.2
rate_hidden = 0.05
rate_output = 0.05
muon_rate = 0.5
momentum_decay = 0.5
schulz_first = 3.4445
schulz_second = -4.775
schulz_third = 2.0315
filter_frequency = 10.0
gelu_scale = math.sqrt(2.0 / math.pi)
gelu_cubic = 0.044715


def contract(a, b, dim_a, dim_b, precision=HIGH):
    return lax.dot_general(
        a,
        b,
        (((dim_a,), (dim_b,)), ((), ())),
        precision=precision,
        preferred_element_type=jnp.float32,
    )


def nn(a, b, precision=HIGH):
    return contract(a, b, 1, 0, precision)


def nt(a, b, precision=HIGH):
    return contract(a, b, 1, 1, precision)


def tn(a, b, precision=HIGH):
    return contract(a, b, 0, 0, precision)


def spectrum_tables(group_len):
    rows = SEQS * group_len
    period = 2 * group_len
    time = np.arange(group_len)
    lags = np.arange(period)
    bins = np.arange(group_len)
    angle = 2.0 * np.pi * (np.outer(time, bins) % period) / period
    real = np.cos(angle)
    imag = -np.sin(angle)
    imag[:, 0] = (-1.0) ** time
    forward = np.zeros((rows, 2 * rows))
    for s in range(SEQS):
        part = slice(s * group_len, (s + 1) * group_len)
        forward[part, part] = real
        forward[part, rows + s * group_len : rows + (s + 1) * group_len] = imag
    of_taps = np.concatenate([real] * SEQS + [imag] * SEQS, axis=1)
    angle = 2.0 * np.pi * (np.outer(bins, lags) % period) / period
    back_real = 2.0 * np.cos(angle) / period
    back_real[0] = 1.0 / period
    back_imag = -2.0 * np.sin(angle) / period
    back_imag[0] = (-1.0) ** lags / period
    inverse = np.zeros((2 * rows, rows))
    for s in range(SEQS):
        part = slice(s * group_len, (s + 1) * group_len)
        inverse[part, part] = back_real[:, :group_len]
        inverse[rows + s * group_len : rows + (s + 1) * group_len, part] = back_imag[:, :group_len]
    window = np.concatenate([back_real] * SEQS + [back_imag] * SEQS, axis=0)
    return tuple(
        v.astype(np.float32)
        for v in (forward, of_taps, inverse, window[:, :group_len], window[:, group_len:])
    )


def feature_table(length):
    fraction = np.arange(length).astype(np.float32) / np.float32(length)
    angle = np.float32(2.0 * math.pi) * fraction
    wide = angle.astype(np.float64)
    twice = (np.float32(2.0) * angle).astype(np.float64)
    columns = [fraction, np.cos(wide), np.sin(wide), np.cos(twice), np.sin(twice)]
    table = np.zeros((length, 8), np.float32)
    for i, column in enumerate(columns):
        table[:, i] = column.astype(np.float32)
    return table


LATE = dict(sq=0, inl=1, vec=2, fo=3, hid=4)


KINDS = ("sq", "inl", "ul", "dr", "dl")


def late_columns(C):
    start = [0, 4 * C, 7 * C, 7 * C + C // 3, 7 * C + C // 3 + 128]
    return start, 7 * C + C // 3 + 256


def when(condition, body):
    if isinstance(condition, bool):
        if condition:
            body()
    else:
        pl.when(condition)(body)


LATE_AFTER = (3, 7, 11, 13)
EARLY = ("block_in", "vec", "out_grad", "fo", "fh", "feat", "tfwd", "ttap", "tinv", "tw1", "tw2")
SMALL = 384


class Ring:
    def __init__(self, grad, total, far_slot, near_slot, ssem, rsem, rows, columns, way, place, count, ids):
        self.grad, self.total = grad, total
        self.far_slot, self.near_slot = far_slot, near_slot
        self.ssem, self.rsem = ssem, rsem
        self.stride, self.offset, self.height = rows
        self.columns = columns
        self.sign = 1 if way == 0 else -1
        self.place, self.count = place, count
        self.ahead, self.behind = ids if way == 0 else ids[::-1]

    def part(self, ref, ahead):
        chunk = lax.rem(self.place + self.sign * ahead + 4 * self.count, self.count)
        start = pl.multiple_of(chunk * self.stride + self.offset, 8)
        return ref.at[pl.ds(start, self.height), self.columns]

    def copy(self, source, target, index, to):
        return pltpu.make_async_remote_copy(
            src_ref=source,
            dst_ref=target,
            send_sem=self.ssem.at[int(index >= self.count - 1)],
            recv_sem=self.rsem.at[index],
            device_id=to,
            device_id_type=MESH,
        )

    def far_sum(self, i):
        n = self.count // 2
        return self.copy(self.part(self.grad, n - i), self.far_slot.at[i], i, self.ahead)

    def near_sum(self, i):
        n = self.count // 2
        source = self.part(self.grad, i - (n - 1))
        return self.copy(source, self.near_slot.at[i], n + i, self.behind)

    def far_total(self, i, hops=0):
        n = self.count // 2
        whole = self.part(self.total, i + hops)
        return self.copy(whole, whole, 2 * n - 1 + i, self.behind)

    def near_total(self, i, hops=0):
        n = self.count // 2
        whole = self.part(self.total, -i - hops)
        return self.copy(whole, whole, 3 * n - 1 + i, self.ahead)

    def begin(self):
        self.far_sum(0).start()
        self.near_sum(0).start()

    def event(self, s):
        n = self.count // 2

        def add_far():
            mine = self.part(self.grad, n - 1 - s)
            mine[...] = mine[...] + self.far_slot[s]
            self.far_sum(s + 1).start()

        def add_near():
            mine = self.part(self.grad, s - (n - 2))
            mine[...] = mine[...] + self.near_slot[s]
            self.near_sum(s + 1).start()

        def turn():
            own = self.part(self.total, 0)
            mine = self.part(self.grad, 0)
            own[...] = mine[...] + self.far_slot[n - 1] + self.near_slot[n - 2]
            self.far_total(0).start()
            self.near_total(0).start()

        both = lambda p, q: p and q if isinstance(p, bool) else p & q
        i = s - n
        when(s < n, lambda: self.far_sum(s).wait_recv())
        when(s < n - 1, add_far)
        when(s < n - 1, lambda: self.near_sum(s).wait_recv())
        when(s < n - 2, add_near)
        when(s == n - 1, turn)
        when(both(s >= n, s < 2 * n), lambda: self.far_total(i, 1).wait_recv())
        when(both(s >= n, s < 2 * n - 1), lambda: self.far_total(i + 1).start())
        when(both(s >= n, s < 2 * n - 1), lambda: self.near_total(i, 1).wait_recv())
        when(both(s >= n, s < 2 * n - 2), lambda: self.near_total(i + 1).start())

    def end(self):
        part = self.total.at[pl.ds(0, self.height * (self.count - 1)), self.columns]
        for index in (0, self.count - 1):
            self.copy(part, part, index, self.ahead).wait_send()


def unit_scale(values):
    return 1.0 / (jnp.sqrt(jnp.sum(values * values)) + 1e-07)


def halves(values):
    high = values.astype(jnp.bfloat16)
    return high, (values - high.astype(jnp.float32)).astype(jnp.bfloat16)


def thrice(left, right, product):
    a, b = left
    c, d = right
    plain = lambda m, n: product(m, n, None)
    return plain(a, c) + plain(a, d) + plain(b, c)


def idle(product):
    pass


def large_schulz(k, between):
    size = k.x.shape[0]
    tile = 256
    strips = [
        (slice(i * tile, (i + 1) * tile), slice(0, (i + 1) * tile)) for i in range(size // tile)
    ]

    def keep(high, low, rows, columns, values):
        high[rows, columns], low[rows, columns] = halves(values)
        if rows.start:
            turned = values[:, 0 : rows.start].T
            high[0 : rows.start, rows], low[0 : rows.start, rows] = halves(turned)

    def newton_step(step):
        k.xh[...], k.xl[...] = halves(k.x[...])
        for i, (rows, columns) in enumerate(strips):
            gram = thrice((k.xh[rows], k.xl[rows]), (k.xh[columns], k.xl[columns]), nt)
            k.a[rows, columns] = gram
            keep(k.ah, k.al, rows, columns, gram)
        between(3 * step)
        for i, (rows, columns) in enumerate(strips):
            squared = thrice(
                (k.ah[rows], k.al[rows]), (k.ah[:, columns], k.al[:, columns]), nn
            )
            values = schulz_second * k.a[rows, columns] + schulz_third * squared
            keep(k.ph, k.pl, rows, columns, values)
        between(3 * step + 1)
        for i in range(2):
            rows = slice(i * size // 2, (i + 1) * size // 2)
            k.x[rows] = schulz_first * k.x[rows] + thrice(
                (k.ph[rows], k.pl[rows]), (k.xh[...], k.xl[...]), nn
            )
        between(3 * step + 2)

    if between is idle:
        pl.loop(0, 5)(newton_step)
    else:
        for step in range(5):
            newton_step(step)


def small_schulz(moments, results, between):
    current = [moment[...] * unit_scale(moment[...]) for moment in moments]
    for step in range(5):
        split = [halves(values) for values in current]
        grams = [thrice(one, one, nt) for one in split]
        split_grams = [halves(gram) for gram in grams]
        squared = [thrice(one, one, nn) for one in split_grams]
        factors = [
            halves(schulz_second * gram + schulz_third * square)
            for gram, square in zip(grams, squared)
        ]
        current = [
            schulz_first * values + thrice(factor, one, nn)
            for values, factor, one in zip(current, factors, split)
        ]
        between()
    for result, values in zip(results, current):
        result[...] = values


def chain_kernel(dims, names, *refs):
    k = types.SimpleNamespace(**dict(zip(names, refs, strict=True)))
    C, M, Q, GL, CP, cpd, F, LEN, ringed = dims
    R = SEQS * GL
    PW = C // M
    FW = F // M
    D = C * M
    r = lax.axis_index("seq")
    e = lax.axis_index("mp")
    nxt = lax.rem(r + 1, Q)
    prv = lax.rem(r + Q - 1, Q)
    sends = []

    def remote(src, dst, ssem, rsem, seq, mp):
        return pltpu.make_async_remote_copy(
            src_ref=src,
            dst_ref=dst,
            send_sem=ssem,
            recv_sem=rsem,
            device_id={"seq": seq, "mp": mp},
            device_id_type=MESH,
        )

    def swap_blocks(src, dst, phase, same=None):
        for d in range(1, M):
            to = lax.rem(e + d, M)
            source = src.at[to] if same is None else same
            remote(source, dst.at[e], k.mp_sent.at[phase], k.mp_here.at[phase], r, to).start()
        sends.append((dst.at[pl.ds(0, M - 1)], k.mp_sent.at[phase]))
        mine = src[pl.ds(e, 1)] if same is None else same[...].reshape((1,) + same.shape)
        dst[pl.ds(e, 1)] = mine

    def arrive(dst, rsem):
        remote(dst, dst, k.mp_sent.at[0], rsem, nxt, e).wait_recv()

    def blocks_arrive(dst, phase):
        arrive(dst.at[pl.ds(0, M - 1)], k.mp_here.at[phase])

    def swap_seq(src, dst, phase):
        for d in range(1, Q):
            to = lax.rem(r + d, Q)
            remote(
                src.at[to], dst.at[r], k.seq_sent.at[phase], k.seq_here.at[phase], to, e
            ).start()
        sends.append((dst.at[pl.ds(0, Q - 1)], k.seq_sent.at[phase]))
        dst[pl.ds(r, 1)] = src[pl.ds(r, 1)]

    def seq_arrive(dst, phase):
        arrive(dst.at[pl.ds(0, Q - 1)], k.seq_here.at[phase])

    def pieces(dst, values, width):
        for b in range(M):
            dst[b, 0:width] = values[width * b : width * (b + 1)]

    def joined(src, width):
        return jnp.concatenate([src[b, 0:width] for b in range(M)], axis=0)

    def extra(src):
        total = src[0, PW : PW + 8]
        for b in range(1, M):
            total = total + src[b, PW : PW + 8]
        return total[0:1]

    def by_channel(dst, values):
        if CP == cpd:
            dst[...] = values.reshape(Q, CP, values.shape[1])
        else:
            dst[...] = jnp.zeros(dst.shape, jnp.float32)
            for q in range(Q):
                dst[q, 0:cpd] = values[q * cpd : (q + 1) * cpd]

    def from_channels(src):
        if CP == cpd:
            return src[...].reshape(Q * CP, src.shape[2])
        return jnp.concatenate([src[q, 0:cpd] for q in range(Q)], axis=0)

    early = {}
    for i, name in enumerate(EARLY):
        early[name] = pltpu.make_async_copy(
            getattr(k, name + "_hbm"), getattr(k, name), k.esem.at[i]
        )
        early[name].start()
    copies = [
        pltpu.make_async_copy(src, dst, k.wsem.at[i])
        for i, (src, dst) in enumerate(
            (
                (k.sq_hbm, k.sq),
                (k.dl_hbm, k.dl),
                (k.inl_hbm, k.inl),
                (k.ul_hbm, k.ul),
                (k.dr_hbm, k.dr),
            )
        )
    ]
    if ringed:
        copies += [
            pltpu.make_async_copy(getattr(k, f"p{name}_hbm"), dst, k.psem.at[i])
            for i, (name, dst) in enumerate(
                (("dr", k.x), ("ul", k.pul), ("dl", k.pdl), ("sq", k.psq), ("inl", k.pinl))
            )
        ]
    for copy in copies:
        copy.start()

    odd = lax.rem(r, 2)
    place = (1 - odd) * (r // 2) + odd * (Q - 1 - r // 2)

    def at_place(p):
        back = p // (Q // 2)
        return (1 - back) * 2 * p + back * (2 * (Q - 1 - p) + 1)

    ring_ids = tuple(
        {"seq": at_place(lax.rem(place + d, Q)), "mp": e} for d in (1, Q - 1)
    )

    barrier = pltpu.get_barrier_semaphore()
    partners = [(lax.rem(r + d, Q), e) for d in range(1, Q)]
    partners += [(r, lax.rem(e + d, M)) for d in range(1, M)]
    partners += [(s, lax.rem(e + d, M)) for s in (nxt, prv) for d in range(1, M)]
    for seq, mp in partners:
        pl.semaphore_signal(
            barrier, inc=1, device_id={"seq": seq, "mp": mp}, device_id_type=MESH
        )

    first_rings, other_rings, late_rings = [], [], []
    if ringed:

        def ring(grad, total, slots, rows, columns, way, index):
            return Ring(
                grad,
                total,
                *slots,
                k.ring_ssem.at[index],
                k.ring_rsem.at[index],
                rows,
                columns,
                way,
                place,
                Q,
                ring_ids,
            )

        tall, low = F // Q, C // Q
        for way in range(2):
            rows = (tall, way * (tall // 2), tall // 2)
            slots = (k.far_dr.at[way], k.near_dr.at[way])
            first_rings.append(ring(k.gdr, k.tdr, slots, rows, slice(0, F), way, way))
        for rings, grad, total, slots, index in (
            (
                other_rings,
                k.gmid,
                k.tmid,
                ((k.far_mid0, k.near_mid0), (k.far_mid1, k.near_mid1)),
                2,
            ),
            (
                late_rings,
                k.glate,
                k.tlate,
                ((k.far_late0, k.near_late0), (k.far_late1, k.near_late1)),
                4,
            ),
        ):
            width = grad.shape[1]
            cut = width // 256 * 128
            for way, columns in enumerate((slice(0, cut), slice(cut, width))):
                rows = (low, 0, low)
                rings.append(ring(grad, total, slots[way], rows, columns, way, index + way))

    def go(rings, s):
        for one in rings:
            one.event(s)

    outs = []

    def put(source, target):
        copy = pltpu.make_async_copy(source, target, k.osem.at[len(outs)])
        copy.start()
        outs.append(copy)

    halves_done = [0]

    def first_halves(count):
        if ringed:
            for _ in range(count):
                i = halves_done[0]
                first_rings[i % 2].event(i // 2)
                halves_done[0] += 1

    lane = lax.broadcasted_iota(jnp.int32, (1, R), 1)
    spot = lax.rem(lane, GL)
    first_bin = spot == 0
    flip = jnp.where(lax.rem(spot, 2) == 0, 1.0, -1.0).astype(jnp.float32)
    keep_bin = jnp.where(first_bin, 0.0, 1.0).astype(jnp.float32)
    length_of = jnp.where(lane < GL, k.lengths[0], k.lengths[1])
    position = r * GL + spot
    valid = (position < length_of).astype(jnp.float32)
    has_prev = (r > 0).astype(jnp.float32)
    has_next = (r < Q - 1).astype(jnp.float32)
    tail = spot >= GL - 2
    head = spot < 2
    halo_mask = jnp.where(tail, has_prev, jnp.where(head, has_next, 0.0))
    end_row = lax.broadcasted_iota(jnp.int32, (8, R), 0)
    end_lane = lax.rem(end_row, 4) // 2 * GL + lax.rem(end_row, 2)
    end_lane = end_lane + jnp.where(end_row < 4, 0, GL - 2)
    ends = (lax.broadcasted_iota(jnp.int32, (8, R), 1) == end_lane).astype(jnp.float32)

    early["block_in"].wait()
    early["vec"].wait()
    k.xt[...] = k.block_in[...].T
    k.vecp[...] = jnp.zeros(k.vecp.shape, jnp.float32)
    k.vecp[0 : 4 + 3 * KS] = k.vec[...]
    k.vt[...] = k.vecp[...].T

    def column(i):
        return k.vt[:, i : i + 1]

    xt = k.xt[...]
    u0 = xt * column(0)
    k.u0[...] = u0
    copies[0].wait()
    pieces(k.s0, tn(k.sq[0], u0), PW)
    squares = jnp.broadcast_to(jnp.sum(xt * xt, axis=0, keepdims=True), (8, R))
    for b in range(M):
        k.s0[b, PW : PW + 8] = squares
    pl.semaphore_wait(barrier, len(partners))
    swap_blocks(k.s0, k.r0, 0)
    for b in range(M):
        k.hs0[b, :, 0 : PW + 8] = nt(ends, k.s0[b], HIGHEST)
    halo_after, halo_before = [], []
    for d in range(M):
        to = lax.rem(e + d, M)
        for copies_to, dst, i, seq in ((halo_after, k.hp0, 0, nxt), (halo_before, k.hn0, 1, prv)):
            copies_to.append(
                remote(k.hs0.at[to], dst.at[e], k.halo_sent.at[i], k.halo_here.at[i], seq, to)
            )

    @pl.when(r < Q - 1)
    def _():
        for copy in halo_after:
            copy.start()

    @pl.when(r > 0)
    def _():
        for copy in halo_before:
            copy.start()

    @pl.when(r == 0)
    def _():
        k.hp0[...] = jnp.zeros(k.hp0.shape, jnp.float32)

    @pl.when(r == Q - 1)
    def _():
        k.hn0[...] = jnp.zeros(k.hn0.shape, jnp.float32)

    early["out_grad"].wait()
    k.ogt[...] = k.out_grad[...].T
    copies[1].wait()
    pieces(k.s4, tn(k.dl[...], k.ogt[...]), FW)
    swap_blocks(k.s4, k.r4, 4)
    by_channel(k.vtc, k.vt[...])
    early["fo"].wait()
    by_channel(k.foc, k.fo[...])
    copies[2].wait()

    blocks_arrive(k.r0, 0)

    @pl.when(r > 0)
    def _():
        arrive(k.hp0, k.halo_here.at[0])

    @pl.when(r < Q - 1)
    def _():
        arrive(k.hn0, k.halo_here.at[1])

    scale_one = lax.rsqrt(extra(k.r0) / D + norm_epsilon)
    w0 = joined(k.r0, PW)
    k.w0[...] = w0
    z = tn(k.inl[...], w0) * scale_one
    first_half = lax.broadcasted_iota(jnp.int32, (8, 128), 0) < 4
    spread = [
        tn(jnp.where(first_half, k.hn0[b], k.hp0[b]), ends, HIGHEST) for b in range(M)
    ]
    w0h = jnp.concatenate([one[0:PW] for one in spread], axis=0)
    squares = spread[0][PW : PW + 1]
    for b in range(1, M):
        squares = squares + spread[b][PW : PW + 1]
    zh = tn(k.inl[...], w0h) * (lax.rsqrt(squares / D + norm_epsilon) * halo_mask)
    zh_far = pltpu.roll(zh, GL, 1)
    k.z[...] = z
    k.z1[...] = pltpu.roll(jnp.where(spot >= GL - 1, zh_far, z), 1, 1)
    k.z2[...] = pltpu.roll(jnp.where(tail, zh_far, z), 2, 1)
    for s in range(3):
        part = slice(s * C, (s + 1) * C)
        k.conv[part] = (
            column(4 + KS * s) * k.z[part]
            + column(5 + KS * s) * k.z1[part]
            + column(6 + KS * s) * k.z2[part]
        )
    product = k.conv[0:C] * k.conv[2 * C : 3 * C] * valid
    k.prod[...] = product
    by_channel(k.ps, product)
    swap_seq(k.ps, k.ur, 0)

    for name in EARLY[4:]:
        early[name].wait()
    pre = filter_frequency * nn(k.feat[...], k.fh[0:8], HIGHEST)
    k.l1[...] = jnp.sin(pre)
    k.c1[...] = filter_frequency * jnp.cos(pre)
    pre = filter_frequency * nn(k.l1[...], k.fh[EMB : EMB + 128], HIGHEST)
    k.l2[...] = jnp.sin(pre)
    k.c2[...] = filter_frequency * jnp.cos(pre)
    foc = k.foc[pl.ds(r, 1)].reshape(CP, 128)
    vtc = k.vtc[pl.ds(r, 1)].reshape(CP, 128)
    rate = vtc[:, 2:3]
    skip_channel = vtc[:, 3:4]
    shaped = nt(foc, k.l2[...], HIGHEST)
    part_lane = lax.broadcasted_iota(jnp.int32, (1, GL), 1)
    for q in range(Q):
        fraction = (part_lane + q * GL).astype(jnp.float32) / LEN
        decay = jnp.exp(-fraction * rate) * (LEN ** (-0.5))
        k.decay[q] = decay
        k.taps[q] = shaped[:, q * GL : (q + 1) * GL] * decay
    spectrum = nn(k.taps[...].reshape(Q * CP, GL), k.ttap[...]).reshape(Q, CP, 2 * R)
    for q in range(Q):
        real = spectrum[q, :, 0:R]
        imag = spectrum[q, :, R : 2 * R]
        if q > 0:
            real = real + flip * spectrum[q - 1, :, 0:R]
            imag = imag + flip * spectrum[q - 1, :, R : 2 * R]
        k.kr[q] = real
        k.km[q] = imag * keep_bin
        k.k4[q] = jnp.where(first_bin, imag, real)

    def total_pairs(count, first, term):
        zero = jnp.zeros((CP, R), jnp.float32)
        if Q <= 8:
            real, imag = zero, zero
            for i in range(count):
                add_real, add_imag = term(first + i)
                real, imag = real + add_real, imag + add_imag
            return real, imag

        def body(i, kept):
            add_real, add_imag = term(first + i)
            return (kept[0] + add_real, kept[1] + add_imag)

        return lax.fori_loop(0, count, body, (zero, zero))

    def each_block(body):
        if Q <= 8:
            for q in range(Q):
                body(q)
        else:
            pl.loop(0, Q)(body)

    seq_arrive(k.ur, 0)
    k.us[...] = nn(k.ur[...].reshape(Q * CP, R), k.tfwd[...]).reshape(Q, CP, 2 * R)

    def forward_block(p):
        def term(q):
            real = k.us[q, :, 0:R]
            imag = k.us[q, :, R : 2 * R]
            lag = p - q
            return (
                k.kr[lag] * real - k.km[lag] * imag,
                k.km[lag] * real + k.k4[lag] * imag,
            )

        real, imag = total_pairs(p + 1, 0, term)
        k.zs[p, :, 0:R] = real
        k.zs[p, :, R : 2 * R] = imag

    each_block(forward_block)
    k.ys[...] = nn(k.zs[...].reshape(Q * CP, 2 * R), k.tinv[...]).reshape(Q, CP, R)
    swap_seq(k.ys, k.yr, 1)
    for q in range(Q):
        real = k.us[q, :, 0:R]
        imag = k.us[q, :, R : 2 * R]
        k.um[q] = imag * keep_bin
        k.u4[q] = jnp.where(first_bin, imag, real)

    seq_arrive(k.yr, 1)
    inner_sum = from_channels(k.yr) + column(3) * k.prod[...]
    k.insum[...] = inner_sum
    gated = k.conv[C : 2 * C] * inner_sum
    k.gated[...] = gated
    pieces(k.s1, tn(k.sq[1], gated), PW)
    swap_blocks(k.s1, k.r1, 1)

    copies[4].wait()
    blocks_arrive(k.r4, 4)
    k.dact[...] = nn(k.dr[...], k.r4[...].reshape(F, R))
    copies[3].wait()

    blocks_arrive(k.r1, 1)
    w1 = k.r1[...].reshape(C, R)
    k.w1[...] = w1
    h = k.xt[...] + tn(k.sq[2], w1)
    k.h[...] = h
    u3 = h * column(1)
    pieces(k.s2, tn(k.sq[3], u3), PW)
    squares = jnp.broadcast_to(jnp.sum(h * h, axis=0, keepdims=True), (8, R))
    for b in range(M):
        k.s2[b, PW : PW + 8] = squares
    swap_blocks(k.s2, k.r2, 2)

    blocks_arrive(k.r2, 2)
    scale_two = lax.rsqrt(extra(k.r2) / D + norm_epsilon)
    k.n2[...] = k.h[...] * scale_two
    w3 = joined(k.r2, PW)
    k.w3[...] = w3
    k.gu[...] = tn(k.ul[...], w3) * scale_two
    gate = k.gu[0:F]
    up = k.gu[F : 2 * F]
    bend = jnp.tanh(gelu_scale * (gate + gelu_cubic * gate * gate * gate))
    gelu = 0.5 * gate * (1.0 + bend)
    slope = 0.5 * (1.0 + bend) + 0.5 * gate * (1.0 - bend * bend) * gelu_scale * (
        1.0 + 3.0 * gelu_cubic * gate * gate
    )
    dact = k.dact[...]
    k.act[...] = gelu * up
    k.dgu[0:F] = dact * up * slope
    k.dgu[F : 2 * F] = dact * gelu
    back = nn(k.ul[...], k.dgu[...])
    pieces(k.s5, back, PW)
    inner = jnp.broadcast_to(jnp.sum(back * k.w3[...], axis=0, keepdims=True), (8, R))
    for b in range(M):
        k.s5[b, PW : PW + 8] = inner
    swap_blocks(k.s5, k.r5, 5)
    k.gdr[...] = nt(k.act[...], k.r4[...].reshape(F, R))
    for one in first_rings:
        one.begin()
    pieces(k.s3, tn(k.dr[...], k.act[...]), FW)
    swap_blocks(k.s3, k.r3, 3)

    k.gmid[:, 0 : 2 * F] = nt(k.w3[...] * scale_two, k.dgu[...])
    blocks_arrive(k.r5, 5)
    back = joined(k.r5, PW)
    inner = extra(k.r5)
    grad_two = nn(k.sq[3], back)
    hidden_grad = (
        k.ogt[...]
        + scale_two * (grad_two * column(1))
        - k.h[...] * (scale_two * scale_two * scale_two * inner / D)
    )
    k.hg[...] = hidden_grad
    pieces(k.s6, nn(k.sq[2], hidden_grad), PW)
    swap_blocks(k.s6, k.r6, 6)
    first_halves(1)
    k.glate[:, 3 * C : 4 * C] = nt(k.n2[...] * column(1), back)
    gain_two = jnp.sum(grad_two * k.n2[...], axis=1, keepdims=True)
    k.glate[:, 2 * C : 3 * C] = nt(k.w1[...], k.hg[...])

    first_halves(1)
    blocks_arrive(k.r6, 6)
    back = k.r6[...].reshape(C, R)
    gated_grad = nn(k.sq[1], back)
    inner_grad = gated_grad * k.conv[C : 2 * C]
    k.inner[...] = inner_grad
    k.d1[...] = gated_grad * k.insum[...]
    by_channel(k.inner_s, inner_grad)
    swap_seq(k.inner_s, k.vr, 2)
    k.glate[:, C : 2 * C] = nt(k.gated[...], back)
    skip_total = jnp.sum(inner_grad * k.prod[...], axis=1, keepdims=True)

    first_halves(2)
    seq_arrive(k.vr, 2)
    k.vs[...] = nn(k.vr[...].reshape(Q * CP, R), k.tfwd[...]).reshape(Q, CP, 2 * R)

    def back_block(q):
        def term(p):
            real = k.vs[p, :, 0:R]
            imag = k.vs[p, :, R : 2 * R]
            lag = p - q
            return (
                k.kr[lag] * real + k.km[lag] * imag,
                k.k4[lag] * imag - k.km[lag] * real,
            )

        real, imag = total_pairs(Q - q, q, term)
        k.zs[q, :, 0:R] = real
        k.zs[q, :, R : 2 * R] = imag

    each_block(back_block)
    k.ds[...] = (
        nn(k.zs[...].reshape(Q * CP, 2 * R), k.tinv[...]).reshape(Q, CP, R)
        + skip_channel[None] * k.vr[...]
    )
    swap_seq(k.ds, k.dmain, 3)
    first_halves(1)
    def lag_block(j):
        def term(p):
            real = k.vs[p, :, 0:R]
            imag = k.vs[p, :, R : 2 * R]
            q = p - j
            return (
                k.us[q, :, 0:R] * real + k.um[q] * imag,
                k.u4[q] * imag - k.um[q] * real,
            )

        real, imag = total_pairs(Q - j, j, term)
        k.zs[j, :, 0:R] = real
        k.zs[j, :, R : 2 * R] = imag

    each_block(lag_block)
    cross = k.zs[...].reshape(Q * CP, 2 * R)
    near = nn(cross, k.tw1[...]).reshape(Q, CP, GL)
    far = nn(cross, k.tw2[...]).reshape(Q, CP, GL)
    decay_total = jnp.zeros((CP, 1), jnp.float32)
    for q in range(Q):
        grad = near[q]
        if q < Q - 1:
            grad = grad + far[q + 1]
        fraction = (part_lane + q * GL).astype(jnp.float32) / LEN
        decay_total = decay_total - jnp.sum(
            grad * k.taps[q] * fraction, axis=1, keepdims=True
        )
        k.draw[:, q * GL : (q + 1) * GL] = grad * k.decay[q]
    raw = k.draw[...]
    k.gfo[...] = jnp.zeros(k.gfo.shape, jnp.float32)
    k.gdec[...] = jnp.zeros(k.gdec.shape, jnp.float32)
    k.gfo[pl.ds(r, 1)] = nn(raw, k.l2[...]).reshape(1, CP, 128)
    k.gdec[pl.ds(r, 1)] = jnp.broadcast_to(decay_total, (CP, 128)).reshape(1, CP, 128)
    first_halves(1)
    blocks_arrive(k.r3, 3)
    w4 = k.r3[...].reshape(F, R)
    k.block_out[...] = (k.h[...] + nn(k.dl[...], w4)).T
    put(k.block_out, k.block_out_hbm)
    k.gmid[:, 2 * F : 3 * F] = nt(k.ogt[...], w4)
    back = tn(raw, foc) * k.c2[...]
    k.hid[8:136] = tn(k.l1[...], back)
    back = nt(back, k.fh[EMB : EMB + 128]) * k.c1[...]
    k.hid[0:8] = tn(k.feat[...], back)
    swap_blocks(None, k.hids, 8, k.hid)


    first_halves(1)
    seq_arrive(k.dmain, 3)
    product_grad = from_channels(k.dmain) * valid
    k.d3[0:C] = product_grad * k.conv[2 * C : 3 * C]
    k.d3[C : 2 * C] = k.d1[...]
    k.d3[2 * C : 3 * C] = product_grad * k.conv[0:C]
    k.hs1[...] = nt(ends, k.d3[...], HIGHEST)
    edge = remote(k.hs1, k.hr1, k.halo_sent.at[2], k.halo_here.at[2], prv, e)

    @pl.when(r > 0)
    def _():
        edge.start()

    @pl.when(r == Q - 1)
    def _():
        k.hr1[...] = jnp.zeros(k.hr1.shape, jnp.float32)

    first_halves(1)

    @pl.when(r < Q - 1)
    def _():
        arrive(k.hr1, k.halo_here.at[2])

    following = pltpu.roll(tn(k.hr1[...], ends, HIGHEST), GL, 1)
    tap_totals = []
    for s in range(3):
        part = slice(s * C, (s + 1) * C)
        grad = k.d3[part]
        one = pltpu.roll(jnp.where(spot == 0, following[part], grad), R - 1, 1)
        two = pltpu.roll(jnp.where(head, following[part], grad), R - 2, 1)
        k.dz[part] = (
            column(4 + KS * s) * grad + column(5 + KS * s) * one + column(6 + KS * s) * two
        )
        for shifted in (k.z, k.z1, k.z2):
            tap_totals.append(jnp.sum(grad * shifted[part], axis=1, keepdims=True))
    back = nn(k.inl[...], k.dz[...])
    pieces(k.s7, back, PW)
    inner = jnp.broadcast_to(jnp.sum(back * k.w0[...], axis=0, keepdims=True), (8, R))
    for b in range(M):
        k.s7[b, PW : PW + 8] = inner
    swap_blocks(k.s7, k.r7, 7)
    k.glate[:, 4 * C : 7 * C] = nt(k.w0[...] * scale_one, k.dz[...])

    first_halves(1)
    blocks_arrive(k.r7, 7)
    back = joined(k.r7, PW)
    inner = extra(k.r7)
    grad_one = nn(k.sq[0], back)
    xt = k.xt[...]
    k.input_grad[...] = (
        k.hg[...]
        + scale_one * (grad_one * column(0))
        - xt * (scale_one * scale_one * scale_one * inner / D)
    ).T
    put(k.input_grad, k.input_grad_hbm)
    k.glate[:, 0:C] = nt(k.u0[...] * scale_one, back)
    gain_one = jnp.sum(grad_one * xt * scale_one, axis=1, keepdims=True)
    starts, width = late_columns(C)
    slot = lax.broadcasted_iota(jnp.int32, (1, 16), 1)
    rows = {0: gain_one, 1: gain_two, 2: from_channels(k.gdec)[:, 0:1], 3: skip_total}
    rows.update({4 + i: total for i, total in enumerate(tap_totals)})
    stacked = jnp.zeros((C, 16), jnp.float32)
    for i, total in rows.items():
        stacked = jnp.where(slot == i, total, stacked)
    k.glate[:, starts[2] : starts[3]] = jnp.zeros((C, starts[3] - starts[2]), jnp.float32)
    k.glate[:, starts[2] : starts[2] + 16] = stacked
    k.glate[:, starts[3] : starts[4]] = from_channels(k.gfo)
    first_halves(1)
    blocks_arrive(k.hids, 8)
    hidden_sum = k.hids[0]
    for b in range(1, M):
        hidden_sum = hidden_sum + k.hids[b]
    k.glate[0:136, starts[4] : width] = hidden_sum
    k.glate[136:C, starts[4] : width] = jnp.zeros((C - 136, 128), jnp.float32)

    if ringed:
        first_halves(2 * Q - 2 - halves_done[0])
        for one in other_rings + late_rings:
            one.begin()
        first_halves(2)
        for copy in copies[5:]:
            copy.wait()
        moment = momentum_decay * k.x[...] + k.tdr[...]
        k.moment[...] = moment
        put(k.moment, k.out_pdr)
        k.x[...] = moment * unit_scale(moment)
        mid_turns, late_turns = iter(range(Q)), iter(range(Q))

        def turn(rings, turns):
            s = next(turns, None)
            if s is not None:
                go(rings, s)

        def between(product):
            if product % 2 == 0:
                turn(other_rings, mid_turns)
            if product in LATE_AFTER:
                turn(late_rings, late_turns)

        large_schulz(k, between)
        put(k.x, k.out_odr)
        for s in mid_turns:
            go(other_rings, s)
        for dst, moment, columns in (
            (k.ul, k.pul, slice(0, 2 * F)),
            (k.dl, k.pdl, slice(2 * F, 3 * F)),
        ):
            dst[...] = momentum_decay * moment[...] + k.tmid[:, columns]
        put(k.ul, k.out_pul)
        put(k.dl, k.out_pdl)
        small_schulz((k.ul, k.dl), (k.oul, k.odl), lambda: turn(late_rings, late_turns))
        put(k.oul, k.out_oul)
        put(k.odl, k.out_odl)
        for s in late_turns:
            go(late_rings, s)
        put(k.tlate.at[:, width - SMALL :], k.out_small)
        for i in range(4):
            k.sq[i] = momentum_decay * k.psq[i] + k.tlate[:, i * C : (i + 1) * C]
        k.inl[...] = momentum_decay * k.pinl[...] + k.tlate[:, starts[1] : starts[2]]
        put(k.sq, k.out_psq)
        put(k.inl, k.out_pinl)
        small_schulz(
            [k.sq.at[i] for i in range(4)] + [k.inl],
            [k.osq.at[i] for i in range(4)] + [k.oinl],
            lambda: None,
        )
        put(k.oinl, k.out_oinl)
        put(k.osq, k.out_osq)
        for one in first_rings + other_rings + late_rings:
            one.end()
    else:
        put(k.gdr, k.out_dr)
        put(k.gmid, k.out_mid)
        put(k.glate, k.out_late)
    for copy in outs:
        copy.wait()
    for ref, sem in sends:
        remote(ref, ref, sem, k.mp_here.at[0], nxt, e).wait_send()

    @pl.when(r < Q - 1)
    def _():
        remote(k.hs0, k.hp0, k.halo_sent.at[0], k.halo_here.at[0], nxt, e).wait_send()

    @pl.when(r > 0)
    def _():
        remote(k.hs0, k.hn0, k.halo_sent.at[1], k.halo_here.at[1], prv, e).wait_send()
        edge.wait_send()


def run_chain(x, og, lengths, weights, moments, vectors, fh, fo):
    M, Q = lax.axis_size("mp"), lax.axis_size("seq")
    sq, inl, ul, dr, dl = weights
    _, GL, C = x.shape
    R = SEQS * GL
    F = dr.shape[0]
    LEN = GL * Q
    cpd = C // Q
    CP = -(-cpd // 8) * 8
    PW, FW = C // M, F // M
    ringed = cpd % 8 == 0 and F % (32 * Q) == 0
    dims = (C, M, Q, GL, CP, cpd, F, LEN, ringed)
    tables = spectrum_tables(GL)
    feat = feature_table(LEN)
    width = late_columns(C)[1]
    sds = lambda *shape: jax.ShapeDtypeStruct(shape, jnp.float32)
    v = lambda *shape: pltpu.VMEM(shape, jnp.float32)
    dma = lambda *shape: pltpu.SemaphoreType.DMA(shape)
    first = dict(
        block_in=x.reshape(R, C),
        out_grad=og.reshape(R, C),
        vec=vectors,
        fh=fh,
        fo=fo,
        feat=feat,
        **dict(zip(("tfwd", "ttap", "tinv", "tw1", "tw2"), tables)),
    )
    in_hbm = {name + "_hbm": array for name, array in first.items()}
    in_hbm.update(sq_hbm=sq, inl_hbm=inl, ul_hbm=ul, dr_hbm=dr, dl_hbm=dl)
    if ringed:
        in_hbm.update((f"p{name}_hbm", moment) for name, moment in zip(KINDS, moments))
    out_first = dict(block_out=sds(R, C), input_grad=sds(R, C))
    out_hbm = dict(out_dr=sds(F, F), out_mid=sds(C, 3 * F), out_late=sds(C, width))
    if ringed:
        out_hbm = {f"out_{x}{n}": sds(*w.shape) for x in "po" for n, w in zip(KINDS, weights)}
        out_hbm["out_small"] = sds(C, SMALL)
    scratch = dict(
        sq=v(4, C, C),
        inl=v(C, 3 * C),
        ul=v(C, 2 * F),
        dr=v(F, F),
        dl=v(C, F),
        vecp=v(128, C),
        vt=v(C, 128),
        vtc=v(Q, CP, 128),
        foc=v(Q, CP, 128),
        gfo=v(Q, CP, 128),
        gdec=v(Q, CP, 128),
        gu=v(2 * F, R),
        act=v(F, R),
        dact=v(F, R),
        dgu=v(2 * F, R),
        block_out=v(R, C),
        input_grad=v(R, C),
        hid=v(136, 128),
        hs0=v(M, 8, 128),
        hp0=v(M, 8, 128),
        hn0=v(M, 8, 128),
        hs1=v(8, 3 * C),
        hr1=v(8, 3 * C),
        hids=v(M, 136, 128),
        taps=v(Q, CP, GL),
        decay=v(Q, CP, GL),
        draw=v(CP, LEN),
        gdr=v(F, F),
        gmid=v(C, 3 * F),
        glate=v(C, width),
    )
    for name, array in first.items():
        scratch[name] = v(*array.shape)
    scratch["esem"] = dma(len(first))
    for name in ("xt", "ogt", "u0", "prod", "insum", "gated", "w0", "w1", "w3", "h", "n2", "hg", "inner", "d1"):
        scratch[name] = v(C, R)
    for name in ("z", "z1", "z2", "conv", "dz", "d3"):
        scratch[name] = v(3 * C, R)
    for name in ("l1", "c1", "l2", "c2"):
        scratch[name] = v(LEN, 128)
    for name in ("kr", "km", "k4", "um", "u4", "ps", "ur", "ys", "yr", "inner_s", "vr", "ds", "dmain"):
        scratch[name] = v(Q, CP, R)
    for name in ("us", "vs", "zs"):
        scratch[name] = v(Q, CP, 2 * R)
    for name in ("s0", "r0", "s2", "r2", "s5", "r5", "s7", "r7"):
        scratch[name] = v(M, PW + 8, R)
    for name in ("s1", "r1", "s6", "r6"):
        scratch[name] = v(M, PW, R)
    for name in ("s3", "r3", "s4", "r4"):
        scratch[name] = v(M, FW, R)
    scratch.update(
        wsem=dma(5),
        osem=dma(13),
        mp_sent=dma(9),
        mp_here=dma(9),
        seq_sent=dma(4),
        seq_here=dma(4),
        halo_sent=dma(3),
        halo_here=dma(3),
    )
    if ringed:
        scratch.update(
            tdr=v(F, F),
            tmid=v(C, 3 * F),
            tlate=v(C, width),
            far_dr=v(2, Q // 2, F // Q // 2, F),
            near_dr=v(2, Q // 2 - 1, F // Q // 2, F),
            ring_ssem=dma(6, 2),
            ring_rsem=dma(6, 2 * Q - 2),
            x=v(F, F),
            a=v(F, F),
            moment=v(F, F),
            psem=dma(5),
            psq=v(4, C, C),
            osq=v(4, C, C),
            pinl=v(C, 3 * C),
            oinl=v(C, 3 * C),
            pul=v(C, 2 * F),
            oul=v(C, 2 * F),
            pdl=v(C, F),
            odl=v(C, F),
        )
        for name in ("xh", "xl", "ah", "al", "ph", "pl"):
            scratch[name] = pltpu.VMEM((F, F), jnp.bfloat16)
        for name, columns in (("mid", 3 * F), ("late", width)):
            cut = columns // 256 * 128
            for i, part in enumerate((cut, columns - cut)):
                scratch[f"far_{name}{i}"] = v(Q // 2, C // Q, part)
                scratch[f"near_{name}{i}"] = v(Q // 2 - 1, C // Q, part)
    vmem = pl.BlockSpec(memory_space=pltpu.VMEM)
    smem = pl.BlockSpec(memory_space=pltpu.SMEM)
    hbm = pl.BlockSpec(memory_space=pl.ANY)
    names = ["lengths", *in_hbm, *(f"{name}_hbm" for name in out_first), *out_hbm, *scratch]
    outs = pl.pallas_call(
        functools.partial(chain_kernel, dims, names),
        out_shape=[*out_first.values(), *out_hbm.values()],
        in_specs=[smem] + [hbm] * len(in_hbm),
        out_specs=[hbm] * (len(out_first) + len(out_hbm)),
        scratch_shapes=list(scratch.values()),
        compiler_params=pltpu.CompilerParams(
            collective_id=0, has_side_effects=True, vmem_limit_bytes=60 * 2**20
        ),
        name="chain",
    )(lengths, *in_hbm.values())
    block_out, input_grad, *rest = outs
    if ringed:
        return block_out, input_grad, dict(zip(out_hbm, rest))
    totals = lax.psum(rest, "seq")
    return block_out, input_grad, dict(zip(out_hbm, totals))


def adam(refs, gradient, rate):
    weights, first, second, first_out, second_out, weights_out, copy_out = refs
    first_new = beta_first * first[...] + (1.0 - beta_first) * gradient
    second_new = beta_second * second[...] + (1.0 - beta_second) * gradient * gradient
    corrected_first = first_new / (1.0 - beta_first**STEP)
    corrected_second = second_new / (1.0 - beta_second**STEP)
    old = weights[...]
    new = old - rate * (
        corrected_first / (jnp.sqrt(corrected_second) + adam_epsilon) + weight_decay * old
    )
    first_out[...] = first_new
    second_out[...] = second_new
    weights_out[...] = new
    copy_out[...] = new.astype(jnp.bfloat16)


def update_kernel(names, loaded, stored, ringed, *refs):
    k = types.SimpleNamespace(**dict(zip(names, refs, strict=True)))
    C = k.wsq.shape[1]
    F = k.wdr.shape[0]
    starts, width = late_columns(C)
    reads = {
        name: pltpu.make_async_copy(
            getattr(k, "hbm_" + name), getattr(k, name), k.read_sem.at[i]
        )
        for i, name in enumerate(loaded)
    }
    writes = {
        name: pltpu.make_async_copy(
            getattr(k, source), getattr(k, "hbm_" + name), k.write_sem.at[i]
        )
        for i, (name, source) in enumerate(stored.items())
    }
    for copy in reads.values():
        copy.start()

    def need(*wanted):
        for name in wanted:
            reads[name].wait()

    def put(*done):
        for name in done:
            writes[name].start()

    if not ringed:
        need("glate", "gmid", "gdr", *["p" + name for name in KINDS])
        totals = {
            "inl": k.glate[:, starts[1] : starts[2]],
            "ul": k.gmid[:, 0 : 2 * F],
            "dr": k.gdr[...],
            "dl": k.gmid[:, 2 * F : 3 * F],
        }
        for i in range(4):
            k.msq[i] = momentum_decay * k.psq[i] + k.glate[:, i * C : (i + 1) * C]
        for name, total in totals.items():
            moment = momentum_decay * getattr(k, "p" + name)[...] + total
            getattr(k, "m" + name)[...] = moment
        moment = k.mdr[...]
        k.x[...] = moment * unit_scale(moment)
        small_schulz(
            [k.msq.at[i] for i in range(4)] + [k.minl, k.mul, k.mdl],
            [k.osq.at[i] for i in range(4)] + [k.oinl, k.oul, k.odl],
            lambda: None,
        )
        large_schulz(k, idle)
        k.odr[...] = k.x[...]
    for name in ("dr", "ul", "sq", "dl", "inl"):
        if ringed:
            need("m" + name)
        put(("new_m" if ringed else "m") + name)
        if ringed:
            need("o" + name)
        need("w" + name)
        rows, cols = getattr(k, "w" + name).shape[-2:]
        if name == "dl":
            rows = cols
        scale = muon_rate * math.sqrt(max(rows, cols) / rows)
        new = getattr(k, "w" + name)[...] - scale * getattr(k, "o" + name)[...]
        getattr(k, "n" + name)[...] = new
        getattr(k, "c" + name)[...] = new.astype(jnp.bfloat16)
        put("n" + name, "c" + name)

    if ringed:
        need("block_out", "input_grad", "small")
        put("new_block_out", "new_input_grad")
        small = k.small[...]
    else:
        small = k.glate[:, width - SMALL :]
    shift = width - SMALL
    lead = starts[2] - shift
    turned = small[:, 0:128].T
    vector_grad = turned[lead : lead + 16][0 : 4 + 3 * KS]
    hidden = small[:, starts[4] - shift :]
    hidden_grad = jnp.concatenate([hidden[0:EMB], hidden[8:136]], axis=0)
    for name, gradient, rate in (
        ("v", vector_grad, rate_vectors),
        ("h", hidden_grad, rate_hidden),
        ("f", small[:, starts[3] - shift : starts[4] - shift], rate_output),
    ):
        adam(
            [getattr(k, name + kind) for kind in ("w", "1", "2", "1n", "2n", "n", "c")],
            gradient,
            rate,
        )
    for copy in writes.values():
        copy.wait()


def run_update(chained, tokens, moments, weights, small):
    ringed = "out_small" in chained
    arrays = {"w" + name: weight for name, weight in zip(KINDS, weights)}
    shapes = {name: weight.shape for name, weight in zip(KINDS, weights)}
    if ringed:
        arrays.update({"m" + name: chained["out_p" + name] for name in KINDS})
        arrays.update({"o" + name: chained["out_o" + name] for name in KINDS})
        arrays["small"] = chained["out_small"]
        loaded = [kind + name for name in ("dr", "ul", "sq", "dl", "inl") for kind in "mow"]
        loaded.append("small")
        for name, array in tokens.items():
            arrays[name] = array
            loaded.append(name)
    else:
        arrays.update({"p" + name: moment for name, moment in zip(KINDS, moments)})
        arrays.update({"g" + name: chained["out_" + name] for name in ("dr", "mid", "late")})
        loaded = list(arrays)
    in_hbm = {"hbm_" + name: array for name, array in arrays.items()}
    out_hbm, stored = {}, {}
    scratch = {name: pltpu.VMEM(arrays[name].shape, jnp.float32) for name in loaded}
    for name, shape in shapes.items():
        for kind, dtype in (("m", jnp.float32), ("n", jnp.float32), ("c", jnp.bfloat16)):
            target = ("new_" if kind == "m" and ringed else "") + kind + name
            out_hbm["hbm_" + target] = jax.ShapeDtypeStruct(shape, dtype)
            stored[target] = kind + name
            scratch.setdefault(kind + name, pltpu.VMEM(shape, dtype))
        if not ringed:
            scratch["o" + name] = pltpu.VMEM(shape, jnp.float32)
    if ringed:
        for name, array in tokens.items():
            out_hbm["hbm_new_" + name] = jax.ShapeDtypeStruct(array.shape, jnp.float32)
            stored["new_" + name] = name
    in_vmem, out_vmem = {}, {}
    for name, (weight, first, second) in small.items():
        in_vmem[name + "w"], in_vmem[name + "1"], in_vmem[name + "2"] = weight, first, second
        for suffix in ("1n", "2n", "n"):
            out_vmem[name + suffix] = jax.ShapeDtypeStruct(weight.shape, jnp.float32)
        out_vmem[name + "c"] = jax.ShapeDtypeStruct(weight.shape, jnp.bfloat16)
    if not ringed:
        size = shapes["dr"]
        scratch.update({n: pltpu.VMEM(size, jnp.float32) for n in ("x", "a")})
        for name in ("xh", "xl", "ah", "al", "ph", "pl"):
            scratch[name] = pltpu.VMEM(size, jnp.bfloat16)
    scratch["read_sem"] = pltpu.SemaphoreType.DMA((len(loaded),))
    scratch["write_sem"] = pltpu.SemaphoreType.DMA((len(stored),))
    vmem = pl.BlockSpec(memory_space=pltpu.VMEM)
    hbm = pl.BlockSpec(memory_space=pl.ANY)
    names = [*in_hbm, *in_vmem, *out_hbm, *out_vmem, *scratch]
    results = pl.pallas_call(
        functools.partial(update_kernel, names, loaded, stored, ringed),
        out_shape=[*out_hbm.values(), *out_vmem.values()],
        in_specs=[hbm] * len(in_hbm) + [vmem] * len(in_vmem),
        out_specs=[hbm] * len(out_hbm) + [vmem] * len(out_vmem),
        scratch_shapes=list(scratch.values()),
        compiler_params=pltpu.CompilerParams(vmem_limit_bytes=60 * 2**20),
        name="update",
    )(*in_hbm.values(), *in_vmem.values())
    new = dict(zip([*out_hbm, *out_vmem], results))
    return {name.removeprefix("hbm_").removeprefix("new_"): value for name, value in new.items()}


def per_device(
    block_input,
    out_grad,
    lengths,
    square_factors,
    square_moment,
    input_left,
    input_left_moment,
    up_left,
    up_left_moment,
    down_right,
    down_right_moment,
    down_left,
    down_left_moment,
    vectors,
    vectors_first,
    vectors_second,
    filter_hidden,
    hidden_first,
    hidden_second,
    filter_out,
    filter_out_first,
    filter_out_second,
):
    weights = (square_factors[:, 0], input_left[0], up_left[0], down_right[0], down_left[0].T)
    moments = (
        square_moment[:, 0],
        input_left_moment[0],
        up_left_moment[0],
        down_right_moment[0],
        down_left_moment[0].T,
    )
    block_output, input_grad, chained = run_chain(
        block_input, out_grad, lengths, weights, moments, vectors, filter_hidden, filter_out.T
    )
    small = dict(
        v=(vectors, vectors_first, vectors_second),
        h=(filter_hidden, hidden_first, hidden_second),
        f=(filter_out.T, filter_out_first.T, filter_out_second.T),
    )
    tokens = dict(block_out=block_output, input_grad=input_grad)
    new = tokens | run_update(chained, tokens, moments, weights, small)
    return (
        new["block_out"].reshape(block_input.shape),
        new["input_grad"].reshape(block_input.shape),
        *[new[kind + "sq"][:, None] for kind in "mnc"],
        *[new[kind + name][None] for name in ("inl", "ul", "dr") for kind in "mnc"],
        *[new[kind + "dl"].T[None] for kind in "mnc"],
        *[new[name + suffix] for name in "vh" for suffix in ("1n", "2n", "n", "c")],
        *[new["f" + suffix].T for suffix in ("1n", "2n", "n", "c")],
    )


def solution(mesh):
    tokens = P(None, "seq", "mp")
    square = P(None, "mp", None, None)
    block = P("mp", None, None)
    row = P(None, "mp")
    return jax.shard_map(
        per_device,
        mesh=mesh,
        in_specs=(tokens, tokens, P(), square, square)
        + (block,) * 8
        + (row,) * 3
        + (P(),) * 3
        + (row,) * 3,
        out_specs=(tokens, tokens)
        + (square,) * 3
        + (block,) * 12
        + (row,) * 4
        + (P(),) * 4
        + (row,) * 4,
        check_vma=False,
    )
```

```python
import functools
import math
import types

import jax
import jax.numpy as jnp
import numpy as np
from jax import lax
from jax.experimental import pallas as pl
from jax.experimental.pallas import tpu as pltpu
from jax.sharding import PartitionSpec as P

EMB = 5
KS = 3
STEP = 10
SEQS = 2

HIGH = lax.Precision.HIGH
HIGHEST = lax.Precision.HIGHEST
MESH = pl.DeviceIdType.MESH
norm_epsilon = 1e-05
beta_first = 0.9
beta_second = 0.95
adam_epsilon = 1e-08
weight_decay = 0.01
rate_vectors = 0.2
rate_hidden = 0.05
rate_output = 0.05
muon_rate = 0.5
momentum_decay = 0.5
schulz_first = 3.4445
schulz_second = -4.775
schulz_third = 2.0315
filter_frequency = 10.0
gelu_scale = math.sqrt(2.0 / math.pi)
gelu_cubic = 0.044715


def contract(a, b, dim_a, dim_b, precision=HIGH):
    return lax.dot_general(
        a,
        b,
        (((dim_a,), (dim_b,)), ((), ())),
        precision=precision,
        preferred_element_type=jnp.float32,
    )


def nn(a, b, precision=HIGH):
    return contract(a, b, 1, 0, precision)


def nt(a, b, precision=HIGH):
    return contract(a, b, 1, 1, precision)


def tn(a, b, precision=HIGH):
    return contract(a, b, 0, 0, precision)


def spectrum_tables(group_len):
    rows = SEQS * group_len
    period = 2 * group_len
    time = np.arange(group_len)
    lags = np.arange(period)
    bins = np.arange(group_len)
    angle = 2.0 * np.pi * (np.outer(time, bins) % period) / period
    real = np.cos(angle)
    imag = -np.sin(angle)
    imag[:, 0] = (-1.0) ** time
    forward = np.zeros((rows, 2 * rows))
    for s in range(SEQS):
        part = slice(s * group_len, (s + 1) * group_len)
        forward[part, part] = real
        forward[part, rows + s * group_len : rows + (s + 1) * group_len] = imag
    of_taps = np.concatenate([real] * SEQS + [imag] * SEQS, axis=1)
    angle = 2.0 * np.pi * (np.outer(bins, lags) % period) / period
    back_real = 2.0 * np.cos(angle) / period
    back_real[0] = 1.0 / period
    back_imag = -2.0 * np.sin(angle) / period
    back_imag[0] = (-1.0) ** lags / period
    inverse = np.zeros((2 * rows, rows))
    for s in range(SEQS):
        part = slice(s * group_len, (s + 1) * group_len)
        inverse[part, part] = back_real[:, :group_len]
        inverse[rows + s * group_len : rows + (s + 1) * group_len, part] = back_imag[:, :group_len]
    window = np.concatenate([back_real] * SEQS + [back_imag] * SEQS, axis=0)
    return tuple(
        v.astype(np.float32)
        for v in (forward, of_taps, inverse, window[:, :group_len], window[:, group_len:])
    )


def feature_table(length):
    fraction = np.arange(length).astype(np.float32) / np.float32(length)
    angle = np.float32(2.0 * math.pi) * fraction
    wide = angle.astype(np.float64)
    twice = (np.float32(2.0) * angle).astype(np.float64)
    columns = [fraction, np.cos(wide), np.sin(wide), np.cos(twice), np.sin(twice)]
    table = np.zeros((length, 8), np.float32)
    for i, column in enumerate(columns):
        table[:, i] = column.astype(np.float32)
    return table


KINDS = ("sq", "inl", "ul", "dr", "dl")


def late_columns(C):
    return [0, 4 * C, 7 * C, 7 * C + C // 3], 7 * C + C // 3 + 128


def hidden_part(M):
    return -(-136 // (8 * M)) * 8


def muon_scale(name, shape):
    rows, cols = shape[-2:]
    if name == "dl":
        rows, cols = cols, rows
    return muon_rate * math.sqrt(max(rows, cols) / rows)


def when(condition, body):
    if isinstance(condition, bool):
        if condition:
            body()
    else:
        pl.when(condition)(body)


SERVED = (
    "M", "L", "", "LM", "", "L", "", "M", "L", "", "M", "L", "", "M", "LM",
)
SERVED_MIDDLE = ("", "L", "", "L", "L")
EARLY = ("block_in", "vec", "out_grad", "fo", "fh", "feat", "tfwd", "ttap", "tinv", "tw1", "tw2")
SMALL = 256


class Ring:
    def __init__(self, grad, total, far_slot, near_slot, ssem, rsem, rows, columns, way, place, count, ids):
        self.grad, self.total = grad, total
        self.far_slot, self.near_slot = far_slot, near_slot
        self.ssem, self.rsem = ssem, rsem
        self.stride, self.offset, self.height = rows
        self.columns = columns
        self.sign = 1 if way == 0 else -1
        self.place, self.count = place, count
        self.ahead, self.behind = ids if way == 0 else ids[::-1]
        self.gathers = far_slot is None

    def part(self, ref, ahead):
        chunk = lax.rem(self.place + self.sign * ahead + 4 * self.count, self.count)
        start = pl.multiple_of(chunk * self.stride + self.offset, 8)
        return ref.at[pl.ds(start, self.height), self.columns]

    def copy(self, source, target, index, to):
        return pltpu.make_async_remote_copy(
            src_ref=source,
            dst_ref=target,
            send_sem=self.ssem.at[int(index >= self.count - 1)],
            recv_sem=self.rsem.at[index],
            device_id=to,
            device_id_type=MESH,
        )

    def far_sum(self, i):
        n = self.count // 2
        return self.copy(self.part(self.grad, n - i), self.far_slot.at[i], i, self.ahead)

    def near_sum(self, i):
        n = self.count // 2
        source = self.part(self.grad, i - (n - 1))
        return self.copy(source, self.near_slot.at[i], n + i, self.behind)

    def far_total(self, i, hops=0):
        n = self.count // 2
        whole = self.part(self.total, i + hops)
        return self.copy(whole, whole, 2 * n - 1 + i, self.behind)

    def near_total(self, i, hops=0):
        n = self.count // 2
        whole = self.part(self.total, -i - hops)
        return self.copy(whole, whole, 3 * n - 1 + i, self.ahead)

    def begin(self):
        self.far_sum(0).start()
        self.near_sum(0).start()

    def begin_totals(self):
        self.far_total(0).start()
        self.near_total(0).start()

    def event(self, s):
        n = self.count // 2

        def add_far():
            mine = self.part(self.grad, n - 1 - s)
            mine[...] = mine[...] + self.far_slot[s]
            self.far_sum(s + 1).start()

        def add_near():
            mine = self.part(self.grad, s - (n - 2))
            mine[...] = mine[...] + self.near_slot[s]
            self.near_sum(s + 1).start()

        def turn():
            own = self.part(self.total, 0)
            mine = self.part(self.grad, 0)
            own[...] = mine[...] + self.far_slot[n - 1] + self.near_slot[n - 2]
            self.begin_totals()

        both = lambda p, q: p and q if isinstance(p, bool) else p & q
        i = s - n
        when(s < n, lambda: self.far_sum(s).wait_recv())
        when(s < n - 1, add_far)
        when(s < n - 1, lambda: self.near_sum(s).wait_recv())
        when(s < n - 2, add_near)
        when(s == n - 1, turn)
        when(both(s >= n, s < 2 * n), lambda: self.far_total(i, 1).wait_recv())
        when(both(s >= n, s < 2 * n - 1), lambda: self.far_total(i + 1).start())
        when(both(s >= n, s < 2 * n - 1), lambda: self.near_total(i, 1).wait_recv())
        when(both(s >= n, s < 2 * n - 2), lambda: self.near_total(i + 1).start())

    def end(self):
        part = self.total.at[pl.ds(0, self.height * (self.count - 1)), self.columns]
        for index in (self.count - 1,) if self.gathers else (0, self.count - 1):
            self.copy(part, part, index, self.ahead).wait_send()


def unit_scale(values):
    return 1.0 / (jnp.sqrt(jnp.sum(values * values)) + 1e-07)


def halves(values):
    high = values.astype(jnp.bfloat16)
    return high, (values - high.astype(jnp.float32)).astype(jnp.bfloat16)


def thrice(left, right, product):
    a, b = left
    c, d = right
    plain = lambda m, n: product(m, n, None)
    return plain(a, c) + plain(a, d) + plain(b, c)


def idle(product):
    pass


def large_schulz(k, between):
    size = k.x.shape[0]
    tile = 256
    strips = [
        (slice(i * tile, (i + 1) * tile), slice(0, (i + 1) * tile)) for i in range(size // tile)
    ]

    def keep(high, low, rows, columns, values):
        high[rows, columns], low[rows, columns] = halves(values)
        if rows.start:
            turned = values[:, 0 : rows.start].T
            high[0 : rows.start, rows], low[0 : rows.start, rows] = halves(turned)

    def newton_step(step):
        k.xh[...], k.xl[...] = halves(k.x[...])
        for i, (rows, columns) in enumerate(strips):
            gram = thrice((k.xh[rows], k.xl[rows]), (k.xh[columns], k.xl[columns]), nt)
            k.a[rows, columns] = gram
            keep(k.ah, k.al, rows, columns, gram)
        between(3 * step)
        for i, (rows, columns) in enumerate(strips):
            squared = thrice(
                (k.ah[rows], k.al[rows]), (k.ah[:, columns], k.al[:, columns]), nn
            )
            values = schulz_second * k.a[rows, columns] + schulz_third * squared
            keep(k.ph, k.pl, rows, columns, values)
        between(3 * step + 1)
        for i in range(2):
            rows = slice(i * size // 2, (i + 1) * size // 2)
            k.x[rows] = schulz_first * k.x[rows] + thrice(
                (k.ph[rows], k.pl[rows]), (k.xh[...], k.xl[...]), nn
            )
        between(3 * step + 2)

    if between is idle:
        pl.loop(0, 5)(newton_step)
    else:
        for step in range(5):
            newton_step(step)


def small_schulz(moments, results, between):
    current = [moment[...] * unit_scale(moment[...]) for moment in moments]
    for step in range(5):
        split = [halves(values) for values in current]
        grams = [thrice(one, one, nt) for one in split]
        split_grams = [halves(gram) for gram in grams]
        squared = [thrice(one, one, nn) for one in split_grams]
        factors = [
            halves(schulz_second * gram + schulz_third * square)
            for gram, square in zip(grams, squared)
        ]
        current = [
            schulz_first * values + thrice(factor, one, nn)
            for values, factor, one in zip(current, factors, split)
        ]
        between()
    for result, values in zip(results, current):
        result[...] = values


def chain_kernel(dims, names, *refs):
    k = types.SimpleNamespace(**dict(zip(names, refs, strict=True)))
    C, M, Q, GL, CP, cpd, F, LEN, ringed = dims
    R = SEQS * GL
    PW = C // M
    FW = F // M
    D = C * M
    HP = hidden_part(M)
    starts, width = late_columns(C)
    r = lax.axis_index("seq")
    e = lax.axis_index("mp")
    nxt = lax.rem(r + 1, Q)
    prv = lax.rem(r + Q - 1, Q)
    sends = []

    def remote(src, dst, ssem, rsem, seq, mp):
        return pltpu.make_async_remote_copy(
            src_ref=src,
            dst_ref=dst,
            send_sem=ssem,
            recv_sem=rsem,
            device_id={"seq": seq, "mp": mp},
            device_id_type=MESH,
        )

    def swap_blocks(src, dst, phase, same=None):
        for d in range(1, M):
            to = lax.rem(e + d, M)
            source = src.at[to] if same is None else same
            remote(source, dst.at[e], k.mp_sent.at[phase], k.mp_here.at[phase], r, to).start()
        sends.append((dst.at[pl.ds(0, M - 1)], k.mp_sent.at[phase]))
        mine = src[pl.ds(e, 1)] if same is None else same[...].reshape((1,) + same.shape)
        dst[pl.ds(e, 1)] = mine

    def arrive(dst, rsem):
        remote(dst, dst, k.mp_sent.at[0], rsem, nxt, e).wait_recv()

    def blocks_arrive(dst, phase):
        arrive(dst.at[pl.ds(0, M - 1)], k.mp_here.at[phase])

    def swap_seq(src, dst, phase):
        for d in range(1, Q):
            to = lax.rem(r + d, Q)
            remote(
                src.at[to], dst.at[r], k.seq_sent.at[phase], k.seq_here.at[phase], to, e
            ).start()
        sends.append((dst.at[pl.ds(0, Q - 1)], k.seq_sent.at[phase]))
        dst[pl.ds(r, 1)] = src[pl.ds(r, 1)]

    def seq_arrive(dst, phase):
        arrive(dst.at[pl.ds(0, Q - 1)], k.seq_here.at[phase])

    def pieces(dst, values, width):
        for b in range(M):
            dst[b, 0:width] = values[width * b : width * (b + 1)]

    def joined(src, width):
        return jnp.concatenate([src[b, 0:width] for b in range(M)], axis=0)

    def extra(src):
        total = src[0, PW : PW + 8]
        for b in range(1, M):
            total = total + src[b, PW : PW + 8]
        return total[0:1]

    def by_channel(dst, values):
        if CP == cpd:
            dst[...] = values.reshape(Q, CP, values.shape[1])
        else:
            dst[...] = jnp.zeros(dst.shape, jnp.float32)
            for q in range(Q):
                dst[q, 0:cpd] = values[q * cpd : (q + 1) * cpd]

    def from_channels(src):
        if CP == cpd:
            return src[...].reshape(Q * CP, src.shape[2])
        return jnp.concatenate([src[q, 0:cpd] for q in range(Q)], axis=0)

    early = {}
    for i, name in enumerate(EARLY):
        early[name] = pltpu.make_async_copy(
            getattr(k, name + "_hbm"), getattr(k, name), k.esem.at[i]
        )
        early[name].start()
    copies = [
        pltpu.make_async_copy(src, dst, k.wsem.at[i])
        for i, (src, dst) in enumerate(
            (
                (k.sq_hbm, k.sq),
                (k.dl_hbm, k.dl),
                (k.inl_hbm, k.inl),
                (k.ul_hbm, k.ul),
                (k.dr_hbm, k.dr),
            )
        )
    ]
    if ringed:
        copies += [
            pltpu.make_async_copy(getattr(k, f"p{name}_hbm"), dst, k.psem.at[i])
            for i, (name, dst) in enumerate(
                (("dr", k.x), ("ul", k.pul), ("dl", k.pdl), ("sq", k.psq), ("inl", k.pinl))
            )
        ]
    for copy in copies:
        copy.start()

    odd = lax.rem(r, 2)
    place = (1 - odd) * (r // 2) + odd * (Q - 1 - r // 2)

    def at_place(p):
        back = p // (Q // 2)
        return (1 - back) * 2 * p + back * (2 * (Q - 1 - p) + 1)

    ring_ids = tuple(
        {"seq": at_place(lax.rem(place + d, Q)), "mp": e} for d in (1, Q - 1)
    )

    barrier = pltpu.get_barrier_semaphore()
    partners = [(lax.rem(r + d, Q), e) for d in range(1, Q)]
    partners += [(r, lax.rem(e + d, M)) for d in range(1, M)]
    partners += [(s, lax.rem(e + d, M)) for s in (nxt, prv) for d in range(1, M)]
    for seq, mp in partners:
        pl.semaphore_signal(
            barrier, inc=1, device_id={"seq": seq, "mp": mp}, device_id_type=MESH
        )

    gather_rings, first_rings, other_rings, late_rings = [], [], [], []
    if ringed:

        def ring(grad, total, slots, rows, columns, way, index):
            return Ring(
                grad,
                total,
                *slots,
                k.ring_ssem.at[index],
                k.ring_rsem.at[index],
                rows,
                columns,
                way,
                place,
                Q,
                ring_ids,
            )

        tall, low = F // Q, C // Q
        for way in range(2):
            rows = (tall, way * (tall // 2), tall // 2)
            first_rings.append(ring(None, k.tdr, (None, None), rows, slice(0, F), way, way))
            rows = (F, way * (F // 2), F // 2)
            gather_rings.append(ring(None, k.dm4_all, (None, None), rows, slice(0, R), way, 6 + way))
        for rings, grad, total, slots, index in (
            (
                other_rings,
                k.gmid,
                k.tmid,
                ((k.far_mid0, k.near_mid0), (k.far_mid1, k.near_mid1)),
                2,
            ),
            (
                late_rings,
                k.glate,
                k.tlate,
                ((k.far_late0, k.near_late0), (k.far_late1, k.near_late1)),
                4,
            ),
        ):
            span = grad.shape[1]
            cut = span // 256 * 128
            for way, columns in enumerate((slice(0, cut), slice(cut, span))):
                rows = (low, 0, low)
                rings.append(ring(grad, total, slots[way], rows, columns, way, index + way))

    def go(rings, s):
        for one in rings:
            one.event(s)

    outs = []

    def put(source, target):
        copy = pltpu.make_async_copy(source, target, k.osem.at[len(outs)])
        copy.start()
        outs.append(copy)

    halves_done = [Q]

    def first_halves(count):
        if ringed:
            for _ in range(count):
                i = halves_done[0]
                first_rings[i % 2].event(i // 2)
                halves_done[0] += 1

    lane = lax.broadcasted_iota(jnp.int32, (1, R), 1)
    spot = lax.rem(lane, GL)
    first_bin = spot == 0
    flip = jnp.where(lax.rem(spot, 2) == 0, 1.0, -1.0).astype(jnp.float32)
    keep_bin = jnp.where(first_bin, 0.0, 1.0).astype(jnp.float32)
    length_of = jnp.where(lane < GL, k.lengths[0], k.lengths[1])
    position = r * GL + spot
    valid = (position < length_of).astype(jnp.float32)
    has_prev = (r > 0).astype(jnp.float32)
    has_next = (r < Q - 1).astype(jnp.float32)
    tail = spot >= GL - 2
    head = spot < 2
    halo_mask = jnp.where(tail, has_prev, jnp.where(head, has_next, 0.0))
    end_row = lax.broadcasted_iota(jnp.int32, (8, R), 0)
    end_lane = lax.rem(end_row, 4) // 2 * GL + lax.rem(end_row, 2)
    end_lane = end_lane + jnp.where(end_row < 4, 0, GL - 2)
    ends = (lax.broadcasted_iota(jnp.int32, (8, R), 1) == end_lane).astype(jnp.float32)

    early["block_in"].wait()
    early["vec"].wait()
    k.xt[...] = k.block_in[...].T
    k.vecp[...] = jnp.zeros(k.vecp.shape, jnp.float32)
    k.vecp[0 : 4 + 3 * KS] = k.vec[...]
    k.vt[...] = k.vecp[...].T

    def column(i):
        return k.vt[:, i : i + 1]

    xt = k.xt[...]
    u0 = xt * column(0)
    k.u0[...] = u0
    copies[0].wait()
    pieces(k.s0, tn(k.sq[0], u0), PW)
    squares = jnp.broadcast_to(jnp.sum(xt * xt, axis=0, keepdims=True), (8, R))
    for b in range(M):
        k.s0[b, PW : PW + 8] = squares
    pl.semaphore_wait(barrier, len(partners))
    swap_blocks(k.s0, k.r0, 0)
    for b in range(M):
        k.hs0[b, :, 0 : PW + 8] = nt(ends, k.s0[b], HIGHEST)
    halo_after, halo_before = [], []
    for d in range(M):
        to = lax.rem(e + d, M)
        for copies_to, dst, i, seq in ((halo_after, k.hp0, 0, nxt), (halo_before, k.hn0, 1, prv)):
            copies_to.append(
                remote(k.hs0.at[to], dst.at[e], k.halo_sent.at[i], k.halo_here.at[i], seq, to)
            )

    @pl.when(r < Q - 1)
    def _():
        for copy in halo_after:
            copy.start()

    @pl.when(r > 0)
    def _():
        for copy in halo_before:
            copy.start()

    @pl.when(r == 0)
    def _():
        k.hp0[...] = jnp.zeros(k.hp0.shape, jnp.float32)

    @pl.when(r == Q - 1)
    def _():
        k.hn0[...] = jnp.zeros(k.hn0.shape, jnp.float32)

    early["out_grad"].wait()
    k.ogt[...] = k.out_grad[...].T
    copies[1].wait()
    pieces(k.s4, tn(k.dl[...], k.ogt[...]), FW)
    swap_blocks(k.s4, k.r4, 4)
    by_channel(k.vtc, k.vt[...])
    early["fo"].wait()
    by_channel(k.foc, k.fo[...])
    copies[2].wait()

    blocks_arrive(k.r0, 0)

    @pl.when(r > 0)
    def _():
        arrive(k.hp0, k.halo_here.at[0])

    @pl.when(r < Q - 1)
    def _():
        arrive(k.hn0, k.halo_here.at[1])

    scale_one = lax.rsqrt(extra(k.r0) / D + norm_epsilon)
    w0 = joined(k.r0, PW)
    k.w0[...] = w0
    first_half = lax.broadcasted_iota(jnp.int32, (8, 128), 0) < 4
    spread = [
        tn(jnp.where(first_half, k.hn0[b], k.hp0[b]), ends, HIGHEST) for b in range(M)
    ]
    w0h = jnp.concatenate([one[0:PW] for one in spread], axis=0)
    squares = spread[0][PW : PW + 1]
    for b in range(1, M):
        squares = squares + spread[b][PW : PW + 1]
    both = tn(k.inl[...], jnp.concatenate([w0, w0h], axis=1))
    z = both[:, 0:R] * scale_one
    zh = both[:, R : 2 * R] * (lax.rsqrt(squares / D + norm_epsilon) * halo_mask)
    zh_far = pltpu.roll(zh, GL, 1)
    k.z[...] = z
    k.z1[...] = pltpu.roll(jnp.where(spot >= GL - 1, zh_far, z), 1, 1)
    k.z2[...] = pltpu.roll(jnp.where(tail, zh_far, z), 2, 1)
    for s in range(3):
        part = slice(s * C, (s + 1) * C)
        k.conv[part] = (
            column(4 + KS * s) * k.z[part]
            + column(5 + KS * s) * k.z1[part]
            + column(6 + KS * s) * k.z2[part]
        )
    product = k.conv[0:C] * k.conv[2 * C : 3 * C] * valid
    k.prod[...] = product
    by_channel(k.ps, product)
    swap_seq(k.ps, k.ur, 0)

    for name in EARLY[4:]:
        early[name].wait()
    pre = filter_frequency * nn(k.feat[...], k.fh[0:8], HIGHEST)
    k.l1[...] = jnp.sin(pre)
    k.c1[...] = filter_frequency * jnp.cos(pre)
    if ringed:
        blocks_arrive(k.r4, 4)
        k.dm4_all[pl.ds(pl.multiple_of(place * F, F), F)] = k.r4[...].reshape(F, R)
        gather_rings[0].begin_totals()
    pre = filter_frequency * nn(k.l1[...], k.fh[EMB : EMB + 128], HIGHEST)
    k.l2[...] = jnp.sin(pre)
    k.c2[...] = filter_frequency * jnp.cos(pre)
    foc = k.foc[pl.ds(r, 1)].reshape(CP, 128)
    vtc = k.vtc[pl.ds(r, 1)].reshape(CP, 128)
    rate = vtc[:, 2:3]
    skip_channel = vtc[:, 3:4]
    shaped = nt(foc, k.l2[...], HIGHEST)
    part_lane = lax.broadcasted_iota(jnp.int32, (1, GL), 1)
    for q in range(Q):
        fraction = (part_lane + q * GL).astype(jnp.float32) / LEN
        decay = jnp.exp(-fraction * rate) * (LEN ** (-0.5))
        k.decay[q] = decay
        k.taps[q] = shaped[:, q * GL : (q + 1) * GL] * decay
    spectrum = nn(k.taps[...].reshape(Q * CP, GL), k.ttap[...]).reshape(Q, CP, 2 * R)
    for q in range(Q):
        real = spectrum[q, :, 0:R]
        imag = spectrum[q, :, R : 2 * R]
        if q > 0:
            real = real + flip * spectrum[q - 1, :, 0:R]
            imag = imag + flip * spectrum[q - 1, :, R : 2 * R]
        k.kr[q] = real
        k.km[q] = imag * keep_bin
        k.k4[q] = jnp.where(first_bin, imag, real)

    def total_pairs(count, first, term):
        zero = jnp.zeros((CP, R), jnp.float32)
        if Q <= 8:
            real, imag = zero, zero
            for i in range(count):
                add_real, add_imag = term(first + i)
                real, imag = real + add_real, imag + add_imag
            return real, imag

        def body(i, kept):
            add_real, add_imag = term(first + i)
            return (kept[0] + add_real, kept[1] + add_imag)

        return lax.fori_loop(0, count, body, (zero, zero))

    def each_block(body):
        if Q <= 8:
            for q in range(Q):
                body(q)
        else:
            pl.loop(0, Q)(body)

    seq_arrive(k.ur, 0)
    k.us[...] = nn(k.ur[...].reshape(Q * CP, R), k.tfwd[...]).reshape(Q, CP, 2 * R)

    def forward_block(p):
        def term(q):
            real = k.us[q, :, 0:R]
            imag = k.us[q, :, R : 2 * R]
            lag = p - q
            return (
                k.kr[lag] * real - k.km[lag] * imag,
                k.km[lag] * real + k.k4[lag] * imag,
            )

        real, imag = total_pairs(p + 1, 0, term)
        k.zs[p, :, 0:R] = real
        k.zs[p, :, R : 2 * R] = imag

    each_block(forward_block)
    k.ys[...] = nn(k.zs[...].reshape(Q * CP, 2 * R), k.tinv[...]).reshape(Q, CP, R)
    swap_seq(k.ys, k.yr, 1)
    if ringed:
        gather_rings[1].begin_totals()
    for q in range(Q):
        real = k.us[q, :, 0:R]
        imag = k.us[q, :, R : 2 * R]
        k.um[q] = imag * keep_bin
        k.u4[q] = jnp.where(first_bin, imag, real)

    copies[3].wait()
    k.ult_h[...], k.ult_l[...] = halves(k.ul[...].T)
    if ringed:
        copies[4].wait()
        k.ph[...], k.pl[...] = halves(k.dr[...].T)
    seq_arrive(k.yr, 1)
    inner_sum = from_channels(k.yr) + column(3) * k.prod[...]
    k.insum[...] = inner_sum
    gated = k.conv[C : 2 * C] * inner_sum
    k.gated[...] = gated
    pieces(k.s1, tn(k.sq[1], gated), PW)
    swap_blocks(k.s1, k.r1, 1)

    if ringed:
        gather_rings[0].event(Q // 2 + 0)
    if not ringed:
        copies[4].wait()
    if not ringed:
        blocks_arrive(k.r4, 4)
    k.dact[...] = nn(k.dr[...], k.r4[...].reshape(F, R))

    if ringed:
        gather_rings[1].event(Q // 2 + 0)
    blocks_arrive(k.r1, 1)
    w1 = k.r1[...].reshape(C, R)
    k.w1[...] = w1
    h = k.xt[...] + tn(k.sq[2], w1)
    k.h[...] = h
    u3 = h * column(1)
    pieces(k.s2, tn(k.sq[3], u3), PW)
    squares = jnp.broadcast_to(jnp.sum(h * h, axis=0, keepdims=True), (8, R))
    for b in range(M):
        k.s2[b, PW : PW + 8] = squares
    swap_blocks(k.s2, k.r2, 2)

    if ringed:
        gather_rings[0].event(Q // 2 + 1)
    blocks_arrive(k.r2, 2)
    scale_two = lax.rsqrt(extra(k.r2) / D + norm_epsilon)
    k.n2[...] = k.h[...] * scale_two
    w3 = joined(k.r2, PW)
    k.w3[...] = w3
    k.gu[...] = thrice((k.ult_h[...], k.ult_l[...]), halves(w3), nn) * scale_two
    gate = k.gu[0:F]
    up = k.gu[F : 2 * F]
    bend = jnp.tanh(gelu_scale * (gate + gelu_cubic * gate * gate * gate))
    gelu = 0.5 * gate * (1.0 + bend)
    slope = 0.5 * (1.0 + bend) + 0.5 * gate * (1.0 - bend * bend) * gelu_scale * (
        1.0 + 3.0 * gelu_cubic * gate * gate
    )
    dact = k.dact[...]
    k.act[...] = gelu * up
    k.dgu[0:F] = dact * up * slope
    k.dgu[F : 2 * F] = dact * gelu
    back = nn(k.ul[...], k.dgu[...])
    pieces(k.s5, back, PW)
    inner = jnp.broadcast_to(jnp.sum(back * k.w3[...], axis=0, keepdims=True), (8, R))
    for b in range(M):
        k.s5[b, PW : PW + 8] = inner
    swap_blocks(k.s5, k.r5, 5)
    if ringed:
        tall = F // Q

        def act_rows(p):
            return k.act.at[pl.ds(pl.multiple_of(p * tall, tall), tall)]

        for d in range(1, Q):
            p = lax.rem(place + d, Q)
            remote(
                act_rows(p),
                k.act_all.at[place],
                k.act_sent.at[0],
                k.act_here.at[0],
                at_place(p),
                e,
            ).start()
        sends.append((k.act_all.at[pl.ds(0, Q - 1)], k.act_sent.at[0]))
        k.act_all[pl.ds(place, 1)] = act_rows(place)[...].reshape(1, tall, R)
        gather_rings[1].event(Q // 2 + 1)
    else:
        k.gdr[...] = nt(k.act[...], k.r4[...].reshape(F, R))
    if ringed:
        pieces(k.s3, thrice((k.ph[...], k.pl[...]), halves(k.act[...]), nn), FW)
    else:
        pieces(k.s3, tn(k.dr[...], k.act[...]), FW)
    swap_blocks(k.s3, k.r3, 3)

    k.gmid[:, 0 : 2 * F] = nt(k.w3[...] * scale_two, k.dgu[...])
    if ringed:
        gather_rings[0].event(Q // 2 + 2)
    blocks_arrive(k.r5, 5)
    back = joined(k.r5, PW)
    inner = extra(k.r5)
    grad_two = nn(k.sq[3], back)
    hidden_grad = (
        k.ogt[...]
        + scale_two * (grad_two * column(1))
        - k.h[...] * (scale_two * scale_two * scale_two * inner / D)
    )
    k.hg[...] = hidden_grad
    pieces(k.s6, nn(k.sq[2], hidden_grad), PW)
    swap_blocks(k.s6, k.r6, 6)
    k.glate[:, 3 * C : 4 * C] = nt(k.n2[...] * column(1), back)
    gain_two = jnp.sum(grad_two * k.n2[...], axis=1, keepdims=True)
    k.glate[:, 2 * C : 3 * C] = nt(k.w1[...], k.hg[...])

    blocks_arrive(k.r6, 6)
    back = k.r6[...].reshape(C, R)
    gated_grad = nn(k.sq[1], back)
    inner_grad = gated_grad * k.conv[C : 2 * C]
    k.inner[...] = inner_grad
    k.d1[...] = gated_grad * k.insum[...]
    by_channel(k.inner_s, inner_grad)
    swap_seq(k.inner_s, k.vr, 2)
    k.glate[:, C : 2 * C] = nt(k.gated[...], back)
    skip_total = jnp.sum(inner_grad * k.prod[...], axis=1, keepdims=True)

    if ringed:
        gather_rings[1].event(Q // 2 + 2)
        for one in gather_rings:
            one.event(Q // 2 + 3)
    seq_arrive(k.vr, 2)
    k.vs[...] = nn(k.vr[...].reshape(Q * CP, R), k.tfwd[...]).reshape(Q, CP, 2 * R)

    def back_block(q):
        def term(p):
            real = k.vs[p, :, 0:R]
            imag = k.vs[p, :, R : 2 * R]
            lag = p - q
            return (
                k.kr[lag] * real + k.km[lag] * imag,
                k.k4[lag] * imag - k.km[lag] * real,
            )

        real, imag = total_pairs(Q - q, q, term)
        k.zs[q, :, 0:R] = real
        k.zs[q, :, R : 2 * R] = imag

    each_block(back_block)
    k.ds[...] = (
        nn(k.zs[...].reshape(Q * CP, 2 * R), k.tinv[...]).reshape(Q, CP, R)
        + skip_channel[None] * k.vr[...]
    )
    swap_seq(k.ds, k.dmain, 3)
    if ringed:
        arrive(k.act_all.at[pl.ds(0, Q - 1)], k.act_here.at[0])
        acts = jnp.concatenate([k.act_all[p] for p in range(Q)], axis=1)
        backs = jnp.concatenate([k.dm4_all[p * F : (p + 1) * F] for p in range(Q)], axis=1)
        k.tdr[pl.ds(pl.multiple_of(place * tall, tall), tall)] = nt(acts, backs)
        for one in first_rings:
            one.begin_totals()
    first_halves(1)
    def lag_block(j):
        def term(p):
            real = k.vs[p, :, 0:R]
            imag = k.vs[p, :, R : 2 * R]
            q = p - j
            return (
                k.us[q, :, 0:R] * real + k.um[q] * imag,
                k.u4[q] * imag - k.um[q] * real,
            )

        real, imag = total_pairs(Q - j, j, term)
        k.zs[j, :, 0:R] = real
        k.zs[j, :, R : 2 * R] = imag

    each_block(lag_block)
    cross = k.zs[...].reshape(Q * CP, 2 * R)
    near = nn(cross, k.tw1[...]).reshape(Q, CP, GL)
    far = nn(cross, k.tw2[...]).reshape(Q, CP, GL)
    decay_total = jnp.zeros((CP, 1), jnp.float32)
    for q in range(Q):
        grad = near[q]
        if q < Q - 1:
            grad = grad + far[q + 1]
        fraction = (part_lane + q * GL).astype(jnp.float32) / LEN
        decay_total = decay_total - jnp.sum(
            grad * k.taps[q] * fraction, axis=1, keepdims=True
        )
        k.draw[:, q * GL : (q + 1) * GL] = grad * k.decay[q]
    raw = k.draw[...]
    k.gfo[...] = jnp.zeros(k.gfo.shape, jnp.float32)
    k.gdec[...] = jnp.zeros(k.gdec.shape, jnp.float32)
    k.gfo[pl.ds(r, 1)] = nn(raw, k.l2[...]).reshape(1, CP, 128)
    k.gdec[pl.ds(r, 1)] = jnp.broadcast_to(decay_total, (CP, 128)).reshape(1, CP, 128)
    first_halves(1)
    blocks_arrive(k.r3, 3)
    w4 = k.r3[...].reshape(F, R)
    k.block_out[...] = (k.h[...] + nn(k.dl[...], w4)).T
    put(k.block_out, k.block_out_hbm)
    k.gmid[:, 2 * F : 3 * F] = nt(k.ogt[...], w4)
    for one in other_rings:
        one.begin()
    back = tn(raw, foc) * k.c2[...]
    k.hid[8:136] = tn(k.l1[...], back)
    back = nt(back, k.fh[EMB : EMB + 128]) * k.c1[...]
    k.hid[0:8] = tn(k.feat[...], back)
    k.hid[136:] = jnp.zeros((M * HP - 136, 128), jnp.float32)

    def hid_rows(b):
        return k.hid.at[pl.ds(pl.multiple_of(b * HP, HP), HP)]

    if ringed:
        for d in range(1, M):
            to = lax.rem(e + d, M)
            remote(hid_rows(to), k.hids.at[e], k.mp_sent.at[8], k.mp_here.at[8], r, to).start()
        sends.append((k.hids.at[pl.ds(0, M - 1)], k.mp_sent.at[8]))
        k.hids[pl.ds(e, 1)] = hid_rows(e)[...].reshape(1, HP, 128)


    first_halves(1)
    seq_arrive(k.dmain, 3)
    product_grad = from_channels(k.dmain) * valid
    k.d3[0:C] = product_grad * k.conv[2 * C : 3 * C]
    k.d3[C : 2 * C] = k.d1[...]
    k.d3[2 * C : 3 * C] = product_grad * k.conv[0:C]
    k.hs1[...] = nt(ends, k.d3[...], HIGHEST)
    edge = remote(k.hs1, k.hr1, k.halo_sent.at[2], k.halo_here.at[2], prv, e)

    @pl.when(r > 0)
    def _():
        edge.start()

    @pl.when(r == Q - 1)
    def _():
        k.hr1[...] = jnp.zeros(k.hr1.shape, jnp.float32)

    first_halves(1)

    @pl.when(r < Q - 1)
    def _():
        arrive(k.hr1, k.halo_here.at[2])

    following = pltpu.roll(tn(k.hr1[...], ends, HIGHEST), GL, 1)
    tap_totals = []
    for s in range(3):
        part = slice(s * C, (s + 1) * C)
        grad = k.d3[part]
        one = pltpu.roll(jnp.where(spot == 0, following[part], grad), R - 1, 1)
        two = pltpu.roll(jnp.where(head, following[part], grad), R - 2, 1)
        k.dz[part] = (
            column(4 + KS * s) * grad + column(5 + KS * s) * one + column(6 + KS * s) * two
        )
        for shifted in (k.z, k.z1, k.z2):
            tap_totals.append(jnp.sum(grad * shifted[part], axis=1, keepdims=True))
    back = nn(k.inl[...], k.dz[...])
    pieces(k.s7, back, PW)
    inner = jnp.broadcast_to(jnp.sum(back * k.w0[...], axis=0, keepdims=True), (8, R))
    for b in range(M):
        k.s7[b, PW : PW + 8] = inner
    swap_blocks(k.s7, k.r7, 7)
    k.glate[:, 4 * C : 7 * C] = nt(k.w0[...] * scale_one, k.dz[...])

    first_halves(1)
    if ringed:
        go(other_rings, 0)
    blocks_arrive(k.r7, 7)
    back = joined(k.r7, PW)
    inner = extra(k.r7)
    grad_one = nn(k.sq[0], back)
    xt = k.xt[...]
    k.input_grad[...] = (
        k.hg[...]
        + scale_one * (grad_one * column(0))
        - xt * (scale_one * scale_one * scale_one * inner / D)
    ).T
    put(k.input_grad, k.input_grad_hbm)
    k.glate[:, 0:C] = nt(k.u0[...] * scale_one, back)
    gain_one = jnp.sum(grad_one * xt * scale_one, axis=1, keepdims=True)
    slot = lax.broadcasted_iota(jnp.int32, (1, 16), 1)
    rows = {0: gain_one, 1: gain_two, 2: from_channels(k.gdec)[:, 0:1], 3: skip_total}
    rows.update({4 + i: total for i, total in enumerate(tap_totals)})
    stacked = jnp.zeros((C, 16), jnp.float32)
    for i, total in rows.items():
        stacked = jnp.where(slot == i, total, stacked)
    k.glate[:, starts[2] : starts[3]] = jnp.zeros((C, starts[3] - starts[2]), jnp.float32)
    k.glate[:, starts[2] : starts[2] + 16] = stacked
    k.glate[:, starts[3] : width] = from_channels(k.gfo)
    first_halves(1)
    if ringed:
        blocks_arrive(k.hids, 8)
        hidden_sum = k.hids[0]
        for b in range(1, M):
            hidden_sum = hidden_sum + k.hids[b]
        k.glate[0:128, starts[2] + 16 : starts[2] + 16 + HP] = hidden_sum.T

    if ringed:
        first_halves(max(0, 2 * Q - 2 - halves_done[0]))
        for one in late_rings:
            one.begin()
        go(other_rings, 1)
        first_halves(2 * Q - halves_done[0])
        for copy in copies[5:]:
            copy.wait()
        moment = momentum_decay * k.x[...] + k.tdr[...]
        k.moment[...] = moment
        put(k.moment, k.out_pdr)
        k.x[...] = moment * unit_scale(moment)
        mid_turns, late_turns = iter(range(2, Q)), iter(range(Q))

        def turn(rings, turns):
            s = next(turns, None)
            if s is not None:
                go(rings, s)

        def serve(letters):
            for letter in letters:
                if letter == "M":
                    turn(other_rings, mid_turns)
                else:
                    turn(late_rings, late_turns)

        def between(product):
            serve(SERVED[product])

        def renew(name, weight, result, target):
            result[...] = weight[...] - muon_scale(name, weight.shape) * result[...]
            put(result, target)

        large_schulz(k, between)
        renew("dr", k.dr, k.x, k.out_odr)
        for s in mid_turns:
            go(other_rings, s)
        steps = iter(SERVED_MIDDLE)
        for moment, columns in ((k.pul, slice(0, 2 * F)), (k.pdl, slice(2 * F, 3 * F))):
            moment[...] = momentum_decay * moment[...] + k.tmid[:, columns]
        put(k.pul, k.out_pul)
        put(k.pdl, k.out_pdl)
        small_schulz((k.pul, k.pdl), (k.oul, k.odl), lambda: serve(next(steps)))
        renew("ul", k.ul, k.oul, k.out_oul)
        renew("dl", k.dl, k.odl, k.out_odl)
        for s in late_turns:
            go(late_rings, s)
        put(k.tlate.at[:, width - SMALL :], k.out_small)
        k.hpart[...] = k.tlate[0:128, starts[2] + 16 : starts[2] + 16 + HP].T
        swap_blocks(None, k.hall, 9, k.hpart)
        for i in range(4):
            k.psq[i] = momentum_decay * k.psq[i] + k.tlate[:, i * C : (i + 1) * C]
        k.pinl[...] = momentum_decay * k.pinl[...] + k.tlate[:, starts[1] : starts[2]]
        put(k.psq, k.out_psq)
        put(k.pinl, k.out_pinl)
        small_schulz(
            [k.psq.at[i] for i in range(4)] + [k.pinl],
            [k.osq.at[i] for i in range(4)] + [k.oinl],
            lambda: None,
        )
        renew("sq", k.sq, k.osq, k.out_osq)
        renew("inl", k.inl, k.oinl, k.out_oinl)
        blocks_arrive(k.hall, 9)
        put(k.hall, k.out_hid)
        for one in gather_rings + first_rings + other_rings + late_rings:
            one.end()
    else:
        put(k.gdr, k.out_dr)
        put(k.gmid, k.out_mid)
        put(k.glate, k.out_late)
        put(k.hid, k.out_hid)
    for copy in outs:
        copy.wait()
    for ref, sem in sends:
        remote(ref, ref, sem, k.mp_here.at[0], nxt, e).wait_send()

    @pl.when(r < Q - 1)
    def _():
        remote(k.hs0, k.hp0, k.halo_sent.at[0], k.halo_here.at[0], nxt, e).wait_send()

    @pl.when(r > 0)
    def _():
        remote(k.hs0, k.hn0, k.halo_sent.at[1], k.halo_here.at[1], prv, e).wait_send()
        edge.wait_send()


def run_chain(x, og, lengths, weights, moments, vectors, fh, fo):
    M, Q = lax.axis_size("mp"), lax.axis_size("seq")
    sq, inl, ul, dr, dl = weights
    _, GL, C = x.shape
    R = SEQS * GL
    F = dr.shape[0]
    LEN = GL * Q
    cpd = C // Q
    CP = -(-cpd // 8) * 8
    PW, FW = C // M, F // M
    ringed = cpd % 8 == 0 and F % (32 * Q) == 0
    dims = (C, M, Q, GL, CP, cpd, F, LEN, ringed)
    tables = spectrum_tables(GL)
    feat = feature_table(LEN)
    width = late_columns(C)[1]
    sds = lambda *shape: jax.ShapeDtypeStruct(shape, jnp.float32)
    v = lambda *shape: pltpu.VMEM(shape, jnp.float32)
    dma = lambda *shape: pltpu.SemaphoreType.DMA(shape)
    first = dict(
        block_in=x.reshape(R, C),
        out_grad=og.reshape(R, C),
        vec=vectors,
        fh=fh,
        fo=fo,
        feat=feat,
        **dict(zip(("tfwd", "ttap", "tinv", "tw1", "tw2"), tables)),
    )
    in_hbm = {name + "_hbm": array for name, array in first.items()}
    in_hbm.update(sq_hbm=sq, inl_hbm=inl, ul_hbm=ul, dr_hbm=dr, dl_hbm=dl)
    if ringed:
        in_hbm.update((f"p{name}_hbm", moment) for name, moment in zip(KINDS, moments))
    out_first = dict(block_out=sds(R, C), input_grad=sds(R, C))
    out_hbm = dict(out_dr=sds(F, F), out_mid=sds(C, 3 * F), out_late=sds(C, width))
    out_hbm["out_hid"] = sds(M * hidden_part(M), 128)
    if ringed:
        out_hbm = {f"out_{x}{n}": sds(*w.shape) for x in "po" for n, w in zip(KINDS, weights)}
        out_hbm["out_small"] = sds(C, SMALL)
        out_hbm["out_hid"] = sds(M, hidden_part(M), 128)
    scratch = dict(
        sq=v(4, C, C),
        inl=v(C, 3 * C),
        ul=v(C, 2 * F),
        dr=v(F, F),
        dl=v(C, F),
        vecp=v(128, C),
        vt=v(C, 128),
        vtc=v(Q, CP, 128),
        foc=v(Q, CP, 128),
        gfo=v(Q, CP, 128),
        gdec=v(Q, CP, 128),
        gu=v(2 * F, R),
        act=v(F, R),
        dact=v(F, R),
        dgu=v(2 * F, R),
        block_out=v(R, C),
        input_grad=v(R, C),
        ult_h=pltpu.VMEM((2 * F, C), jnp.bfloat16),
        ult_l=pltpu.VMEM((2 * F, C), jnp.bfloat16),
        hid=v(M * hidden_part(M), 128),
        hs0=v(M, 8, 128),
        hp0=v(M, 8, 128),
        hn0=v(M, 8, 128),
        hs1=v(8, 3 * C),
        hr1=v(8, 3 * C),
        hids=v(M, hidden_part(M), 128),
        hall=v(M, hidden_part(M), 128),
        hpart=v(hidden_part(M), 128),
        taps=v(Q, CP, GL),
        decay=v(Q, CP, GL),
        draw=v(CP, LEN),
        gdr=v(8 if ringed else F, F),
        gmid=v(C, 3 * F),
        glate=v(C, width),
    )
    for name, array in first.items():
        scratch[name] = v(*array.shape)
    scratch["esem"] = dma(len(first))
    for name in ("xt", "ogt", "u0", "prod", "insum", "gated", "w0", "w1", "w3", "h", "n2", "hg", "inner", "d1"):
        scratch[name] = v(C, R)
    for name in ("z", "z1", "z2", "conv", "dz", "d3"):
        scratch[name] = v(3 * C, R)
    for name in ("l1", "c1", "l2", "c2"):
        scratch[name] = v(LEN, 128)
    for name in ("kr", "km", "k4", "um", "u4", "ps", "ur", "ys", "yr", "inner_s", "vr", "ds", "dmain"):
        scratch[name] = v(Q, CP, R)
    for name in ("us", "vs", "zs"):
        scratch[name] = v(Q, CP, 2 * R)
    for name in ("s0", "r0", "s2", "r2", "s5", "r5", "s7", "r7"):
        scratch[name] = v(M, PW + 8, R)
    for name in ("s1", "r1", "s6", "r6"):
        scratch[name] = v(M, PW, R)
    for name in ("s3", "r3", "s4", "r4"):
        scratch[name] = v(M, FW, R)
    scratch.update(
        wsem=dma(5),
        osem=dma(14),
        mp_sent=dma(10),
        mp_here=dma(10),
        seq_sent=dma(4),
        seq_here=dma(4),
        halo_sent=dma(3),
        halo_here=dma(3),
    )
    if ringed:
        scratch.update(
            tdr=v(F, F),
            tmid=v(C, 3 * F),
            tlate=v(C, width),
            dm4_all=v(Q * F, R),
            act_all=v(Q, F // Q, R),
            act_sent=dma(1),
            act_here=dma(1),
            ring_ssem=dma(8, 2),
            ring_rsem=dma(8, 2 * Q - 2),
            x=v(F, F),
            a=v(F, F),
            moment=v(F, F),
            psem=dma(5),
            psq=v(4, C, C),
            osq=v(4, C, C),
            pinl=v(C, 3 * C),
            oinl=v(C, 3 * C),
            pul=v(C, 2 * F),
            oul=v(C, 2 * F),
            pdl=v(C, F),
            odl=v(C, F),
        )
        for name in ("xh", "xl", "ah", "al", "ph", "pl"):
            scratch[name] = pltpu.VMEM((F, F), jnp.bfloat16)
        for name, columns in (("mid", 3 * F), ("late", width)):
            cut = columns // 256 * 128
            for i, part in enumerate((cut, columns - cut)):
                scratch[f"far_{name}{i}"] = v(Q // 2, C // Q, part)
                scratch[f"near_{name}{i}"] = v(Q // 2 - 1, C // Q, part)
    vmem = pl.BlockSpec(memory_space=pltpu.VMEM)
    smem = pl.BlockSpec(memory_space=pltpu.SMEM)
    hbm = pl.BlockSpec(memory_space=pl.ANY)
    names = ["lengths", *in_hbm, *(f"{name}_hbm" for name in out_first), *out_hbm, *scratch]
    outs = pl.pallas_call(
        functools.partial(chain_kernel, dims, names),
        out_shape=[*out_first.values(), *out_hbm.values()],
        in_specs=[smem] + [hbm] * len(in_hbm),
        out_specs=[hbm] * (len(out_first) + len(out_hbm)),
        scratch_shapes=list(scratch.values()),
        compiler_params=pltpu.CompilerParams(
            collective_id=0, has_side_effects=True, vmem_limit_bytes=60 * 2**20
        ),
        name="chain",
    )(lengths, *in_hbm.values())
    block_out, input_grad, *rest = outs
    if ringed:
        return block_out, input_grad, dict(zip(out_hbm, rest))
    totals = dict(zip(out_hbm, rest))
    hidden = lax.psum(totals.pop("out_hid"), ("seq", "mp"))
    return block_out, input_grad, dict(lax.psum(totals, "seq"), out_hid=hidden)


def adam(refs, gradient, rate):
    weights, first, second, first_out, second_out, weights_out, copy_out = refs
    first_new = beta_first * first[...] + (1.0 - beta_first) * gradient
    second_new = beta_second * second[...] + (1.0 - beta_second) * gradient * gradient
    corrected_first = first_new / (1.0 - beta_first**STEP)
    corrected_second = second_new / (1.0 - beta_second**STEP)
    old = weights[...]
    new = old - rate * (
        corrected_first / (jnp.sqrt(corrected_second) + adam_epsilon) + weight_decay * old
    )
    first_out[...] = first_new
    second_out[...] = second_new
    weights_out[...] = new
    copy_out[...] = new.astype(jnp.bfloat16)


def update_kernel(names, loaded, stored, ringed, *refs):
    k = types.SimpleNamespace(**dict(zip(names, refs, strict=True)))
    C, F = k.nsq.shape[1], k.ndr.shape[0]
    starts, width = late_columns(C)
    reads = {
        name: pltpu.make_async_copy(
            getattr(k, "hbm_" + name), getattr(k, name), k.read_sem.at[i]
        )
        for i, name in enumerate(loaded)
    }
    writes = {
        name: pltpu.make_async_copy(
            getattr(k, source), getattr(k, "hbm_" + name), k.write_sem.at[i]
        )
        for i, (name, source) in enumerate(stored.items())
    }
    for copy in reads.values():
        copy.start()

    def need(*wanted):
        for name in wanted:
            reads[name].wait()

    def put(*done):
        for name in done:
            writes[name].start()

    if not ringed:
        need("glate", "gmid", "gdr", "hid", *["p" + name for name in KINDS])
        totals = {
            "inl": k.glate[:, starts[1] : starts[2]],
            "ul": k.gmid[:, 0 : 2 * F],
            "dr": k.gdr[...],
            "dl": k.gmid[:, 2 * F : 3 * F],
        }
        for i in range(4):
            k.msq[i] = momentum_decay * k.psq[i] + k.glate[:, i * C : (i + 1) * C]
        for name, total in totals.items():
            moment = momentum_decay * getattr(k, "p" + name)[...] + total
            getattr(k, "m" + name)[...] = moment
        moment = k.mdr[...]
        k.x[...] = moment * unit_scale(moment)
        small_schulz(
            [k.msq.at[i] for i in range(4)] + [k.minl, k.mul, k.mdl],
            [k.osq.at[i] for i in range(4)] + [k.oinl, k.oul, k.odl],
            lambda: None,
        )
        large_schulz(k, idle)
        k.odr[...] = k.x[...]
    for name in ("dr", "ul", "sq", "dl", "inl"):
        new = getattr(k, "n" + name)
        if ringed:
            need("n" + name)
            put("new_n" + name)
        else:
            need("w" + name)
            weight = getattr(k, "w" + name)[...]
            new[...] = weight - muon_scale(name, weight.shape) * getattr(k, "o" + name)[...]
            put("n" + name)
        getattr(k, "c" + name)[...] = new[...].astype(jnp.bfloat16)
        put("c" + name)
        if ringed:
            need("m" + name)
            put("new_m" + name)
        else:
            put("m" + name)

    if ringed:
        need("block_out", "input_grad", "small", "hid")
        put("new_block_out", "new_input_grad")
        small = k.small[...]
    else:
        small = k.glate[:, width - SMALL :]
    shift = width - SMALL
    lead = starts[2] - shift
    turned = small[:, 0:128].T
    vector_grad = turned[lead : lead + 16][0 : 4 + 3 * KS]
    hidden_grad = jnp.concatenate([k.hid[0:EMB], k.hid[8:136]], axis=0)
    for name, gradient, rate in (
        ("v", vector_grad, rate_vectors),
        ("h", hidden_grad, rate_hidden),
        ("f", small[:, starts[3] - shift :], rate_output),
    ):
        adam(
            [getattr(k, name + kind) for kind in ("w", "1", "2", "1n", "2n", "n", "c")],
            gradient,
            rate,
        )
    for copy in writes.values():
        copy.wait()


def run_update(chained, tokens, moments, weights, small):
    ringed = "out_small" in chained
    hidden = chained["out_hid"].reshape(-1, 128)
    arrays = {}
    shapes = {name: weight.shape for name, weight in zip(KINDS, weights)}
    if ringed:
        arrays.update({"m" + name: chained["out_p" + name] for name in KINDS})
        arrays.update({"n" + name: chained["out_o" + name] for name in KINDS})
        arrays["small"] = chained["out_small"]
        arrays["hid"] = hidden
        loaded = [kind + name for name in ("dr", "ul", "sq", "dl", "inl") for kind in "nm"]
        loaded += ["small", "hid"]
        for name, array in tokens.items():
            arrays[name] = array
            loaded.append(name)
    else:
        arrays.update({"w" + name: weight for name, weight in zip(KINDS, weights)})
        arrays.update({"p" + name: moment for name, moment in zip(KINDS, moments)})
        arrays.update({"g" + name: chained["out_" + name] for name in ("dr", "mid", "late")})
        arrays["hid"] = hidden
        loaded = list(arrays)
    in_hbm = {"hbm_" + name: array for name, array in arrays.items()}
    out_hbm, stored = {}, {}
    scratch = {name: pltpu.VMEM(arrays[name].shape, jnp.float32) for name in loaded}
    for name, shape in shapes.items():
        for kind, dtype in (("m", jnp.float32), ("n", jnp.float32), ("c", jnp.bfloat16)):
            target = ("new_" if kind in "mn" and ringed else "") + kind + name
            out_hbm["hbm_" + target] = jax.ShapeDtypeStruct(shape, dtype)
            stored[target] = kind + name
            scratch.setdefault(kind + name, pltpu.VMEM(shape, dtype))
        if not ringed:
            scratch["o" + name] = pltpu.VMEM(shape, jnp.float32)
    if ringed:
        for name, array in tokens.items():
            out_hbm["hbm_new_" + name] = jax.ShapeDtypeStruct(array.shape, jnp.float32)
            stored["new_" + name] = name
    in_vmem, out_vmem = {}, {}
    for name, (weight, first, second) in small.items():
        in_vmem[name + "w"], in_vmem[name + "1"], in_vmem[name + "2"] = weight, first, second
        for suffix in ("1n", "2n", "n"):
            out_vmem[name + suffix] = jax.ShapeDtypeStruct(weight.shape, jnp.float32)
        out_vmem[name + "c"] = jax.ShapeDtypeStruct(weight.shape, jnp.bfloat16)
    if not ringed:
        size = shapes["dr"]
        scratch.update({n: pltpu.VMEM(size, jnp.float32) for n in ("x", "a")})
        for name in ("xh", "xl", "ah", "al", "ph", "pl"):
            scratch[name] = pltpu.VMEM(size, jnp.bfloat16)
    scratch["read_sem"] = pltpu.SemaphoreType.DMA((len(loaded),))
    scratch["write_sem"] = pltpu.SemaphoreType.DMA((len(stored),))
    vmem = pl.BlockSpec(memory_space=pltpu.VMEM)
    hbm = pl.BlockSpec(memory_space=pl.ANY)
    names = [*in_hbm, *in_vmem, *out_hbm, *out_vmem, *scratch]
    results = pl.pallas_call(
        functools.partial(update_kernel, names, loaded, stored, ringed),
        out_shape=[*out_hbm.values(), *out_vmem.values()],
        in_specs=[hbm] * len(in_hbm) + [vmem] * len(in_vmem),
        out_specs=[hbm] * len(out_hbm) + [vmem] * len(out_vmem),
        scratch_shapes=list(scratch.values()),
        compiler_params=pltpu.CompilerParams(vmem_limit_bytes=60 * 2**20),
        name="update",
    )(*in_hbm.values(), *in_vmem.values())
    new = dict(zip([*out_hbm, *out_vmem], results))
    return {name.removeprefix("hbm_").removeprefix("new_"): value for name, value in new.items()}


def per_device(
    block_input,
    out_grad,
    lengths,
    square_factors,
    square_moment,
    input_left,
    input_left_moment,
    up_left,
    up_left_moment,
    down_right,
    down_right_moment,
    down_left,
    down_left_moment,
    vectors,
    vectors_first,
    vectors_second,
    filter_hidden,
    hidden_first,
    hidden_second,
    filter_out,
    filter_out_first,
    filter_out_second,
):
    weights = (square_factors[:, 0], input_left[0], up_left[0], down_right[0], down_left[0].T)
    moments = (
        square_moment[:, 0],
        input_left_moment[0],
        up_left_moment[0],
        down_right_moment[0],
        down_left_moment[0].T,
    )
    block_output, input_grad, chained = run_chain(
        block_input, out_grad, lengths, weights, moments, vectors, filter_hidden, filter_out.T
    )
    small = dict(
        v=(vectors, vectors_first, vectors_second),
        h=(filter_hidden, hidden_first, hidden_second),
        f=(filter_out.T, filter_out_first.T, filter_out_second.T),
    )
    tokens = dict(block_out=block_output, input_grad=input_grad)
    new = tokens | run_update(chained, tokens, moments, weights, small)
    return (
        new["block_out"].reshape(block_input.shape),
        new["input_grad"].reshape(block_input.shape),
        *[new[kind + "sq"][:, None] for kind in "mnc"],
        *[new[kind + name][None] for name in ("inl", "ul", "dr") for kind in "mnc"],
        *[new[kind + "dl"].T[None] for kind in "mnc"],
        *[new[name + suffix] for name in "vh" for suffix in ("1n", "2n", "n", "c")],
        *[new["f" + suffix].T for suffix in ("1n", "2n", "n", "c")],
    )


def solution(mesh):
    tokens = P(None, "seq", "mp")
    square = P(None, "mp", None, None)
    block = P("mp", None, None)
    row = P(None, "mp")
    return jax.shard_map(
        per_device,
        mesh=mesh,
        in_specs=(tokens, tokens, P(), square, square)
        + (block,) * 8
        + (row,) * 3
        + (P(),) * 3
        + (row,) * 3,
        out_specs=(tokens, tokens)
        + (square,) * 3
        + (block,) * 12
        + (row,) * 4
        + (P(),) * 4
        + (row,) * 4,
        check_vma=False,
    )
```

```python
import functools
import math
import types

import jax
import jax.numpy as jnp
import numpy as np
from jax import lax
from jax.experimental import pallas as pl
from jax.experimental.pallas import tpu as pltpu
from jax.sharding import PartitionSpec as P

EMB = 5
KS = 3
STEP = 10
SEQS = 2

HIGH = lax.Precision.HIGH
HIGHEST = lax.Precision.HIGHEST
MESH = pl.DeviceIdType.MESH
norm_epsilon = 1e-05
beta_first = 0.9
beta_second = 0.95
adam_epsilon = 1e-08
weight_decay = 0.01
rate_vectors = 0.2
rate_hidden = 0.05
rate_output = 0.05
muon_rate = 0.5
momentum_decay = 0.5
schulz_first = 3.4445
schulz_second = -4.775
schulz_third = 2.0315
filter_frequency = 10.0
gelu_scale = math.sqrt(2.0 / math.pi)
gelu_cubic = 0.044715


def contract(a, b, dim_a, dim_b, precision=HIGH):
    return lax.dot_general(
        a,
        b,
        (((dim_a,), (dim_b,)), ((), ())),
        precision=precision,
        preferred_element_type=jnp.float32,
    )


def nn(a, b, precision=HIGH):
    return contract(a, b, 1, 0, precision)


def nt(a, b, precision=HIGH):
    return contract(a, b, 1, 1, precision)


def tn(a, b, precision=HIGH):
    return contract(a, b, 0, 0, precision)


def spectrum_tables(group_len):
    rows = SEQS * group_len
    period = 2 * group_len
    time = np.arange(group_len)
    lags = np.arange(period)
    bins = np.arange(group_len)
    angle = 2.0 * np.pi * (np.outer(time, bins) % period) / period
    real = np.cos(angle)
    imag = -np.sin(angle)
    imag[:, 0] = (-1.0) ** time
    forward = np.zeros((rows, 2 * rows))
    for s in range(SEQS):
        part = slice(s * group_len, (s + 1) * group_len)
        forward[part, part] = real
        forward[part, rows + s * group_len : rows + (s + 1) * group_len] = imag
    of_taps = np.concatenate([real] * SEQS + [imag] * SEQS, axis=1)
    angle = 2.0 * np.pi * (np.outer(bins, lags) % period) / period
    back_real = 2.0 * np.cos(angle) / period
    back_real[0] = 1.0 / period
    back_imag = -2.0 * np.sin(angle) / period
    back_imag[0] = (-1.0) ** lags / period
    inverse = np.zeros((2 * rows, rows))
    for s in range(SEQS):
        part = slice(s * group_len, (s + 1) * group_len)
        inverse[part, part] = back_real[:, :group_len]
        inverse[rows + s * group_len : rows + (s + 1) * group_len, part] = back_imag[:, :group_len]
    window = np.concatenate([back_real] * SEQS + [back_imag] * SEQS, axis=0)
    return tuple(
        v.astype(np.float32)
        for v in (forward, of_taps, inverse, window[:, :group_len], window[:, group_len:])
    )


def feature_table(length):
    fraction = np.arange(length).astype(np.float32) / np.float32(length)
    angle = np.float32(2.0 * math.pi) * fraction
    wide = angle.astype(np.float64)
    twice = (np.float32(2.0) * angle).astype(np.float64)
    columns = [fraction, np.cos(wide), np.sin(wide), np.cos(twice), np.sin(twice)]
    table = np.zeros((length, 8), np.float32)
    for i, column in enumerate(columns):
        table[:, i] = column.astype(np.float32)
    return table


KINDS = ("sq", "inl", "ul", "dr", "dl")
LARGE = ("dr", "ul", "dl")


def muon_scale(name, shape):
    rows, cols = shape[-2:]
    if name == "dl":
        rows, cols = cols, rows
    return muon_rate * math.sqrt(max(rows, cols) / rows)


def late_columns(C):
    start = [0, 4 * C, 7 * C, 7 * C + C // 3, 7 * C + C // 3 + 128]
    return start, 7 * C + C // 3 + 256


def when(condition, body):
    if isinstance(condition, bool):
        if condition:
            body()
    else:
        pl.when(condition)(body)


SERVED = (
    "M", "L", "", "LM", "", "L", "", "M", "L", "", "M", "L", "", "M", "LM",
)
SERVED_MIDDLE = ("", "L", "", "L", "L")
EARLY = ("block_in", "vec", "out_grad", "fo", "fh", "feat", "tfwd", "ttap", "tinv", "tw1", "tw2")


class Ring:
    def __init__(self, grad, total, far_slot, near_slot, ssem, rsem, rows, columns, way, place, count, ids):
        self.grad, self.total = grad, total
        self.far_slot, self.near_slot = far_slot, near_slot
        self.ssem, self.rsem = ssem, rsem
        self.stride, self.offset, self.height = rows
        self.columns = columns
        self.sign = 1 if way == 0 else -1
        self.place, self.count = place, count
        self.ahead, self.behind = ids if way == 0 else ids[::-1]
        self.gathers = far_slot is None

    def part(self, ref, ahead):
        chunk = lax.rem(self.place + self.sign * ahead + 4 * self.count, self.count)
        start = pl.multiple_of(chunk * self.stride + self.offset, 8)
        return ref.at[pl.ds(start, self.height), self.columns]

    def copy(self, source, target, index, to):
        return pltpu.make_async_remote_copy(
            src_ref=source,
            dst_ref=target,
            send_sem=self.ssem.at[int(index >= self.count - 1)],
            recv_sem=self.rsem.at[index],
            device_id=to,
            device_id_type=MESH,
        )

    def far_sum(self, i):
        n = self.count // 2
        return self.copy(self.part(self.grad, n - i), self.far_slot.at[i], i, self.ahead)

    def near_sum(self, i):
        n = self.count // 2
        source = self.part(self.grad, i - (n - 1))
        return self.copy(source, self.near_slot.at[i], n + i, self.behind)

    def far_total(self, i, hops=0):
        n = self.count // 2
        whole = self.part(self.total, i + hops)
        return self.copy(whole, whole, 2 * n - 1 + i, self.behind)

    def near_total(self, i, hops=0):
        n = self.count // 2
        whole = self.part(self.total, -i - hops)
        return self.copy(whole, whole, 3 * n - 1 + i, self.ahead)

    def begin(self):
        self.far_sum(0).start()
        self.near_sum(0).start()

    def begin_totals(self):
        self.far_total(0).start()
        self.near_total(0).start()

    def event(self, s):
        n = self.count // 2

        def add_far():
            mine = self.part(self.grad, n - 1 - s)
            mine[...] = mine[...] + self.far_slot[s]
            self.far_sum(s + 1).start()

        def add_near():
            mine = self.part(self.grad, s - (n - 2))
            mine[...] = mine[...] + self.near_slot[s]
            self.near_sum(s + 1).start()

        def turn():
            own = self.part(self.total, 0)
            mine = self.part(self.grad, 0)
            own[...] = mine[...] + self.far_slot[n - 1] + self.near_slot[n - 2]
            self.begin_totals()

        both = lambda p, q: p and q if isinstance(p, bool) else p & q
        i = s - n
        when(s < n, lambda: self.far_sum(s).wait_recv())
        when(s < n - 1, add_far)
        when(s < n - 1, lambda: self.near_sum(s).wait_recv())
        when(s < n - 2, add_near)
        when(s == n - 1, turn)
        when(both(s >= n, s < 2 * n), lambda: self.far_total(i, 1).wait_recv())
        when(both(s >= n, s < 2 * n - 1), lambda: self.far_total(i + 1).start())
        when(both(s >= n, s < 2 * n - 1), lambda: self.near_total(i, 1).wait_recv())
        when(both(s >= n, s < 2 * n - 2), lambda: self.near_total(i + 1).start())

    def end(self):
        part = self.total.at[pl.ds(0, self.height * (self.count - 1)), self.columns]
        for index in (self.count - 1,) if self.gathers else (0, self.count - 1):
            self.copy(part, part, index, self.ahead).wait_send()


def unit_scale(values):
    return 1.0 / (jnp.sqrt(jnp.sum(values * values)) + 1e-07)


def halves(values):
    high = values.astype(jnp.bfloat16)
    return high, (values - high.astype(jnp.float32)).astype(jnp.bfloat16)


def thrice(left, right, product):
    a, b = left
    c, d = right
    plain = lambda m, n: product(m, n, None)
    return plain(a, c) + plain(a, d) + plain(b, c)


def idle(product):
    pass


def large_schulz(k, between):
    size = k.x.shape[0]
    tile = 256
    strips = [
        (slice(i * tile, (i + 1) * tile), slice(0, (i + 1) * tile)) for i in range(size // tile)
    ]

    def keep(high, low, rows, columns, values):
        high[rows, columns], low[rows, columns] = halves(values)
        if rows.start:
            turned = values[:, 0 : rows.start].T
            high[0 : rows.start, rows], low[0 : rows.start, rows] = halves(turned)

    def newton_step(step):
        k.xh[...], k.xl[...] = halves(k.x[...])
        for i, (rows, columns) in enumerate(strips):
            gram = thrice((k.xh[rows], k.xl[rows]), (k.xh[columns], k.xl[columns]), nt)
            k.a[rows, columns] = gram
            keep(k.ah, k.al, rows, columns, gram)
        between(3 * step)
        for i, (rows, columns) in enumerate(strips):
            squared = thrice(
                (k.ah[rows], k.al[rows]), (k.ah[:, columns], k.al[:, columns]), nn
            )
            values = schulz_second * k.a[rows, columns] + schulz_third * squared
            keep(k.ph, k.pl, rows, columns, values)
        between(3 * step + 1)
        for i in range(2):
            rows = slice(i * size // 2, (i + 1) * size // 2)
            k.x[rows] = schulz_first * k.x[rows] + thrice(
                (k.ph[rows], k.pl[rows]), (k.xh[...], k.xl[...]), nn
            )
        between(3 * step + 2)

    if between is idle:
        pl.loop(0, 5)(newton_step)
    else:
        for step in range(5):
            newton_step(step)


def small_schulz(moments, results, between):
    current = [moment[...] * unit_scale(moment[...]) for moment in moments]
    for step in range(5):
        split = [halves(values) for values in current]
        grams = [thrice(one, one, nt) for one in split]
        split_grams = [halves(gram) for gram in grams]
        squared = [thrice(one, one, nn) for one in split_grams]
        factors = [
            halves(schulz_second * gram + schulz_third * square)
            for gram, square in zip(grams, squared)
        ]
        current = [
            schulz_first * values + thrice(factor, one, nn)
            for values, factor, one in zip(current, factors, split)
        ]
        between()
    for result, values in zip(results, current):
        result[...] = values


def chain_kernel(dims, names, *refs):
    k = types.SimpleNamespace(**dict(zip(names, refs, strict=True)))
    C, M, Q, GL, CP, cpd, F, LEN, ringed = dims
    R = SEQS * GL
    PW = C // M
    FW = F // M
    D = C * M
    r = lax.axis_index("seq")
    e = lax.axis_index("mp")
    nxt = lax.rem(r + 1, Q)
    prv = lax.rem(r + Q - 1, Q)
    sends = []

    def remote(src, dst, ssem, rsem, seq, mp):
        return pltpu.make_async_remote_copy(
            src_ref=src,
            dst_ref=dst,
            send_sem=ssem,
            recv_sem=rsem,
            device_id={"seq": seq, "mp": mp},
            device_id_type=MESH,
        )

    def swap_blocks(src, dst, phase, same=None):
        for d in range(1, M):
            to = lax.rem(e + d, M)
            source = src.at[to] if same is None else same
            remote(source, dst.at[e], k.mp_sent.at[phase], k.mp_here.at[phase], r, to).start()
        sends.append((dst.at[pl.ds(0, M - 1)], k.mp_sent.at[phase]))
        mine = src[pl.ds(e, 1)] if same is None else same[...].reshape((1,) + same.shape)
        dst[pl.ds(e, 1)] = mine

    def arrive(dst, rsem):
        remote(dst, dst, k.mp_sent.at[0], rsem, nxt, e).wait_recv()

    def blocks_arrive(dst, phase):
        arrive(dst.at[pl.ds(0, M - 1)], k.mp_here.at[phase])

    def swap_seq(src, dst, phase):
        for d in range(1, Q):
            to = lax.rem(r + d, Q)
            remote(
                src.at[to], dst.at[r], k.seq_sent.at[phase], k.seq_here.at[phase], to, e
            ).start()
        sends.append((dst.at[pl.ds(0, Q - 1)], k.seq_sent.at[phase]))
        dst[pl.ds(r, 1)] = src[pl.ds(r, 1)]

    def seq_arrive(dst, phase):
        arrive(dst.at[pl.ds(0, Q - 1)], k.seq_here.at[phase])

    def pieces(dst, values, width):
        for b in range(M):
            dst[b, 0:width] = values[width * b : width * (b + 1)]

    def joined(src, width):
        return jnp.concatenate([src[b, 0:width] for b in range(M)], axis=0)

    def extra(src):
        total = src[0, PW : PW + 8]
        for b in range(1, M):
            total = total + src[b, PW : PW + 8]
        return total[0:1]

    def by_channel(dst, values):
        if CP == cpd:
            dst[...] = values.reshape(Q, CP, values.shape[1])
        else:
            dst[...] = jnp.zeros(dst.shape, jnp.float32)
            for q in range(Q):
                dst[q, 0:cpd] = values[q * cpd : (q + 1) * cpd]

    def from_channels(src):
        if CP == cpd:
            return src[...].reshape(Q * CP, src.shape[2])
        return jnp.concatenate([src[q, 0:cpd] for q in range(Q)], axis=0)

    early = {}
    for i, name in enumerate(EARLY):
        early[name] = pltpu.make_async_copy(
            getattr(k, name + "_hbm"), getattr(k, name), k.esem.at[i]
        )
        early[name].start()
    copies = [
        pltpu.make_async_copy(src, dst, k.wsem.at[i])
        for i, (src, dst) in enumerate(
            (
                (k.sq_hbm, k.sq),
                (k.dl_hbm, k.dl),
                (k.inl_hbm, k.inl),
                (k.ul_hbm, k.ul),
                (k.dr_hbm, k.dr),
            )
        )
    ]
    if ringed:
        copies += [
            pltpu.make_async_copy(getattr(k, f"p{name}_hbm"), dst, k.psem.at[i])
            for i, (name, dst) in enumerate(
                (("dr", k.x), ("ul", k.pul), ("dl", k.pdl))
            )
        ]
    for copy in copies:
        copy.start()

    odd = lax.rem(r, 2)
    place = (1 - odd) * (r // 2) + odd * (Q - 1 - r // 2)

    def at_place(p):
        back = p // (Q // 2)
        return (1 - back) * 2 * p + back * (2 * (Q - 1 - p) + 1)

    ring_ids = tuple(
        {"seq": at_place(lax.rem(place + d, Q)), "mp": e} for d in (1, Q - 1)
    )

    barrier = pltpu.get_barrier_semaphore()
    partners = [(lax.rem(r + d, Q), e) for d in range(1, Q)]
    partners += [(r, lax.rem(e + d, M)) for d in range(1, M)]
    partners += [(s, lax.rem(e + d, M)) for s in (nxt, prv) for d in range(1, M)]
    for seq, mp in partners:
        pl.semaphore_signal(
            barrier, inc=1, device_id={"seq": seq, "mp": mp}, device_id_type=MESH
        )

    gather_rings, first_rings, other_rings, late_rings = [], [], [], []
    if ringed:

        def ring(grad, total, slots, rows, columns, way, index):
            return Ring(
                grad,
                total,
                *slots,
                k.ring_ssem.at[index],
                k.ring_rsem.at[index],
                rows,
                columns,
                way,
                place,
                Q,
                ring_ids,
            )

        tall, low = F // Q, C // Q
        for way in range(2):
            rows = (tall, way * (tall // 2), tall // 2)
            first_rings.append(ring(None, k.tdr, (None, None), rows, slice(0, F), way, way))
            rows = (F, way * (F // 2), F // 2)
            gather_rings.append(ring(None, k.dm4_all, (None, None), rows, slice(0, R), way, 6 + way))
        for rings, grad, total, slots, index in (
            (
                other_rings,
                k.gmid,
                k.tmid,
                ((k.far_mid0, k.near_mid0), (k.far_mid1, k.near_mid1)),
                2,
            ),
            (
                late_rings,
                k.glate,
                k.tlate,
                ((k.far_late0, k.near_late0), (k.far_late1, k.near_late1)),
                4,
            ),
        ):
            width = grad.shape[1]
            cut = width // 256 * 128
            for way, columns in enumerate((slice(0, cut), slice(cut, width))):
                rows = (low, 0, low)
                rings.append(ring(grad, total, slots[way], rows, columns, way, index + way))

    def go(rings, s):
        for one in rings:
            one.event(s)

    outs = []

    def put(source, target):
        copy = pltpu.make_async_copy(source, target, k.osem.at[len(outs)])
        copy.start()
        outs.append(copy)

    halves_done = [Q]

    def first_halves(count):
        if ringed:
            for _ in range(count):
                i = halves_done[0]
                first_rings[i % 2].event(i // 2)
                halves_done[0] += 1

    lane = lax.broadcasted_iota(jnp.int32, (1, R), 1)
    spot = lax.rem(lane, GL)
    first_bin = spot == 0
    flip = jnp.where(lax.rem(spot, 2) == 0, 1.0, -1.0).astype(jnp.float32)
    keep_bin = jnp.where(first_bin, 0.0, 1.0).astype(jnp.float32)
    length_of = jnp.where(lane < GL, k.lengths[0], k.lengths[1])
    position = r * GL + spot
    valid = (position < length_of).astype(jnp.float32)
    has_prev = (r > 0).astype(jnp.float32)
    has_next = (r < Q - 1).astype(jnp.float32)
    tail = spot >= GL - 2
    head = spot < 2
    halo_mask = jnp.where(tail, has_prev, jnp.where(head, has_next, 0.0))
    end_row = lax.broadcasted_iota(jnp.int32, (8, R), 0)
    end_lane = lax.rem(end_row, 4) // 2 * GL + lax.rem(end_row, 2)
    end_lane = end_lane + jnp.where(end_row < 4, 0, GL - 2)
    ends = (lax.broadcasted_iota(jnp.int32, (8, R), 1) == end_lane).astype(jnp.float32)

    early["block_in"].wait()
    early["vec"].wait()
    k.xt[...] = k.block_in[...].T
    k.vecp[...] = jnp.zeros(k.vecp.shape, jnp.float32)
    k.vecp[0 : 4 + 3 * KS] = k.vec[...]
    k.vt[...] = k.vecp[...].T

    def column(i):
        return k.vt[:, i : i + 1]

    xt = k.xt[...]
    u0 = xt * column(0)
    k.u0[...] = u0
    copies[0].wait()
    pieces(k.s0, tn(k.sq[0], u0), PW)
    squares = jnp.broadcast_to(jnp.sum(xt * xt, axis=0, keepdims=True), (8, R))
    for b in range(M):
        k.s0[b, PW : PW + 8] = squares
    pl.semaphore_wait(barrier, len(partners))
    swap_blocks(k.s0, k.r0, 0)
    for b in range(M):
        k.hs0[b, :, 0 : PW + 8] = nt(ends, k.s0[b], HIGHEST)
    halo_after, halo_before = [], []
    for d in range(M):
        to = lax.rem(e + d, M)
        for copies_to, dst, i, seq in ((halo_after, k.hp0, 0, nxt), (halo_before, k.hn0, 1, prv)):
            copies_to.append(
                remote(k.hs0.at[to], dst.at[e], k.halo_sent.at[i], k.halo_here.at[i], seq, to)
            )

    @pl.when(r < Q - 1)
    def _():
        for copy in halo_after:
            copy.start()

    @pl.when(r > 0)
    def _():
        for copy in halo_before:
            copy.start()

    @pl.when(r == 0)
    def _():
        k.hp0[...] = jnp.zeros(k.hp0.shape, jnp.float32)

    @pl.when(r == Q - 1)
    def _():
        k.hn0[...] = jnp.zeros(k.hn0.shape, jnp.float32)

    early["out_grad"].wait()
    k.ogt[...] = k.out_grad[...].T
    copies[1].wait()
    pieces(k.s4, tn(k.dl[...], k.ogt[...]), FW)
    swap_blocks(k.s4, k.r4, 4)
    by_channel(k.vtc, k.vt[...])
    early["fo"].wait()
    by_channel(k.foc, k.fo[...])
    copies[2].wait()

    blocks_arrive(k.r0, 0)

    @pl.when(r > 0)
    def _():
        arrive(k.hp0, k.halo_here.at[0])

    @pl.when(r < Q - 1)
    def _():
        arrive(k.hn0, k.halo_here.at[1])

    scale_one = lax.rsqrt(extra(k.r0) / D + norm_epsilon)
    w0 = joined(k.r0, PW)
    k.w0[...] = w0
    first_half = lax.broadcasted_iota(jnp.int32, (8, 128), 0) < 4
    spread = [
        tn(jnp.where(first_half, k.hn0[b], k.hp0[b]), ends, HIGHEST) for b in range(M)
    ]
    w0h = jnp.concatenate([one[0:PW] for one in spread], axis=0)
    squares = spread[0][PW : PW + 1]
    for b in range(1, M):
        squares = squares + spread[b][PW : PW + 1]
    both = tn(k.inl[...], jnp.concatenate([w0, w0h], axis=1))
    z = both[:, 0:R] * scale_one
    zh = both[:, R : 2 * R] * (lax.rsqrt(squares / D + norm_epsilon) * halo_mask)
    zh_far = pltpu.roll(zh, GL, 1)
    k.z[...] = z
    k.z1[...] = pltpu.roll(jnp.where(spot >= GL - 1, zh_far, z), 1, 1)
    k.z2[...] = pltpu.roll(jnp.where(tail, zh_far, z), 2, 1)
    for s in range(3):
        part = slice(s * C, (s + 1) * C)
        k.conv[part] = (
            column(4 + KS * s) * k.z[part]
            + column(5 + KS * s) * k.z1[part]
            + column(6 + KS * s) * k.z2[part]
        )
    product = k.conv[0:C] * k.conv[2 * C : 3 * C] * valid
    k.prod[...] = product
    by_channel(k.ps, product)
    swap_seq(k.ps, k.ur, 0)

    for name in EARLY[4:]:
        early[name].wait()
    pre = filter_frequency * nn(k.feat[...], k.fh[0:8], HIGHEST)
    k.l1[...] = jnp.sin(pre)
    k.c1[...] = filter_frequency * jnp.cos(pre)
    if ringed:
        blocks_arrive(k.r4, 4)
        k.dm4_all[pl.ds(pl.multiple_of(place * F, F), F)] = k.r4[...].reshape(F, R)
        gather_rings[0].begin_totals()
    pre = filter_frequency * nn(k.l1[...], k.fh[EMB : EMB + 128], HIGHEST)
    k.l2[...] = jnp.sin(pre)
    k.c2[...] = filter_frequency * jnp.cos(pre)
    foc = k.foc[pl.ds(r, 1)].reshape(CP, 128)
    vtc = k.vtc[pl.ds(r, 1)].reshape(CP, 128)
    rate = vtc[:, 2:3]
    skip_channel = vtc[:, 3:4]
    shaped = nt(foc, k.l2[...], HIGHEST)
    part_lane = lax.broadcasted_iota(jnp.int32, (1, GL), 1)
    for q in range(Q):
        fraction = (part_lane + q * GL).astype(jnp.float32) / LEN
        decay = jnp.exp(-fraction * rate) * (LEN ** (-0.5))
        k.decay[q] = decay
        k.taps[q] = shaped[:, q * GL : (q + 1) * GL] * decay
    spectrum = nn(k.taps[...].reshape(Q * CP, GL), k.ttap[...]).reshape(Q, CP, 2 * R)
    for q in range(Q):
        real = spectrum[q, :, 0:R]
        imag = spectrum[q, :, R : 2 * R]
        if q > 0:
            real = real + flip * spectrum[q - 1, :, 0:R]
            imag = imag + flip * spectrum[q - 1, :, R : 2 * R]
        k.kr[q] = real
        k.km[q] = imag * keep_bin
        k.k4[q] = jnp.where(first_bin, imag, real)

    def total_pairs(count, first, term):
        zero = jnp.zeros((CP, R), jnp.float32)
        if Q <= 8:
            real, imag = zero, zero
            for i in range(count):
                add_real, add_imag = term(first + i)
                real, imag = real + add_real, imag + add_imag
            return real, imag

        def body(i, kept):
            add_real, add_imag = term(first + i)
            return (kept[0] + add_real, kept[1] + add_imag)

        return lax.fori_loop(0, count, body, (zero, zero))

    def each_block(body):
        if Q <= 8:
            for q in range(Q):
                body(q)
        else:
            pl.loop(0, Q)(body)

    seq_arrive(k.ur, 0)
    k.us[...] = nn(k.ur[...].reshape(Q * CP, R), k.tfwd[...]).reshape(Q, CP, 2 * R)

    def forward_block(p):
        def term(q):
            real = k.us[q, :, 0:R]
            imag = k.us[q, :, R : 2 * R]
            lag = p - q
            return (
                k.kr[lag] * real - k.km[lag] * imag,
                k.km[lag] * real + k.k4[lag] * imag,
            )

        real, imag = total_pairs(p + 1, 0, term)
        k.zs[p, :, 0:R] = real
        k.zs[p, :, R : 2 * R] = imag

    each_block(forward_block)
    k.ys[...] = nn(k.zs[...].reshape(Q * CP, 2 * R), k.tinv[...]).reshape(Q, CP, R)
    swap_seq(k.ys, k.yr, 1)
    if ringed:
        gather_rings[1].begin_totals()
    for q in range(Q):
        real = k.us[q, :, 0:R]
        imag = k.us[q, :, R : 2 * R]
        k.um[q] = imag * keep_bin
        k.u4[q] = jnp.where(first_bin, imag, real)

    copies[3].wait()
    k.ult_h[...], k.ult_l[...] = halves(k.ul[...].T)
    if ringed:
        copies[4].wait()
        k.ph[...], k.pl[...] = halves(k.dr[...].T)
    seq_arrive(k.yr, 1)
    inner_sum = from_channels(k.yr) + column(3) * k.prod[...]
    k.insum[...] = inner_sum
    gated = k.conv[C : 2 * C] * inner_sum
    k.gated[...] = gated
    pieces(k.s1, tn(k.sq[1], gated), PW)
    swap_blocks(k.s1, k.r1, 1)

    if ringed:
        gather_rings[0].event(Q // 2 + 0)
    if not ringed:
        copies[4].wait()
    if not ringed:
        blocks_arrive(k.r4, 4)
    k.dact[...] = nn(k.dr[...], k.r4[...].reshape(F, R))

    if ringed:
        gather_rings[1].event(Q // 2 + 0)
    blocks_arrive(k.r1, 1)
    w1 = k.r1[...].reshape(C, R)
    k.w1[...] = w1
    h = k.xt[...] + tn(k.sq[2], w1)
    k.h[...] = h
    u3 = h * column(1)
    pieces(k.s2, tn(k.sq[3], u3), PW)
    squares = jnp.broadcast_to(jnp.sum(h * h, axis=0, keepdims=True), (8, R))
    for b in range(M):
        k.s2[b, PW : PW + 8] = squares
    swap_blocks(k.s2, k.r2, 2)

    if ringed:
        gather_rings[0].event(Q // 2 + 1)
    blocks_arrive(k.r2, 2)
    scale_two = lax.rsqrt(extra(k.r2) / D + norm_epsilon)
    k.n2[...] = k.h[...] * scale_two
    w3 = joined(k.r2, PW)
    k.w3[...] = w3
    k.gu[...] = thrice((k.ult_h[...], k.ult_l[...]), halves(w3), nn) * scale_two
    gate = k.gu[0:F]
    up = k.gu[F : 2 * F]
    bend = jnp.tanh(gelu_scale * (gate + gelu_cubic * gate * gate * gate))
    gelu = 0.5 * gate * (1.0 + bend)
    slope = 0.5 * (1.0 + bend) + 0.5 * gate * (1.0 - bend * bend) * gelu_scale * (
        1.0 + 3.0 * gelu_cubic * gate * gate
    )
    dact = k.dact[...]
    k.act[...] = gelu * up
    k.dgu[0:F] = dact * up * slope
    k.dgu[F : 2 * F] = dact * gelu
    back = nn(k.ul[...], k.dgu[...])
    pieces(k.s5, back, PW)
    inner = jnp.broadcast_to(jnp.sum(back * k.w3[...], axis=0, keepdims=True), (8, R))
    for b in range(M):
        k.s5[b, PW : PW + 8] = inner
    swap_blocks(k.s5, k.r5, 5)
    if ringed:
        tall = F // Q

        def act_rows(p):
            return k.act.at[pl.ds(pl.multiple_of(p * tall, tall), tall)]

        for d in range(1, Q):
            p = lax.rem(place + d, Q)
            remote(
                act_rows(p),
                k.act_all.at[place],
                k.act_sent.at[0],
                k.act_here.at[0],
                at_place(p),
                e,
            ).start()
        sends.append((k.act_all.at[pl.ds(0, Q - 1)], k.act_sent.at[0]))
        k.act_all[pl.ds(place, 1)] = act_rows(place)[...].reshape(1, tall, R)
        gather_rings[1].event(Q // 2 + 1)
    else:
        k.gdr[...] = nt(k.act[...], k.r4[...].reshape(F, R))
    if ringed:
        pieces(k.s3, thrice((k.ph[...], k.pl[...]), halves(k.act[...]), nn), FW)
    else:
        pieces(k.s3, tn(k.dr[...], k.act[...]), FW)
    swap_blocks(k.s3, k.r3, 3)

    k.gmid[:, 0 : 2 * F] = nt(k.w3[...] * scale_two, k.dgu[...])
    if ringed:
        gather_rings[0].event(Q // 2 + 2)
    blocks_arrive(k.r5, 5)
    back = joined(k.r5, PW)
    inner = extra(k.r5)
    grad_two = nn(k.sq[3], back)
    hidden_grad = (
        k.ogt[...]
        + scale_two * (grad_two * column(1))
        - k.h[...] * (scale_two * scale_two * scale_two * inner / D)
    )
    k.hg[...] = hidden_grad
    pieces(k.s6, nn(k.sq[2], hidden_grad), PW)
    swap_blocks(k.s6, k.r6, 6)
    k.glate[:, 3 * C : 4 * C] = nt(k.n2[...] * column(1), back)
    gain_two = jnp.sum(grad_two * k.n2[...], axis=1, keepdims=True)
    k.glate[:, 2 * C : 3 * C] = nt(k.w1[...], k.hg[...])

    blocks_arrive(k.r6, 6)
    back = k.r6[...].reshape(C, R)
    gated_grad = nn(k.sq[1], back)
    inner_grad = gated_grad * k.conv[C : 2 * C]
    k.inner[...] = inner_grad
    k.d1[...] = gated_grad * k.insum[...]
    by_channel(k.inner_s, inner_grad)
    swap_seq(k.inner_s, k.vr, 2)
    k.glate[:, C : 2 * C] = nt(k.gated[...], back)
    skip_total = jnp.sum(inner_grad * k.prod[...], axis=1, keepdims=True)

    if ringed:
        gather_rings[1].event(Q // 2 + 2)
        for one in gather_rings:
            one.event(Q // 2 + 3)
    seq_arrive(k.vr, 2)
    k.vs[...] = nn(k.vr[...].reshape(Q * CP, R), k.tfwd[...]).reshape(Q, CP, 2 * R)

    def back_block(q):
        def term(p):
            real = k.vs[p, :, 0:R]
            imag = k.vs[p, :, R : 2 * R]
            lag = p - q
            return (
                k.kr[lag] * real + k.km[lag] * imag,
                k.k4[lag] * imag - k.km[lag] * real,
            )

        real, imag = total_pairs(Q - q, q, term)
        k.zs[q, :, 0:R] = real
        k.zs[q, :, R : 2 * R] = imag

    each_block(back_block)
    k.ds[...] = (
        nn(k.zs[...].reshape(Q * CP, 2 * R), k.tinv[...]).reshape(Q, CP, R)
        + skip_channel[None] * k.vr[...]
    )
    swap_seq(k.ds, k.dmain, 3)
    if ringed:
        arrive(k.act_all.at[pl.ds(0, Q - 1)], k.act_here.at[0])
        acts = jnp.concatenate([k.act_all[p] for p in range(Q)], axis=1)
        backs = jnp.concatenate([k.dm4_all[p * F : (p + 1) * F] for p in range(Q)], axis=1)
        k.tdr[pl.ds(pl.multiple_of(place * tall, tall), tall)] = nt(acts, backs)
        for one in first_rings:
            one.begin_totals()
    first_halves(1)
    def lag_block(j):
        def term(p):
            real = k.vs[p, :, 0:R]
            imag = k.vs[p, :, R : 2 * R]
            q = p - j
            return (
                k.us[q, :, 0:R] * real + k.um[q] * imag,
                k.u4[q] * imag - k.um[q] * real,
            )

        real, imag = total_pairs(Q - j, j, term)
        k.zs[j, :, 0:R] = real
        k.zs[j, :, R : 2 * R] = imag

    each_block(lag_block)
    cross = k.zs[...].reshape(Q * CP, 2 * R)
    near = nn(cross, k.tw1[...]).reshape(Q, CP, GL)
    far = nn(cross, k.tw2[...]).reshape(Q, CP, GL)
    decay_total = jnp.zeros((CP, 1), jnp.float32)
    for q in range(Q):
        grad = near[q]
        if q < Q - 1:
            grad = grad + far[q + 1]
        fraction = (part_lane + q * GL).astype(jnp.float32) / LEN
        decay_total = decay_total - jnp.sum(
            grad * k.taps[q] * fraction, axis=1, keepdims=True
        )
        k.draw[:, q * GL : (q + 1) * GL] = grad * k.decay[q]
    raw = k.draw[...]
    k.gfo[...] = jnp.zeros(k.gfo.shape, jnp.float32)
    k.gdec[...] = jnp.zeros(k.gdec.shape, jnp.float32)
    k.gfo[pl.ds(r, 1)] = nn(raw, k.l2[...]).reshape(1, CP, 128)
    k.gdec[pl.ds(r, 1)] = jnp.broadcast_to(decay_total, (CP, 128)).reshape(1, CP, 128)
    first_halves(1)
    blocks_arrive(k.r3, 3)
    w4 = k.r3[...].reshape(F, R)
    k.block_out[...] = (k.h[...] + nn(k.dl[...], w4)).T
    put(k.block_out, k.block_out_hbm)
    k.gmid[:, 2 * F : 3 * F] = nt(k.ogt[...], w4)
    for one in other_rings:
        one.begin()
    back = tn(raw, foc) * k.c2[...]
    k.hid[8:136] = tn(k.l1[...], back)
    back = nt(back, k.fh[EMB : EMB + 128]) * k.c1[...]
    k.hid[0:8] = tn(k.feat[...], back)
    swap_blocks(None, k.hids, 8, k.hid)


    first_halves(1)
    seq_arrive(k.dmain, 3)
    product_grad = from_channels(k.dmain) * valid
    k.d3[0:C] = product_grad * k.conv[2 * C : 3 * C]
    k.d3[C : 2 * C] = k.d1[...]
    k.d3[2 * C : 3 * C] = product_grad * k.conv[0:C]
    k.hs1[...] = nt(ends, k.d3[...], HIGHEST)
    edge = remote(k.hs1, k.hr1, k.halo_sent.at[2], k.halo_here.at[2], prv, e)

    @pl.when(r > 0)
    def _():
        edge.start()

    @pl.when(r == Q - 1)
    def _():
        k.hr1[...] = jnp.zeros(k.hr1.shape, jnp.float32)

    first_halves(1)

    @pl.when(r < Q - 1)
    def _():
        arrive(k.hr1, k.halo_here.at[2])

    following = pltpu.roll(tn(k.hr1[...], ends, HIGHEST), GL, 1)
    tap_totals = []
    for s in range(3):
        part = slice(s * C, (s + 1) * C)
        grad = k.d3[part]
        one = pltpu.roll(jnp.where(spot == 0, following[part], grad), R - 1, 1)
        two = pltpu.roll(jnp.where(head, following[part], grad), R - 2, 1)
        k.dz[part] = (
            column(4 + KS * s) * grad + column(5 + KS * s) * one + column(6 + KS * s) * two
        )
        for shifted in (k.z, k.z1, k.z2):
            tap_totals.append(jnp.sum(grad * shifted[part], axis=1, keepdims=True))
    back = nn(k.inl[...], k.dz[...])
    pieces(k.s7, back, PW)
    inner = jnp.broadcast_to(jnp.sum(back * k.w0[...], axis=0, keepdims=True), (8, R))
    for b in range(M):
        k.s7[b, PW : PW + 8] = inner
    swap_blocks(k.s7, k.r7, 7)
    k.glate[:, 4 * C : 7 * C] = nt(k.w0[...] * scale_one, k.dz[...])

    first_halves(1)
    if ringed:
        go(other_rings, 0)
    blocks_arrive(k.r7, 7)
    back = joined(k.r7, PW)
    inner = extra(k.r7)
    grad_one = nn(k.sq[0], back)
    xt = k.xt[...]
    k.input_grad[...] = (
        k.hg[...]
        + scale_one * (grad_one * column(0))
        - xt * (scale_one * scale_one * scale_one * inner / D)
    ).T
    put(k.input_grad, k.input_grad_hbm)
    k.glate[:, 0:C] = nt(k.u0[...] * scale_one, back)
    gain_one = jnp.sum(grad_one * xt * scale_one, axis=1, keepdims=True)
    starts, width = late_columns(C)
    slot = lax.broadcasted_iota(jnp.int32, (1, 16), 1)
    rows = {0: gain_one, 1: gain_two, 2: from_channels(k.gdec)[:, 0:1], 3: skip_total}
    rows.update({4 + i: total for i, total in enumerate(tap_totals)})
    stacked = jnp.zeros((C, 16), jnp.float32)
    for i, total in rows.items():
        stacked = jnp.where(slot == i, total, stacked)
    k.glate[:, starts[2] : starts[3]] = jnp.zeros((C, starts[3] - starts[2]), jnp.float32)
    k.glate[:, starts[2] : starts[2] + 16] = stacked
    k.glate[:, starts[3] : starts[4]] = from_channels(k.gfo)
    first_halves(1)
    blocks_arrive(k.hids, 8)
    hidden_sum = k.hids[0]
    for b in range(1, M):
        hidden_sum = hidden_sum + k.hids[b]
    k.glate[0:136, starts[4] : width] = hidden_sum
    k.glate[136:C, starts[4] : width] = jnp.zeros((C - 136, 128), jnp.float32)

    if ringed:
        first_halves(max(0, 2 * Q - 2 - halves_done[0]))
        for one in late_rings:
            one.begin()
        go(other_rings, 1)
        first_halves(2 * Q - halves_done[0])
        for copy in copies[5:]:
            copy.wait()
        moment = momentum_decay * k.x[...] + k.tdr[...]
        k.moment[...] = moment
        put(k.moment, k.out_pdr)
        k.x[...] = moment * unit_scale(moment)
        mid_turns, late_turns = iter(range(2, Q)), iter(range(Q))

        def turn(rings, turns):
            s = next(turns, None)
            if s is not None:
                go(rings, s)

        def serve(letters):
            for letter in letters:
                if letter == "M":
                    turn(other_rings, mid_turns)
                else:
                    turn(late_rings, late_turns)

        def between(product):
            serve(SERVED[product])

        def renew(name, weight, result, target):
            result[...] = weight[...] - muon_scale(name, weight.shape) * result[...]
            put(result, target)

        large_schulz(k, between)
        renew("dr", k.dr, k.x, k.out_odr)
        for s in mid_turns:
            go(other_rings, s)
        steps = iter(SERVED_MIDDLE)
        for moment, columns in ((k.pul, slice(0, 2 * F)), (k.pdl, slice(2 * F, 3 * F))):
            moment[...] = momentum_decay * moment[...] + k.tmid[:, columns]
        put(k.pul, k.out_pul)
        put(k.pdl, k.out_pdl)
        small_schulz((k.pul, k.pdl), (k.oul, k.odl), lambda: serve(next(steps)))
        renew("ul", k.ul, k.oul, k.out_oul)
        renew("dl", k.dl, k.odl, k.out_odl)
        for s in late_turns:
            go(late_rings, s)
        put(k.tlate, k.out_late)
        for one in gather_rings + first_rings + other_rings + late_rings:
            one.end()
    else:
        put(k.gdr, k.out_dr)
        put(k.gmid, k.out_mid)
        put(k.glate, k.out_late)
    for copy in outs:
        copy.wait()
    for ref, sem in sends:
        remote(ref, ref, sem, k.mp_here.at[0], nxt, e).wait_send()

    @pl.when(r < Q - 1)
    def _():
        remote(k.hs0, k.hp0, k.halo_sent.at[0], k.halo_here.at[0], nxt, e).wait_send()

    @pl.when(r > 0)
    def _():
        remote(k.hs0, k.hn0, k.halo_sent.at[1], k.halo_here.at[1], prv, e).wait_send()
        edge.wait_send()


def run_chain(x, og, lengths, weights, moments, vectors, fh, fo):
    M, Q = lax.axis_size("mp"), lax.axis_size("seq")
    sq, inl, ul, dr, dl = weights
    _, GL, C = x.shape
    R = SEQS * GL
    F = dr.shape[0]
    LEN = GL * Q
    cpd = C // Q
    CP = -(-cpd // 8) * 8
    PW, FW = C // M, F // M
    ringed = cpd % 8 == 0 and F % (32 * Q) == 0
    dims = (C, M, Q, GL, CP, cpd, F, LEN, ringed)
    tables = spectrum_tables(GL)
    feat = feature_table(LEN)
    width = late_columns(C)[1]
    sds = lambda *shape: jax.ShapeDtypeStruct(shape, jnp.float32)
    v = lambda *shape: pltpu.VMEM(shape, jnp.float32)
    dma = lambda *shape: pltpu.SemaphoreType.DMA(shape)
    first = dict(
        block_in=x.reshape(R, C),
        out_grad=og.reshape(R, C),
        vec=vectors,
        fh=fh,
        fo=fo,
        feat=feat,
        **dict(zip(("tfwd", "ttap", "tinv", "tw1", "tw2"), tables)),
    )
    in_hbm = {name + "_hbm": array for name, array in first.items()}
    in_hbm.update(sq_hbm=sq, inl_hbm=inl, ul_hbm=ul, dr_hbm=dr, dl_hbm=dl)
    if ringed:
        in_hbm.update((f"p{n}_hbm", p) for n, p in zip(KINDS, moments) if n in LARGE)
    out_first = dict(block_out=sds(R, C), input_grad=sds(R, C))
    out_hbm = dict(out_dr=sds(F, F), out_mid=sds(C, 3 * F), out_late=sds(C, width))
    if ringed:
        out_hbm = {
            f"out_{x}{n}": sds(*w.shape) for x in "po" for n, w in zip(KINDS, weights) if n in LARGE
        }
        out_hbm["out_late"] = sds(C, width)
    scratch = dict(
        sq=v(4, C, C),
        inl=v(C, 3 * C),
        ul=v(C, 2 * F),
        dr=v(F, F),
        dl=v(C, F),
        vecp=v(128, C),
        vt=v(C, 128),
        vtc=v(Q, CP, 128),
        foc=v(Q, CP, 128),
        gfo=v(Q, CP, 128),
        gdec=v(Q, CP, 128),
        gu=v(2 * F, R),
        act=v(F, R),
        dact=v(F, R),
        dgu=v(2 * F, R),
        block_out=v(R, C),
        input_grad=v(R, C),
        ult_h=pltpu.VMEM((2 * F, C), jnp.bfloat16),
        ult_l=pltpu.VMEM((2 * F, C), jnp.bfloat16),
        hid=v(136, 128),
        hs0=v(M, 8, 128),
        hp0=v(M, 8, 128),
        hn0=v(M, 8, 128),
        hs1=v(8, 3 * C),
        hr1=v(8, 3 * C),
        hids=v(M, 136, 128),
        taps=v(Q, CP, GL),
        decay=v(Q, CP, GL),
        draw=v(CP, LEN),
        gdr=v(8 if ringed else F, F),
        gmid=v(C, 3 * F),
        glate=v(C, width),
    )
    for name, array in first.items():
        scratch[name] = v(*array.shape)
    scratch["esem"] = dma(len(first))
    for name in ("xt", "ogt", "u0", "prod", "insum", "gated", "w0", "w1", "w3", "h", "n2", "hg", "inner", "d1"):
        scratch[name] = v(C, R)
    for name in ("z", "z1", "z2", "conv", "dz", "d3"):
        scratch[name] = v(3 * C, R)
    for name in ("l1", "c1", "l2", "c2"):
        scratch[name] = v(LEN, 128)
    for name in ("kr", "km", "k4", "um", "u4", "ps", "ur", "ys", "yr", "inner_s", "vr", "ds", "dmain"):
        scratch[name] = v(Q, CP, R)
    for name in ("us", "vs", "zs"):
        scratch[name] = v(Q, CP, 2 * R)
    for name in ("s0", "r0", "s2", "r2", "s5", "r5", "s7", "r7"):
        scratch[name] = v(M, PW + 8, R)
    for name in ("s1", "r1", "s6", "r6"):
        scratch[name] = v(M, PW, R)
    for name in ("s3", "r3", "s4", "r4"):
        scratch[name] = v(M, FW, R)
    scratch.update(
        wsem=dma(5),
        osem=dma(13),
        mp_sent=dma(9),
        mp_here=dma(9),
        seq_sent=dma(4),
        seq_here=dma(4),
        halo_sent=dma(3),
        halo_here=dma(3),
    )
    if ringed:
        scratch.update(
            tdr=v(F, F),
            tmid=v(C, 3 * F),
            tlate=v(C, width),
            dm4_all=v(Q * F, R),
            act_all=v(Q, F // Q, R),
            act_sent=dma(1),
            act_here=dma(1),
            ring_ssem=dma(8, 2),
            ring_rsem=dma(8, 2 * Q - 2),
            x=v(F, F),
            a=v(F, F),
            moment=v(F, F),
            psem=dma(3),
            pul=v(C, 2 * F),
            oul=v(C, 2 * F),
            pdl=v(C, F),
            odl=v(C, F),
        )
        for name in ("xh", "xl", "ah", "al", "ph", "pl"):
            scratch[name] = pltpu.VMEM((F, F), jnp.bfloat16)
        for name, columns in (("mid", 3 * F), ("late", width)):
            cut = columns // 256 * 128
            for i, part in enumerate((cut, columns - cut)):
                scratch[f"far_{name}{i}"] = v(Q // 2, C // Q, part)
                scratch[f"near_{name}{i}"] = v(Q // 2 - 1, C // Q, part)
    vmem = pl.BlockSpec(memory_space=pltpu.VMEM)
    smem = pl.BlockSpec(memory_space=pltpu.SMEM)
    hbm = pl.BlockSpec(memory_space=pl.ANY)
    names = ["lengths", *in_hbm, *(f"{name}_hbm" for name in out_first), *out_hbm, *scratch]
    outs = pl.pallas_call(
        functools.partial(chain_kernel, dims, names),
        out_shape=[*out_first.values(), *out_hbm.values()],
        in_specs=[smem] + [hbm] * len(in_hbm),
        out_specs=[hbm] * (len(out_first) + len(out_hbm)),
        scratch_shapes=list(scratch.values()),
        compiler_params=pltpu.CompilerParams(
            collective_id=0, has_side_effects=True, vmem_limit_bytes=60 * 2**20
        ),
        name="chain",
    )(lengths, *in_hbm.values())
    block_out, input_grad, *rest = outs
    if ringed:
        return block_out, input_grad, dict(zip(out_hbm, rest))
    totals = lax.psum(rest, "seq")
    return block_out, input_grad, dict(zip(out_hbm, totals))


def adam(refs, gradient, rate):
    weights, first, second, first_out, second_out, weights_out, copy_out = refs
    first_new = beta_first * first[...] + (1.0 - beta_first) * gradient
    second_new = beta_second * second[...] + (1.0 - beta_second) * gradient * gradient
    corrected_first = first_new / (1.0 - beta_first**STEP)
    corrected_second = second_new / (1.0 - beta_second**STEP)
    old = weights[...]
    new = old - rate * (
        corrected_first / (jnp.sqrt(corrected_second) + adam_epsilon) + weight_decay * old
    )
    first_out[...] = first_new
    second_out[...] = second_new
    weights_out[...] = new
    copy_out[...] = new.astype(jnp.bfloat16)


def update_kernel(names, loaded, stored, ringed, *refs):
    k = types.SimpleNamespace(**dict(zip(names, refs, strict=True)))
    C, F = k.nsq.shape[1], k.ndr.shape[0]
    starts, width = late_columns(C)
    reads = {
        name: pltpu.make_async_copy(
            getattr(k, "hbm_" + name), getattr(k, name), k.read_sem.at[i]
        )
        for i, name in enumerate(loaded)
    }
    writes = {
        name: pltpu.make_async_copy(
            getattr(k, source), getattr(k, "hbm_" + name), k.write_sem.at[i]
        )
        for i, (name, source) in enumerate(stored.items())
    }
    for copy in reads.values():
        copy.start()

    def need(*wanted):
        for name in wanted:
            reads[name].wait()

    def put(*done):
        for name in done:
            writes[name].start()

    def renew(name):
        need("w" + name)
        weight = getattr(k, "w" + name)[...]
        new = weight - muon_scale(name, weight.shape) * getattr(k, "o" + name)[...]
        getattr(k, "n" + name)[...] = new
        getattr(k, "c" + name)[...] = new.astype(jnp.bfloat16)
        put("n" + name, "c" + name)

    def pass_on(name):
        need("n" + name)
        put("new_n" + name)
        getattr(k, "c" + name)[...] = getattr(k, "n" + name)[...].astype(jnp.bfloat16)
        put("c" + name)
        need("m" + name)
        put("new_m" + name)

    def small_ones():
        lead = starts[2] % 128
        turned = k.glate[:, starts[3] - 128 : starts[3]].T
        vector_grad = turned[lead : lead + 16][0 : 4 + 3 * KS]
        hidden = k.glate[:, starts[4] : width]
        hidden_grad = jnp.concatenate([hidden[0:EMB], hidden[8:136]], axis=0)
        for name, gradient, rate in (
            ("v", vector_grad, rate_vectors),
            ("h", hidden_grad, rate_hidden),
            ("f", k.glate[:, starts[3] : starts[4]], rate_output),
        ):
            adam(
                [getattr(k, name + kind) for kind in ("w", "1", "2", "1n", "2n", "n", "c")],
                gradient,
                rate,
            )

    need("glate", "psq", "pinl")
    for i in range(4):
        k.msq[i] = momentum_decay * k.psq[i] + k.glate[:, i * C : (i + 1) * C]
    k.minl[...] = momentum_decay * k.pinl[...] + k.glate[:, starts[1] : starts[2]]
    put("msq", "minl")
    moments = [k.msq.at[i] for i in range(4)] + [k.minl]
    results = [k.osq.at[i] for i in range(4)] + [k.oinl]
    if ringed:

        def tokens():
            need("block_out", "input_grad")
            put("new_block_out", "new_input_grad")

        beside = iter(
            [lambda: pass_on("dr"), lambda: pass_on("ul"), lambda: pass_on("dl"), small_ones, tokens]
        )
        small_schulz(moments, results, lambda: next(beside)())
    else:
        need("gmid", "gdr", "pul", "pdr", "pdl")
        for name, total in (
            ("ul", k.gmid[:, 0 : 2 * F]),
            ("dr", k.gdr[...]),
            ("dl", k.gmid[:, 2 * F : 3 * F]),
        ):
            moment = getattr(k, "m" + name)
            moment[...] = momentum_decay * getattr(k, "p" + name)[...] + total
            put("m" + name)
        k.x[...] = k.mdr[...] * unit_scale(k.mdr[...])
        small_schulz(moments + [k.mul, k.mdl], results + [k.oul, k.odl], lambda: None)
        large_schulz(k, idle)
        k.odr[...] = k.x[...]
        small_ones()
        for name in LARGE:
            renew(name)
    renew("sq")
    renew("inl")
    for copy in writes.values():
        copy.wait()


def run_update(chained, tokens, moments, weights, small):
    ringed = "out_odr" in chained
    shapes = {name: weight.shape for name, weight in zip(KINDS, weights)}
    arrays = dict(glate=chained["out_late"])
    for name, moment, weight in zip(KINDS, moments, weights):
        if ringed and name in LARGE:
            arrays["n" + name], arrays["m" + name] = chained["out_o" + name], chained["out_p" + name]
        else:
            arrays["p" + name], arrays["w" + name] = moment, weight
    if ringed:
        arrays |= tokens
    else:
        arrays.update(gmid=chained["out_mid"], gdr=chained["out_dr"])
    first = ["glate", "psq", "pinl", *(kind + name for name in LARGE for kind in "nm")]
    first = [name for name in first if name in arrays]
    loaded = first + [name for name in arrays if name not in first]
    in_hbm = {"hbm_" + name: array for name, array in arrays.items()}
    out_hbm, stored = {}, {}
    scratch = {name: pltpu.VMEM(arrays[name].shape, jnp.float32) for name in loaded}
    for name, shape in shapes.items():
        for kind, dtype in (("m", jnp.float32), ("n", jnp.float32), ("c", jnp.bfloat16)):
            through = ringed and name in LARGE and kind in "mn"
            target = ("new_" if through else "") + kind + name
            out_hbm["hbm_" + target] = jax.ShapeDtypeStruct(shape, dtype)
            stored[target] = kind + name
            scratch.setdefault(kind + name, pltpu.VMEM(shape, dtype))
        if not (ringed and name in LARGE):
            scratch["o" + name] = pltpu.VMEM(shape, jnp.float32)
    if ringed:
        for name, array in tokens.items():
            out_hbm["hbm_new_" + name] = jax.ShapeDtypeStruct(array.shape, jnp.float32)
            stored["new_" + name] = name
    in_vmem, out_vmem = {}, {}
    for name, (weight, first, second) in small.items():
        in_vmem[name + "w"], in_vmem[name + "1"], in_vmem[name + "2"] = weight, first, second
        for suffix in ("1n", "2n", "n"):
            out_vmem[name + suffix] = jax.ShapeDtypeStruct(weight.shape, jnp.float32)
        out_vmem[name + "c"] = jax.ShapeDtypeStruct(weight.shape, jnp.bfloat16)
    if not ringed:
        size = shapes["dr"]
        scratch.update({n: pltpu.VMEM(size, jnp.float32) for n in ("x", "a")})
        for name in ("xh", "xl", "ah", "al", "ph", "pl"):
            scratch[name] = pltpu.VMEM(size, jnp.bfloat16)
    scratch["read_sem"] = pltpu.SemaphoreType.DMA((len(loaded),))
    scratch["write_sem"] = pltpu.SemaphoreType.DMA((len(stored),))
    vmem = pl.BlockSpec(memory_space=pltpu.VMEM)
    hbm = pl.BlockSpec(memory_space=pl.ANY)
    names = [*in_hbm, *in_vmem, *out_hbm, *out_vmem, *scratch]
    results = pl.pallas_call(
        functools.partial(update_kernel, names, loaded, stored, ringed),
        out_shape=[*out_hbm.values(), *out_vmem.values()],
        in_specs=[hbm] * len(in_hbm) + [vmem] * len(in_vmem),
        out_specs=[hbm] * len(out_hbm) + [vmem] * len(out_vmem),
        scratch_shapes=list(scratch.values()),
        compiler_params=pltpu.CompilerParams(vmem_limit_bytes=60 * 2**20),
        name="update",
    )(*in_hbm.values(), *in_vmem.values())
    new = dict(zip([*out_hbm, *out_vmem], results))
    return {name.removeprefix("hbm_").removeprefix("new_"): value for name, value in new.items()}


def per_device(
    block_input,
    out_grad,
    lengths,
    square_factors,
    square_moment,
    input_left,
    input_left_moment,
    up_left,
    up_left_moment,
    down_right,
    down_right_moment,
    down_left,
    down_left_moment,
    vectors,
    vectors_first,
    vectors_second,
    filter_hidden,
    hidden_first,
    hidden_second,
    filter_out,
    filter_out_first,
    filter_out_second,
):
    weights = (square_factors[:, 0], input_left[0], up_left[0], down_right[0], down_left[0].T)
    moments = (
        square_moment[:, 0],
        input_left_moment[0],
        up_left_moment[0],
        down_right_moment[0],
        down_left_moment[0].T,
    )
    block_output, input_grad, chained = run_chain(
        block_input, out_grad, lengths, weights, moments, vectors, filter_hidden, filter_out.T
    )
    small = dict(
        v=(vectors, vectors_first, vectors_second),
        h=(filter_hidden, hidden_first, hidden_second),
        f=(filter_out.T, filter_out_first.T, filter_out_second.T),
    )
    tokens = dict(block_out=block_output, input_grad=input_grad)
    new = tokens | run_update(chained, tokens, moments, weights, small)
    return (
        new["block_out"].reshape(block_input.shape),
        new["input_grad"].reshape(block_input.shape),
        *[new[kind + "sq"][:, None] for kind in "mnc"],
        *[new[kind + name][None] for name in ("inl", "ul", "dr") for kind in "mnc"],
        *[new[kind + "dl"].T[None] for kind in "mnc"],
        *[new[name + suffix] for name in "vh" for suffix in ("1n", "2n", "n", "c")],
        *[new["f" + suffix].T for suffix in ("1n", "2n", "n", "c")],
    )


def solution(mesh):
    tokens = P(None, "seq", "mp")
    square = P(None, "mp", None, None)
    block = P("mp", None, None)
    row = P(None, "mp")
    return jax.shard_map(
        per_device,
        mesh=mesh,
        in_specs=(tokens, tokens, P(), square, square)
        + (block,) * 8
        + (row,) * 3
        + (P(),) * 3
        + (row,) * 3,
        out_specs=(tokens, tokens)
        + (square,) * 3
        + (block,) * 12
        + (row,) * 4
        + (P(),) * 4
        + (row,) * 4,
        check_vma=False,
    )
```

```python
import functools
import math
import types

import jax
import jax.numpy as jnp
import numpy as np
from jax import lax
from jax.experimental import pallas as pl
from jax.experimental.pallas import tpu as pltpu
from jax.sharding import PartitionSpec as P

EMB = 5
KS = 3
STEP = 10
SEQS = 2

HIGH = lax.Precision.HIGH
HIGHEST = lax.Precision.HIGHEST
MESH = pl.DeviceIdType.MESH
norm_epsilon = 1e-05
beta_first = 0.9
beta_second = 0.95
adam_epsilon = 1e-08
weight_decay = 0.01
rate_vectors = 0.2
rate_hidden = 0.05
rate_output = 0.05
muon_rate = 0.5
momentum_decay = 0.5
schulz_first = 3.4445
schulz_second = -4.775
schulz_third = 2.0315
filter_frequency = 10.0
gelu_scale = math.sqrt(2.0 / math.pi)
gelu_cubic = 0.044715


def contract(a, b, dim_a, dim_b, precision=HIGH):
    return lax.dot_general(
        a,
        b,
        (((dim_a,), (dim_b,)), ((), ())),
        precision=precision,
        preferred_element_type=jnp.float32,
    )


def nn(a, b, precision=HIGH):
    return contract(a, b, 1, 0, precision)


def nt(a, b, precision=HIGH):
    return contract(a, b, 1, 1, precision)


def tn(a, b, precision=HIGH):
    return contract(a, b, 0, 0, precision)


def spectrum_tables(group_len):
    rows = SEQS * group_len
    period = 2 * group_len
    time = np.arange(group_len)
    lags = np.arange(period)
    bins = np.arange(group_len)
    angle = 2.0 * np.pi * (np.outer(time, bins) % period) / period
    real = np.cos(angle)
    imag = -np.sin(angle)
    imag[:, 0] = (-1.0) ** time
    forward = np.zeros((rows, 2 * rows))
    for s in range(SEQS):
        part = slice(s * group_len, (s + 1) * group_len)
        forward[part, part] = real
        forward[part, rows + s * group_len : rows + (s + 1) * group_len] = imag
    of_taps = np.concatenate([real] * SEQS + [imag] * SEQS, axis=1)
    angle = 2.0 * np.pi * (np.outer(bins, lags) % period) / period
    back_real = 2.0 * np.cos(angle) / period
    back_real[0] = 1.0 / period
    back_imag = -2.0 * np.sin(angle) / period
    back_imag[0] = (-1.0) ** lags / period
    inverse = np.zeros((2 * rows, rows))
    for s in range(SEQS):
        part = slice(s * group_len, (s + 1) * group_len)
        inverse[part, part] = back_real[:, :group_len]
        inverse[rows + s * group_len : rows + (s + 1) * group_len, part] = back_imag[:, :group_len]
    window = np.concatenate([back_real] * SEQS + [back_imag] * SEQS, axis=0)
    return tuple(
        v.astype(np.float32)
        for v in (forward, of_taps, inverse, window[:, :group_len], window[:, group_len:])
    )


def feature_table(length):
    fraction = np.arange(length).astype(np.float32) / np.float32(length)
    angle = np.float32(2.0 * math.pi) * fraction
    wide = angle.astype(np.float64)
    twice = (np.float32(2.0) * angle).astype(np.float64)
    columns = [fraction, np.cos(wide), np.sin(wide), np.cos(twice), np.sin(twice)]
    table = np.zeros((length, 8), np.float32)
    for i, column in enumerate(columns):
        table[:, i] = column.astype(np.float32)
    return table


KINDS = ("sq", "inl", "ul", "dr", "dl")
LARGE = ("dr", "ul", "dl")


def muon_scale(name, shape):
    rows, cols = shape[-2:]
    if name == "dl":
        rows, cols = cols, rows
    return muon_rate * math.sqrt(max(rows, cols) / rows)


def late_columns(C):
    start = [0, 4 * C, 7 * C, 7 * C + C // 3, 7 * C + C // 3 + 128]
    return start, 7 * C + C // 3 + 256


def when(condition, body):
    if isinstance(condition, bool):
        if condition:
            body()
    else:
        pl.when(condition)(body)


SERVED = (
    "M", "L", "M", "", "L", "M", "", "L", "M", "L", "", "M", "L", "M", "LM",
)
SERVED_MIDDLE = ("", "L", "", "L", "L")
EARLY = ("block_in", "vec", "out_grad", "fo", "fh", "feat", "tfwd", "ttap", "tinv", "tw1", "tw2")


class Ring:
    def __init__(self, grad, total, far_slot, near_slot, ssem, rsem, rows, columns, way, place, count, ids):
        self.grad, self.total = grad, total
        self.far_slot, self.near_slot = far_slot, near_slot
        self.ssem, self.rsem = ssem, rsem
        self.stride, self.offset, self.height = rows
        self.columns = columns
        self.sign = 1 if way == 0 else -1
        self.place, self.count = place, count
        self.ahead, self.behind = ids if way == 0 else ids[::-1]
        self.gathers = far_slot is None

    def part(self, ref, ahead):
        chunk = lax.rem(self.place + self.sign * ahead + 4 * self.count, self.count)
        start = pl.multiple_of(chunk * self.stride + self.offset, 8)
        return ref.at[pl.ds(start, self.height), self.columns]

    def copy(self, source, target, index, to):
        return pltpu.make_async_remote_copy(
            src_ref=source,
            dst_ref=target,
            send_sem=self.ssem.at[int(index >= self.count - 1)],
            recv_sem=self.rsem.at[index],
            device_id=to,
            device_id_type=MESH,
        )

    def far_sum(self, i):
        n = self.count // 2
        return self.copy(self.part(self.grad, n - i), self.far_slot.at[i], i, self.ahead)

    def near_sum(self, i):
        n = self.count // 2
        source = self.part(self.grad, i - (n - 1))
        return self.copy(source, self.near_slot.at[i], n + i, self.behind)

    def far_total(self, i, hops=0):
        n = self.count // 2
        whole = self.part(self.total, i + hops)
        return self.copy(whole, whole, 2 * n - 1 + i, self.behind)

    def near_total(self, i, hops=0):
        n = self.count // 2
        whole = self.part(self.total, -i - hops)
        return self.copy(whole, whole, 3 * n - 1 + i, self.ahead)

    def begin(self):
        self.far_sum(0).start()
        self.near_sum(0).start()

    def begin_totals(self):
        self.far_total(0).start()
        self.near_total(0).start()

    def event(self, s):
        n = self.count // 2

        def add_far():
            mine = self.part(self.grad, n - 1 - s)
            mine[...] = mine[...] + self.far_slot[s]
            self.far_sum(s + 1).start()

        def add_near():
            mine = self.part(self.grad, s - (n - 2))
            mine[...] = mine[...] + self.near_slot[s]
            self.near_sum(s + 1).start()

        def turn():
            own = self.part(self.total, 0)
            mine = self.part(self.grad, 0)
            own[...] = mine[...] + self.far_slot[n - 1] + self.near_slot[n - 2]
            self.begin_totals()

        both = lambda p, q: p and q if isinstance(p, bool) else p & q
        i = s - n
        when(s < n, lambda: self.far_sum(s).wait_recv())
        when(s < n - 1, add_far)
        when(s < n - 1, lambda: self.near_sum(s).wait_recv())
        when(s < n - 2, add_near)
        when(s == n - 1, turn)
        when(both(s >= n, s < 2 * n), lambda: self.far_total(i, 1).wait_recv())
        when(both(s >= n, s < 2 * n - 1), lambda: self.far_total(i + 1).start())
        when(both(s >= n, s < 2 * n - 1), lambda: self.near_total(i, 1).wait_recv())
        when(both(s >= n, s < 2 * n - 2), lambda: self.near_total(i + 1).start())

    def end(self):
        part = self.total.at[pl.ds(0, self.height * (self.count - 1)), self.columns]
        for index in (self.count - 1,) if self.gathers else (0, self.count - 1):
            self.copy(part, part, index, self.ahead).wait_send()


def unit_scale(values):
    return 1.0 / (jnp.sqrt(jnp.sum(values * values)) + 1e-07)


def halves(values):
    high = values.astype(jnp.bfloat16)
    return high, (values - high.astype(jnp.float32)).astype(jnp.bfloat16)


def thrice(left, right, product):
    a, b = left
    c, d = right
    plain = lambda m, n: product(m, n, None)
    return plain(a, c) + plain(a, d) + plain(b, c)


def idle(product):
    pass


def large_schulz(k, between):
    size = k.x.shape[0]
    tile = 256
    strips = [
        (slice(i * tile, (i + 1) * tile), slice(0, (i + 1) * tile)) for i in range(size // tile)
    ]

    def keep(high, low, rows, columns, values):
        high[rows, columns], low[rows, columns] = halves(values)
        if rows.start:
            turned = values[:, 0 : rows.start].T
            high[0 : rows.start, rows], low[0 : rows.start, rows] = halves(turned)

    def newton_step(step):
        k.xh[...], k.xl[...] = halves(k.x[...])
        for i, (rows, columns) in enumerate(strips):
            gram = thrice((k.xh[rows], k.xl[rows]), (k.xh[columns], k.xl[columns]), nt)
            k.a[rows, columns] = gram
            keep(k.ah, k.al, rows, columns, gram)
        between(3 * step)
        for i, (rows, columns) in enumerate(strips):
            squared = thrice(
                (k.ah[rows], k.al[rows]), (k.ah[:, columns], k.al[:, columns]), nn
            )
            values = schulz_second * k.a[rows, columns] + schulz_third * squared
            keep(k.ph, k.pl, rows, columns, values)
        between(3 * step + 1)
        for i in range(2):
            rows = slice(i * size // 2, (i + 1) * size // 2)
            k.x[rows] = schulz_first * k.x[rows] + thrice(
                (k.ph[rows], k.pl[rows]), (k.xh[...], k.xl[...]), nn
            )
        between(3 * step + 2)

    if between is idle:
        pl.loop(0, 5)(newton_step)
    else:
        for step in range(5):
            newton_step(step)


def small_schulz(moments, results, between):
    current = [moment[...] * unit_scale(moment[...]) for moment in moments]
    for step in range(5):
        split = [halves(values) for values in current]
        grams = [thrice(one, one, nt) for one in split]
        split_grams = [halves(gram) for gram in grams]
        squared = [thrice(one, one, nn) for one in split_grams]
        factors = [
            halves(schulz_second * gram + schulz_third * square)
            for gram, square in zip(grams, squared)
        ]
        current = [
            schulz_first * values + thrice(factor, one, nn)
            for values, factor, one in zip(current, factors, split)
        ]
        between()
    for result, values in zip(results, current):
        result[...] = values


def chain_kernel(dims, names, *refs):
    k = types.SimpleNamespace(**dict(zip(names, refs, strict=True)))
    C, M, Q, GL, CP, cpd, F, LEN, ringed = dims
    R = SEQS * GL
    PW = C // M
    FW = F // M
    D = C * M
    r = lax.axis_index("seq")
    e = lax.axis_index("mp")
    nxt = lax.rem(r + 1, Q)
    prv = lax.rem(r + Q - 1, Q)
    sends = []

    def remote(src, dst, ssem, rsem, seq, mp):
        return pltpu.make_async_remote_copy(
            src_ref=src,
            dst_ref=dst,
            send_sem=ssem,
            recv_sem=rsem,
            device_id={"seq": seq, "mp": mp},
            device_id_type=MESH,
        )

    def swap_blocks(src, dst, phase, same=None):
        for d in range(1, M):
            to = lax.rem(e + d, M)
            source = src.at[to] if same is None else same
            remote(source, dst.at[e], k.mp_sent.at[phase], k.mp_here.at[phase], r, to).start()
        sends.append((dst.at[pl.ds(0, M - 1)], k.mp_sent.at[phase]))
        mine = src[pl.ds(e, 1)] if same is None else same[...].reshape((1,) + same.shape)
        dst[pl.ds(e, 1)] = mine

    def arrive(dst, rsem):
        remote(dst, dst, k.mp_sent.at[0], rsem, nxt, e).wait_recv()

    def blocks_arrive(dst, phase):
        arrive(dst.at[pl.ds(0, M - 1)], k.mp_here.at[phase])

    def swap_seq(src, dst, phase):
        for d in range(1, Q):
            to = lax.rem(r + d, Q)
            remote(
                src.at[to], dst.at[r], k.seq_sent.at[phase], k.seq_here.at[phase], to, e
            ).start()
        sends.append((dst.at[pl.ds(0, Q - 1)], k.seq_sent.at[phase]))
        dst[pl.ds(r, 1)] = src[pl.ds(r, 1)]

    def seq_arrive(dst, phase):
        arrive(dst.at[pl.ds(0, Q - 1)], k.seq_here.at[phase])

    def pieces(dst, values, width):
        for b in range(M):
            dst[b, 0:width] = values[width * b : width * (b + 1)]

    def joined(src, width):
        return jnp.concatenate([src[b, 0:width] for b in range(M)], axis=0)

    def extra(src):
        total = src[0, PW : PW + 8]
        for b in range(1, M):
            total = total + src[b, PW : PW + 8]
        return total[0:1]

    def by_channel(dst, values):
        if CP == cpd:
            dst[...] = values.reshape(Q, CP, values.shape[1])
        else:
            dst[...] = jnp.zeros(dst.shape, jnp.float32)
            for q in range(Q):
                dst[q, 0:cpd] = values[q * cpd : (q + 1) * cpd]

    def from_channels(src):
        if CP == cpd:
            return src[...].reshape(Q * CP, src.shape[2])
        return jnp.concatenate([src[q, 0:cpd] for q in range(Q)], axis=0)

    early = {}
    for i, name in enumerate(EARLY):
        early[name] = pltpu.make_async_copy(
            getattr(k, name + "_hbm"), getattr(k, name), k.esem.at[i]
        )
        early[name].start()
    copies = [
        pltpu.make_async_copy(src, dst, k.wsem.at[i])
        for i, (src, dst) in enumerate(
            (
                (k.sq_hbm, k.sq),
                (k.dl_hbm, k.dl),
                (k.inl_hbm, k.inl),
                (k.ul_hbm, k.ul),
                (k.dr_hbm, k.dr),
            )
        )
    ]
    if ringed:
        copies += [
            pltpu.make_async_copy(getattr(k, f"p{name}_hbm"), dst, k.psem.at[i])
            for i, (name, dst) in enumerate(
                (("dr", k.x), ("ul", k.pul), ("dl", k.pdl))
            )
        ]
    for copy in copies:
        copy.start()

    odd = lax.rem(r, 2)
    place = (1 - odd) * (r // 2) + odd * (Q - 1 - r // 2)

    def at_place(p):
        back = p // (Q // 2)
        return (1 - back) * 2 * p + back * (2 * (Q - 1 - p) + 1)

    ring_ids = tuple(
        {"seq": at_place(lax.rem(place + d, Q)), "mp": e} for d in (1, Q - 1)
    )

    barrier = pltpu.get_barrier_semaphore()
    partners = [(lax.rem(r + d, Q), e) for d in range(1, Q)]
    partners += [(r, lax.rem(e + d, M)) for d in range(1, M)]
    partners += [(s, lax.rem(e + d, M)) for s in (nxt, prv) for d in range(1, M)]
    for seq, mp in partners:
        pl.semaphore_signal(
            barrier, inc=1, device_id={"seq": seq, "mp": mp}, device_id_type=MESH
        )

    gather_rings, first_rings, other_rings, late_rings = [], [], [], []
    if ringed:

        def ring(grad, total, slots, rows, columns, way, index):
            return Ring(
                grad,
                total,
                *slots,
                k.ring_ssem.at[index],
                k.ring_rsem.at[index],
                rows,
                columns,
                way,
                place,
                Q,
                ring_ids,
            )

        tall, low = F // Q, C // Q
        for way in range(2):
            rows = (tall, way * (tall // 2), tall // 2)
            first_rings.append(ring(None, k.tdr, (None, None), rows, slice(0, F), way, way))
            rows = (F, way * (F // 2), F // 2)
            gather_rings.append(ring(None, k.dm4_all, (None, None), rows, slice(0, R), way, 6 + way))
        for rings, grad, total, slots, index in (
            (
                other_rings,
                k.gmid,
                k.tmid,
                ((k.far_mid0, k.near_mid0), (k.far_mid1, k.near_mid1)),
                2,
            ),
            (
                late_rings,
                k.glate,
                k.tlate,
                ((k.far_late0, k.near_late0), (k.far_late1, k.near_late1)),
                4,
            ),
        ):
            width = grad.shape[1]
            cut = width // 256 * 128
            for way, columns in enumerate((slice(0, cut), slice(cut, width))):
                rows = (low, 0, low)
                rings.append(ring(grad, total, slots[way], rows, columns, way, index + way))

    def go(rings, s):
        for one in rings:
            one.event(s)

    outs = []

    def put(source, target):
        copy = pltpu.make_async_copy(source, target, k.osem.at[len(outs)])
        copy.start()
        outs.append(copy)

    halves_done = [Q]

    def first_halves(count):
        if ringed:
            for _ in range(count):
                i = halves_done[0]
                first_rings[i % 2].event(i // 2)
                halves_done[0] += 1

    lane = lax.broadcasted_iota(jnp.int32, (1, R), 1)
    spot = lax.rem(lane, GL)
    first_bin = spot == 0
    flip = jnp.where(lax.rem(spot, 2) == 0, 1.0, -1.0).astype(jnp.float32)
    keep_bin = jnp.where(first_bin, 0.0, 1.0).astype(jnp.float32)
    length_of = jnp.where(lane < GL, k.lengths[0], k.lengths[1])
    position = r * GL + spot
    valid = (position < length_of).astype(jnp.float32)
    has_prev = (r > 0).astype(jnp.float32)
    has_next = (r < Q - 1).astype(jnp.float32)
    tail = spot >= GL - 2
    head = spot < 2
    halo_mask = jnp.where(tail, has_prev, jnp.where(head, has_next, 0.0))
    end_row = lax.broadcasted_iota(jnp.int32, (8, R), 0)
    end_lane = lax.rem(end_row, 4) // 2 * GL + lax.rem(end_row, 2)
    end_lane = end_lane + jnp.where(end_row < 4, 0, GL - 2)
    ends = (lax.broadcasted_iota(jnp.int32, (8, R), 1) == end_lane).astype(jnp.float32)

    early["block_in"].wait()
    early["vec"].wait()
    k.xt[...] = k.block_in[...].T
    k.vecp[...] = jnp.zeros(k.vecp.shape, jnp.float32)
    k.vecp[0 : 4 + 3 * KS] = k.vec[...]
    k.vt[...] = k.vecp[...].T

    def column(i):
        return k.vt[:, i : i + 1]

    xt = k.xt[...]
    u0 = xt * column(0)
    k.u0[...] = u0
    copies[0].wait()
    pieces(k.s0, tn(k.sq[0], u0), PW)
    squares = jnp.broadcast_to(jnp.sum(xt * xt, axis=0, keepdims=True), (8, R))
    for b in range(M):
        k.s0[b, PW : PW + 8] = squares
    pl.semaphore_wait(barrier, len(partners))
    swap_blocks(k.s0, k.r0, 0)
    for b in range(M):
        k.hs0[b, :, 0 : PW + 8] = nt(ends, k.s0[b], HIGHEST)
    halo_after, halo_before = [], []
    for d in range(M):
        to = lax.rem(e + d, M)
        for copies_to, dst, i, seq in ((halo_after, k.hp0, 0, nxt), (halo_before, k.hn0, 1, prv)):
            copies_to.append(
                remote(k.hs0.at[to], dst.at[e], k.halo_sent.at[i], k.halo_here.at[i], seq, to)
            )

    @pl.when(r < Q - 1)
    def _():
        for copy in halo_after:
            copy.start()

    @pl.when(r > 0)
    def _():
        for copy in halo_before:
            copy.start()

    @pl.when(r == 0)
    def _():
        k.hp0[...] = jnp.zeros(k.hp0.shape, jnp.float32)

    @pl.when(r == Q - 1)
    def _():
        k.hn0[...] = jnp.zeros(k.hn0.shape, jnp.float32)

    early["out_grad"].wait()
    k.ogt[...] = k.out_grad[...].T
    copies[1].wait()
    pieces(k.s4, tn(k.dl[...], k.ogt[...]), FW)
    swap_blocks(k.s4, k.r4, 4)
    by_channel(k.vtc, k.vt[...])
    early["fo"].wait()
    by_channel(k.foc, k.fo[...])
    copies[2].wait()

    blocks_arrive(k.r0, 0)

    @pl.when(r > 0)
    def _():
        arrive(k.hp0, k.halo_here.at[0])

    @pl.when(r < Q - 1)
    def _():
        arrive(k.hn0, k.halo_here.at[1])

    scale_one = lax.rsqrt(extra(k.r0) / D + norm_epsilon)
    w0 = joined(k.r0, PW)
    k.w0[...] = w0
    first_half = lax.broadcasted_iota(jnp.int32, (8, 128), 0) < 4
    spread = [
        tn(jnp.where(first_half, k.hn0[b], k.hp0[b]), ends, HIGHEST) for b in range(M)
    ]
    w0h = jnp.concatenate([one[0:PW] for one in spread], axis=0)
    squares = spread[0][PW : PW + 1]
    for b in range(1, M):
        squares = squares + spread[b][PW : PW + 1]
    both = tn(k.inl[...], jnp.concatenate([w0, w0h], axis=1))
    z = both[:, 0:R] * scale_one
    zh = both[:, R : 2 * R] * (lax.rsqrt(squares / D + norm_epsilon) * halo_mask)
    zh_far = pltpu.roll(zh, GL, 1)
    k.z[...] = z
    k.z1[...] = pltpu.roll(jnp.where(spot >= GL - 1, zh_far, z), 1, 1)
    k.z2[...] = pltpu.roll(jnp.where(tail, zh_far, z), 2, 1)
    for s in range(3):
        part = slice(s * C, (s + 1) * C)
        k.conv[part] = (
            column(4 + KS * s) * k.z[part]
            + column(5 + KS * s) * k.z1[part]
            + column(6 + KS * s) * k.z2[part]
        )
    product = k.conv[0:C] * k.conv[2 * C : 3 * C] * valid
    k.prod[...] = product
    by_channel(k.ps, product)
    swap_seq(k.ps, k.ur, 0)

    for name in EARLY[4:]:
        early[name].wait()
    pre = filter_frequency * nn(k.feat[...], k.fh[0:8], HIGHEST)
    k.l1[...] = jnp.sin(pre)
    k.c1[...] = filter_frequency * jnp.cos(pre)
    if ringed:
        blocks_arrive(k.r4, 4)
        k.dm4_all[pl.ds(pl.multiple_of(place * F, F), F)] = k.r4[...].reshape(F, R)
        gather_rings[0].begin_totals()
    pre = filter_frequency * nn(k.l1[...], k.fh[EMB : EMB + 128], HIGHEST)
    k.l2[...] = jnp.sin(pre)
    k.c2[...] = filter_frequency * jnp.cos(pre)
    foc = k.foc[pl.ds(r, 1)].reshape(CP, 128)
    vtc = k.vtc[pl.ds(r, 1)].reshape(CP, 128)
    rate = vtc[:, 2:3]
    skip_channel = vtc[:, 3:4]
    shaped = nt(foc, k.l2[...], HIGHEST)
    part_lane = lax.broadcasted_iota(jnp.int32, (1, GL), 1)
    for q in range(Q):
        fraction = (part_lane + q * GL).astype(jnp.float32) / LEN
        decay = jnp.exp(-fraction * rate) * (LEN ** (-0.5))
        k.decay[q] = decay
        k.taps[q] = shaped[:, q * GL : (q + 1) * GL] * decay
    spectrum = nn(k.taps[...].reshape(Q * CP, GL), k.ttap[...]).reshape(Q, CP, 2 * R)
    for q in range(Q):
        real = spectrum[q, :, 0:R]
        imag = spectrum[q, :, R : 2 * R]
        if q > 0:
            real = real + flip * spectrum[q - 1, :, 0:R]
            imag = imag + flip * spectrum[q - 1, :, R : 2 * R]
        k.kr[q] = real
        k.km[q] = imag * keep_bin
        k.k4[q] = jnp.where(first_bin, imag, real)

    def total_pairs(count, first, term):
        zero = jnp.zeros((CP, R), jnp.float32)
        if Q <= 8:
            real, imag = zero, zero
            for i in range(count):
                add_real, add_imag = term(first + i)
                real, imag = real + add_real, imag + add_imag
            return real, imag

        def body(i, kept):
            add_real, add_imag = term(first + i)
            return (kept[0] + add_real, kept[1] + add_imag)

        return lax.fori_loop(0, count, body, (zero, zero))

    def each_block(body):
        if Q <= 8:
            for q in range(Q):
                body(q)
        else:
            pl.loop(0, Q)(body)

    seq_arrive(k.ur, 0)
    k.us[...] = nn(k.ur[...].reshape(Q * CP, R), k.tfwd[...]).reshape(Q, CP, 2 * R)

    def forward_block(p):
        def term(q):
            real = k.us[q, :, 0:R]
            imag = k.us[q, :, R : 2 * R]
            lag = p - q
            return (
                k.kr[lag] * real - k.km[lag] * imag,
                k.km[lag] * real + k.k4[lag] * imag,
            )

        real, imag = total_pairs(p + 1, 0, term)
        k.zs[p, :, 0:R] = real
        k.zs[p, :, R : 2 * R] = imag

    each_block(forward_block)
    k.ys[...] = nn(k.zs[...].reshape(Q * CP, 2 * R), k.tinv[...]).reshape(Q, CP, R)
    swap_seq(k.ys, k.yr, 1)
    if ringed:
        gather_rings[1].begin_totals()
    for q in range(Q):
        real = k.us[q, :, 0:R]
        imag = k.us[q, :, R : 2 * R]
        k.um[q] = imag * keep_bin
        k.u4[q] = jnp.where(first_bin, imag, real)

    copies[3].wait()
    k.ult_h[...], k.ult_l[...] = halves(k.ul[...].T)
    if ringed:
        copies[4].wait()
        k.ph[...], k.pl[...] = halves(k.dr[...].T)
    seq_arrive(k.yr, 1)
    inner_sum = from_channels(k.yr) + column(3) * k.prod[...]
    k.insum[...] = inner_sum
    gated = k.conv[C : 2 * C] * inner_sum
    k.gated[...] = gated
    pieces(k.s1, tn(k.sq[1], gated), PW)
    swap_blocks(k.s1, k.r1, 1)

    if ringed:
        gather_rings[0].event(Q // 2 + 0)
    if not ringed:
        copies[4].wait()
    if not ringed:
        blocks_arrive(k.r4, 4)
    k.dact[...] = nn(k.dr[...], k.r4[...].reshape(F, R))

    if ringed:
        gather_rings[1].event(Q // 2 + 0)
    blocks_arrive(k.r1, 1)
    w1 = k.r1[...].reshape(C, R)
    k.w1[...] = w1
    h = k.xt[...] + tn(k.sq[2], w1)
    k.h[...] = h
    u3 = h * column(1)
    pieces(k.s2, tn(k.sq[3], u3), PW)
    squares = jnp.broadcast_to(jnp.sum(h * h, axis=0, keepdims=True), (8, R))
    for b in range(M):
        k.s2[b, PW : PW + 8] = squares
    swap_blocks(k.s2, k.r2, 2)

    if ringed:
        gather_rings[0].event(Q // 2 + 1)
    blocks_arrive(k.r2, 2)
    scale_two = lax.rsqrt(extra(k.r2) / D + norm_epsilon)
    k.n2[...] = k.h[...] * scale_two
    w3 = joined(k.r2, PW)
    k.w3[...] = w3
    k.gu[...] = thrice((k.ult_h[...], k.ult_l[...]), halves(w3), nn) * scale_two
    gate = k.gu[0:F]
    up = k.gu[F : 2 * F]
    bend = jnp.tanh(gelu_scale * (gate + gelu_cubic * gate * gate * gate))
    gelu = 0.5 * gate * (1.0 + bend)
    slope = 0.5 * (1.0 + bend) + 0.5 * gate * (1.0 - bend * bend) * gelu_scale * (
        1.0 + 3.0 * gelu_cubic * gate * gate
    )
    dact = k.dact[...]
    k.act[...] = gelu * up
    k.dgu[0:F] = dact * up * slope
    k.dgu[F : 2 * F] = dact * gelu
    back = nn(k.ul[...], k.dgu[...])
    pieces(k.s5, back, PW)
    inner = jnp.broadcast_to(jnp.sum(back * k.w3[...], axis=0, keepdims=True), (8, R))
    for b in range(M):
        k.s5[b, PW : PW + 8] = inner
    swap_blocks(k.s5, k.r5, 5)
    if ringed:
        tall = F // Q

        def act_rows(p):
            return k.act.at[pl.ds(pl.multiple_of(p * tall, tall), tall)]

        for d in range(1, Q):
            p = lax.rem(place + d, Q)
            remote(
                act_rows(p),
                k.act_all.at[place],
                k.act_sent.at[0],
                k.act_here.at[0],
                at_place(p),
                e,
            ).start()
        sends.append((k.act_all.at[pl.ds(0, Q - 1)], k.act_sent.at[0]))
        k.act_all[pl.ds(place, 1)] = act_rows(place)[...].reshape(1, tall, R)
        gather_rings[1].event(Q // 2 + 1)
    else:
        k.gdr[...] = nt(k.act[...], k.r4[...].reshape(F, R))
    if ringed:
        pieces(k.s3, thrice((k.ph[...], k.pl[...]), halves(k.act[...]), nn), FW)
    else:
        pieces(k.s3, tn(k.dr[...], k.act[...]), FW)
    swap_blocks(k.s3, k.r3, 3)

    k.gmid[:, 0 : 2 * F] = nt(k.w3[...] * scale_two, k.dgu[...])
    if ringed:
        gather_rings[0].event(Q // 2 + 2)
    blocks_arrive(k.r5, 5)
    back = joined(k.r5, PW)
    inner = extra(k.r5)
    grad_two = nn(k.sq[3], back)
    hidden_grad = (
        k.ogt[...]
        + scale_two * (grad_two * column(1))
        - k.h[...] * (scale_two * scale_two * scale_two * inner / D)
    )
    k.hg[...] = hidden_grad
    pieces(k.s6, nn(k.sq[2], hidden_grad), PW)
    swap_blocks(k.s6, k.r6, 6)
    k.glate[:, 3 * C : 4 * C] = nt(k.n2[...] * column(1), back)
    gain_two = jnp.sum(grad_two * k.n2[...], axis=1, keepdims=True)
    k.glate[:, 2 * C : 3 * C] = nt(k.w1[...], k.hg[...])

    blocks_arrive(k.r6, 6)
    back = k.r6[...].reshape(C, R)
    gated_grad = nn(k.sq[1], back)
    inner_grad = gated_grad * k.conv[C : 2 * C]
    k.inner[...] = inner_grad
    k.d1[...] = gated_grad * k.insum[...]
    by_channel(k.inner_s, inner_grad)
    swap_seq(k.inner_s, k.vr, 2)
    k.glate[:, C : 2 * C] = nt(k.gated[...], back)
    skip_total = jnp.sum(inner_grad * k.prod[...], axis=1, keepdims=True)

    if ringed:
        gather_rings[1].event(Q // 2 + 2)
        for one in gather_rings:
            one.event(Q // 2 + 3)
    seq_arrive(k.vr, 2)
    k.vs[...] = nn(k.vr[...].reshape(Q * CP, R), k.tfwd[...]).reshape(Q, CP, 2 * R)

    def back_block(q):
        def term(p):
            real = k.vs[p, :, 0:R]
            imag = k.vs[p, :, R : 2 * R]
            lag = p - q
            return (
                k.kr[lag] * real + k.km[lag] * imag,
                k.k4[lag] * imag - k.km[lag] * real,
            )

        real, imag = total_pairs(Q - q, q, term)
        k.zs[q, :, 0:R] = real
        k.zs[q, :, R : 2 * R] = imag

    each_block(back_block)
    k.ds[...] = (
        nn(k.zs[...].reshape(Q * CP, 2 * R), k.tinv[...]).reshape(Q, CP, R)
        + skip_channel[None] * k.vr[...]
    )
    swap_seq(k.ds, k.dmain, 3)
    if ringed:
        arrive(k.act_all.at[pl.ds(0, Q - 1)], k.act_here.at[0])
        acts = jnp.concatenate([k.act_all[p] for p in range(Q)], axis=1)
        backs = jnp.concatenate([k.dm4_all[p * F : (p + 1) * F] for p in range(Q)], axis=1)
        k.tdr[pl.ds(pl.multiple_of(place * tall, tall), tall)] = nt(acts, backs)
        for one in first_rings:
            one.begin_totals()
    first_halves(1)
    def lag_block(j):
        def term(p):
            real = k.vs[p, :, 0:R]
            imag = k.vs[p, :, R : 2 * R]
            q = p - j
            return (
                k.us[q, :, 0:R] * real + k.um[q] * imag,
                k.u4[q] * imag - k.um[q] * real,
            )

        real, imag = total_pairs(Q - j, j, term)
        k.zs[j, :, 0:R] = real
        k.zs[j, :, R : 2 * R] = imag

    each_block(lag_block)
    cross = k.zs[...].reshape(Q * CP, 2 * R)
    near = nn(cross, k.tw1[...]).reshape(Q, CP, GL)
    far = nn(cross, k.tw2[...]).reshape(Q, CP, GL)
    decay_total = jnp.zeros((CP, 1), jnp.float32)
    for q in range(Q):
        grad = near[q]
        if q < Q - 1:
            grad = grad + far[q + 1]
        fraction = (part_lane + q * GL).astype(jnp.float32) / LEN
        decay_total = decay_total - jnp.sum(
            grad * k.taps[q] * fraction, axis=1, keepdims=True
        )
        k.draw[:, q * GL : (q + 1) * GL] = grad * k.decay[q]
    raw = k.draw[...]
    k.gfo[...] = jnp.zeros(k.gfo.shape, jnp.float32)
    k.gdec[...] = jnp.zeros(k.gdec.shape, jnp.float32)
    k.gfo[pl.ds(r, 1)] = nn(raw, k.l2[...]).reshape(1, CP, 128)
    k.gdec[pl.ds(r, 1)] = jnp.broadcast_to(decay_total, (CP, 128)).reshape(1, CP, 128)
    first_halves(1)
    blocks_arrive(k.r3, 3)
    w4 = k.r3[...].reshape(F, R)
    k.block_out[...] = (k.h[...] + nn(k.dl[...], w4)).T
    put(k.block_out, k.block_out_hbm)
    k.gmid[:, 2 * F : 3 * F] = nt(k.ogt[...], w4)
    back = tn(raw, foc) * k.c2[...]
    k.hid[8:136] = tn(k.l1[...], back)
    back = nt(back, k.fh[EMB : EMB + 128]) * k.c1[...]
    k.hid[0:8] = tn(k.feat[...], back)
    swap_blocks(None, k.hids, 8, k.hid)


    first_halves(1)
    seq_arrive(k.dmain, 3)
    product_grad = from_channels(k.dmain) * valid
    k.d3[0:C] = product_grad * k.conv[2 * C : 3 * C]
    k.d3[C : 2 * C] = k.d1[...]
    k.d3[2 * C : 3 * C] = product_grad * k.conv[0:C]
    k.hs1[...] = nt(ends, k.d3[...], HIGHEST)
    edge = remote(k.hs1, k.hr1, k.halo_sent.at[2], k.halo_here.at[2], prv, e)

    @pl.when(r > 0)
    def _():
        edge.start()

    @pl.when(r == Q - 1)
    def _():
        k.hr1[...] = jnp.zeros(k.hr1.shape, jnp.float32)

    first_halves(1)

    @pl.when(r < Q - 1)
    def _():
        arrive(k.hr1, k.halo_here.at[2])

    for one in other_rings:
        one.begin()
    following = pltpu.roll(tn(k.hr1[...], ends, HIGHEST), GL, 1)
    tap_totals = []
    for s in range(3):
        part = slice(s * C, (s + 1) * C)
        grad = k.d3[part]
        one = pltpu.roll(jnp.where(spot == 0, following[part], grad), R - 1, 1)
        two = pltpu.roll(jnp.where(head, following[part], grad), R - 2, 1)
        k.dz[part] = (
            column(4 + KS * s) * grad + column(5 + KS * s) * one + column(6 + KS * s) * two
        )
        for shifted in (k.z, k.z1, k.z2):
            tap_totals.append(jnp.sum(grad * shifted[part], axis=1, keepdims=True))
    back = nn(k.inl[...], k.dz[...])
    pieces(k.s7, back, PW)
    inner = jnp.broadcast_to(jnp.sum(back * k.w0[...], axis=0, keepdims=True), (8, R))
    for b in range(M):
        k.s7[b, PW : PW + 8] = inner
    swap_blocks(k.s7, k.r7, 7)
    k.glate[:, 4 * C : 7 * C] = nt(k.w0[...] * scale_one, k.dz[...])

    first_halves(1)
    blocks_arrive(k.r7, 7)
    back = joined(k.r7, PW)
    inner = extra(k.r7)
    grad_one = nn(k.sq[0], back)
    xt = k.xt[...]
    k.input_grad[...] = (
        k.hg[...]
        + scale_one * (grad_one * column(0))
        - xt * (scale_one * scale_one * scale_one * inner / D)
    ).T
    put(k.input_grad, k.input_grad_hbm)
    k.glate[:, 0:C] = nt(k.u0[...] * scale_one, back)
    gain_one = jnp.sum(grad_one * xt * scale_one, axis=1, keepdims=True)
    starts, width = late_columns(C)
    slot = lax.broadcasted_iota(jnp.int32, (1, 16), 1)
    rows = {0: gain_one, 1: gain_two, 2: from_channels(k.gdec)[:, 0:1], 3: skip_total}
    rows.update({4 + i: total for i, total in enumerate(tap_totals)})
    stacked = jnp.zeros((C, 16), jnp.float32)
    for i, total in rows.items():
        stacked = jnp.where(slot == i, total, stacked)
    k.glate[:, starts[2] : starts[3]] = jnp.zeros((C, starts[3] - starts[2]), jnp.float32)
    k.glate[:, starts[2] : starts[2] + 16] = stacked
    k.glate[:, starts[3] : starts[4]] = from_channels(k.gfo)
    first_halves(1)
    blocks_arrive(k.hids, 8)
    hidden_sum = k.hids[0]
    for b in range(1, M):
        hidden_sum = hidden_sum + k.hids[b]
    k.glate[0:136, starts[4] : width] = hidden_sum
    k.glate[136:C, starts[4] : width] = jnp.zeros((C - 136, 128), jnp.float32)

    if ringed:
        first_halves(max(0, 2 * Q - 2 - halves_done[0]))
        for one in late_rings:
            one.begin()
        go(other_rings, 0)
        first_halves(2 * Q - halves_done[0])
        for copy in copies[5:]:
            copy.wait()
        moment = momentum_decay * k.x[...] + k.tdr[...]
        k.moment[...] = moment
        put(k.moment, k.out_pdr)
        k.x[...] = moment * unit_scale(moment)
        mid_turns, late_turns = iter(range(1, Q)), iter(range(Q))

        def turn(rings, turns):
            s = next(turns, None)
            if s is not None:
                go(rings, s)

        def serve(letters):
            for letter in letters:
                if letter == "M":
                    turn(other_rings, mid_turns)
                else:
                    turn(late_rings, late_turns)

        def between(product):
            serve(SERVED[product])

        def renew(name, weight, result, target):
            result[...] = weight[...] - muon_scale(name, weight.shape) * result[...]
            put(result, target)

        large_schulz(k, between)
        renew("dr", k.dr, k.x, k.out_odr)
        for s in mid_turns:
            go(other_rings, s)
        steps = iter(SERVED_MIDDLE)
        for moment, columns in ((k.pul, slice(0, 2 * F)), (k.pdl, slice(2 * F, 3 * F))):
            moment[...] = momentum_decay * moment[...] + k.tmid[:, columns]
        put(k.pul, k.out_pul)
        put(k.pdl, k.out_pdl)
        small_schulz((k.pul, k.pdl), (k.oul, k.odl), lambda: serve(next(steps)))
        renew("ul", k.ul, k.oul, k.out_oul)
        renew("dl", k.dl, k.odl, k.out_odl)
        for s in late_turns:
            go(late_rings, s)
        put(k.tlate, k.out_late)
        for one in gather_rings + first_rings + other_rings + late_rings:
            one.end()
    else:
        put(k.gdr, k.out_dr)
        put(k.gmid, k.out_mid)
        put(k.glate, k.out_late)
    for copy in outs:
        copy.wait()
    for ref, sem in sends:
        remote(ref, ref, sem, k.mp_here.at[0], nxt, e).wait_send()

    @pl.when(r < Q - 1)
    def _():
        remote(k.hs0, k.hp0, k.halo_sent.at[0], k.halo_here.at[0], nxt, e).wait_send()

    @pl.when(r > 0)
    def _():
        remote(k.hs0, k.hn0, k.halo_sent.at[1], k.halo_here.at[1], prv, e).wait_send()
        edge.wait_send()


def run_chain(x, og, lengths, weights, moments, vectors, fh, fo):
    M, Q = lax.axis_size("mp"), lax.axis_size("seq")
    sq, inl, ul, dr, dl = weights
    _, GL, C = x.shape
    R = SEQS * GL
    F = dr.shape[0]
    LEN = GL * Q
    cpd = C // Q
    CP = -(-cpd // 8) * 8
    PW, FW = C // M, F // M
    ringed = cpd % 8 == 0 and F % (32 * Q) == 0
    dims = (C, M, Q, GL, CP, cpd, F, LEN, ringed)
    tables = spectrum_tables(GL)
    feat = feature_table(LEN)
    width = late_columns(C)[1]
    sds = lambda *shape: jax.ShapeDtypeStruct(shape, jnp.float32)
    v = lambda *shape: pltpu.VMEM(shape, jnp.float32)
    dma = lambda *shape: pltpu.SemaphoreType.DMA(shape)
    first = dict(
        block_in=x.reshape(R, C),
        out_grad=og.reshape(R, C),
        vec=vectors,
        fh=fh,
        fo=fo,
        feat=feat,
        **dict(zip(("tfwd", "ttap", "tinv", "tw1", "tw2"), tables)),
    )
    in_hbm = {name + "_hbm": array for name, array in first.items()}
    in_hbm.update(sq_hbm=sq, inl_hbm=inl, ul_hbm=ul, dr_hbm=dr, dl_hbm=dl)
    if ringed:
        in_hbm.update((f"p{n}_hbm", p) for n, p in zip(KINDS, moments) if n in LARGE)
    out_first = dict(block_out=sds(R, C), input_grad=sds(R, C))
    out_hbm = dict(out_dr=sds(F, F), out_mid=sds(C, 3 * F), out_late=sds(C, width))
    if ringed:
        out_hbm = {
            f"out_{x}{n}": sds(*w.shape) for x in "po" for n, w in zip(KINDS, weights) if n in LARGE
        }
        out_hbm["out_late"] = sds(C, width)
    scratch = dict(
        sq=v(4, C, C),
        inl=v(C, 3 * C),
        ul=v(C, 2 * F),
        dr=v(F, F),
        dl=v(C, F),
        vecp=v(128, C),
        vt=v(C, 128),
        vtc=v(Q, CP, 128),
        foc=v(Q, CP, 128),
        gfo=v(Q, CP, 128),
        gdec=v(Q, CP, 128),
        gu=v(2 * F, R),
        act=v(F, R),
        dact=v(F, R),
        dgu=v(2 * F, R),
        block_out=v(R, C),
        input_grad=v(R, C),
        ult_h=pltpu.VMEM((2 * F, C), jnp.bfloat16),
        ult_l=pltpu.VMEM((2 * F, C), jnp.bfloat16),
        hid=v(136, 128),
        hs0=v(M, 8, 128),
        hp0=v(M, 8, 128),
        hn0=v(M, 8, 128),
        hs1=v(8, 3 * C),
        hr1=v(8, 3 * C),
        hids=v(M, 136, 128),
        taps=v(Q, CP, GL),
        decay=v(Q, CP, GL),
        draw=v(CP, LEN),
        gdr=v(8 if ringed else F, F),
        gmid=v(C, 3 * F),
        glate=v(C, width),
    )
    for name, array in first.items():
        scratch[name] = v(*array.shape)
    scratch["esem"] = dma(len(first))
    for name in ("xt", "ogt", "u0", "prod", "insum", "gated", "w0", "w1", "w3", "h", "n2", "hg", "inner", "d1"):
        scratch[name] = v(C, R)
    for name in ("z", "z1", "z2", "conv", "dz", "d3"):
        scratch[name] = v(3 * C, R)
    for name in ("l1", "c1", "l2", "c2"):
        scratch[name] = v(LEN, 128)
    for name in ("kr", "km", "k4", "um", "u4", "ps", "ur", "ys", "yr", "inner_s", "vr", "ds", "dmain"):
        scratch[name] = v(Q, CP, R)
    for name in ("us", "vs", "zs"):
        scratch[name] = v(Q, CP, 2 * R)
    for name in ("s0", "r0", "s2", "r2", "s5", "r5", "s7", "r7"):
        scratch[name] = v(M, PW + 8, R)
    for name in ("s1", "r1", "s6", "r6"):
        scratch[name] = v(M, PW, R)
    for name in ("s3", "r3", "s4", "r4"):
        scratch[name] = v(M, FW, R)
    scratch.update(
        wsem=dma(5),
        osem=dma(13),
        mp_sent=dma(9),
        mp_here=dma(9),
        seq_sent=dma(4),
        seq_here=dma(4),
        halo_sent=dma(3),
        halo_here=dma(3),
    )
    if ringed:
        scratch.update(
            tdr=v(F, F),
            tmid=v(C, 3 * F),
            tlate=v(C, width),
            dm4_all=v(Q * F, R),
            act_all=v(Q, F // Q, R),
            act_sent=dma(1),
            act_here=dma(1),
            ring_ssem=dma(8, 2),
            ring_rsem=dma(8, 2 * Q - 2),
            x=v(F, F),
            a=v(F, F),
            moment=v(F, F),
            psem=dma(3),
            pul=v(C, 2 * F),
            oul=v(C, 2 * F),
            pdl=v(C, F),
            odl=v(C, F),
        )
        for name in ("xh", "xl", "ah", "al", "ph", "pl"):
            scratch[name] = pltpu.VMEM((F, F), jnp.bfloat16)
        for name, columns in (("mid", 3 * F), ("late", width)):
            cut = columns // 256 * 128
            for i, part in enumerate((cut, columns - cut)):
                scratch[f"far_{name}{i}"] = v(Q // 2, C // Q, part)
                scratch[f"near_{name}{i}"] = v(Q // 2 - 1, C // Q, part)
    vmem = pl.BlockSpec(memory_space=pltpu.VMEM)
    smem = pl.BlockSpec(memory_space=pltpu.SMEM)
    hbm = pl.BlockSpec(memory_space=pl.ANY)
    names = ["lengths", *in_hbm, *(f"{name}_hbm" for name in out_first), *out_hbm, *scratch]
    outs = pl.pallas_call(
        functools.partial(chain_kernel, dims, names),
        out_shape=[*out_first.values(), *out_hbm.values()],
        in_specs=[smem] + [hbm] * len(in_hbm),
        out_specs=[hbm] * (len(out_first) + len(out_hbm)),
        scratch_shapes=list(scratch.values()),
        compiler_params=pltpu.CompilerParams(
            collective_id=0, has_side_effects=True, vmem_limit_bytes=60 * 2**20
        ),
        name="chain",
    )(lengths, *in_hbm.values())
    block_out, input_grad, *rest = outs
    if ringed:
        return block_out, input_grad, dict(zip(out_hbm, rest))
    totals = lax.psum(rest, "seq")
    return block_out, input_grad, dict(zip(out_hbm, totals))


def adam(refs, gradient, rate):
    weights, first, second, first_out, second_out, weights_out, copy_out = refs
    first_new = beta_first * first[...] + (1.0 - beta_first) * gradient
    second_new = beta_second * second[...] + (1.0 - beta_second) * gradient * gradient
    corrected_first = first_new / (1.0 - beta_first**STEP)
    corrected_second = second_new / (1.0 - beta_second**STEP)
    old = weights[...]
    new = old - rate * (
        corrected_first / (jnp.sqrt(corrected_second) + adam_epsilon) + weight_decay * old
    )
    first_out[...] = first_new
    second_out[...] = second_new
    weights_out[...] = new
    copy_out[...] = new.astype(jnp.bfloat16)


def update_kernel(names, loaded, stored, ringed, *refs):
    k = types.SimpleNamespace(**dict(zip(names, refs, strict=True)))
    C, F = k.nsq.shape[1], k.ndr.shape[0]
    starts, width = late_columns(C)
    reads = {
        name: pltpu.make_async_copy(
            getattr(k, "hbm_" + name), getattr(k, name), k.read_sem.at[i]
        )
        for i, name in enumerate(loaded)
    }
    writes = {
        name: pltpu.make_async_copy(
            getattr(k, source), getattr(k, "hbm_" + name), k.write_sem.at[i]
        )
        for i, (name, source) in enumerate(stored.items())
    }
    for copy in reads.values():
        copy.start()

    def need(*wanted):
        for name in wanted:
            reads[name].wait()

    def put(*done):
        for name in done:
            writes[name].start()

    def renew(name):
        need("w" + name)
        weight = getattr(k, "w" + name)[...]
        new = weight - muon_scale(name, weight.shape) * getattr(k, "o" + name)[...]
        getattr(k, "n" + name)[...] = new
        getattr(k, "c" + name)[...] = new.astype(jnp.bfloat16)
        put("n" + name, "c" + name)

    def pass_on(name):
        need("n" + name)
        put("new_n" + name)
        getattr(k, "c" + name)[...] = getattr(k, "n" + name)[...].astype(jnp.bfloat16)
        put("c" + name)
        need("m" + name)
        put("new_m" + name)

    def small_ones():
        lead = starts[2] % 128
        turned = k.glate[:, starts[3] - 128 : starts[3]].T
        vector_grad = turned[lead : lead + 16][0 : 4 + 3 * KS]
        hidden = k.glate[:, starts[4] : width]
        hidden_grad = jnp.concatenate([hidden[0:EMB], hidden[8:136]], axis=0)
        for name, gradient, rate in (
            ("v", vector_grad, rate_vectors),
            ("h", hidden_grad, rate_hidden),
            ("f", k.glate[:, starts[3] : starts[4]], rate_output),
        ):
            adam(
                [getattr(k, name + kind) for kind in ("w", "1", "2", "1n", "2n", "n", "c")],
                gradient,
                rate,
            )

    need("glate", "psq", "pinl")
    for i in range(4):
        k.msq[i] = momentum_decay * k.psq[i] + k.glate[:, i * C : (i + 1) * C]
    k.minl[...] = momentum_decay * k.pinl[...] + k.glate[:, starts[1] : starts[2]]
    put("msq", "minl")
    moments = [k.msq.at[i] for i in range(4)] + [k.minl]
    results = [k.osq.at[i] for i in range(4)] + [k.oinl]
    if ringed:

        def tokens():
            need("block_out", "input_grad")
            put("new_block_out", "new_input_grad")

        beside = iter(
            [lambda: pass_on("dr"), lambda: pass_on("ul"), lambda: pass_on("dl"), small_ones, tokens]
        )
        small_schulz(moments, results, lambda: next(beside)())
    else:
        need("gmid", "gdr", "pul", "pdr", "pdl")
        for name, total in (
            ("ul", k.gmid[:, 0 : 2 * F]),
            ("dr", k.gdr[...]),
            ("dl", k.gmid[:, 2 * F : 3 * F]),
        ):
            moment = getattr(k, "m" + name)
            moment[...] = momentum_decay * getattr(k, "p" + name)[...] + total
            put("m" + name)
        k.x[...] = k.mdr[...] * unit_scale(k.mdr[...])
        small_schulz(moments + [k.mul, k.mdl], results + [k.oul, k.odl], lambda: None)
        large_schulz(k, idle)
        k.odr[...] = k.x[...]
        small_ones()
        for name in LARGE:
            renew(name)
    renew("sq")
    renew("inl")
    for copy in writes.values():
        copy.wait()


def run_update(chained, tokens, moments, weights, small):
    ringed = "out_odr" in chained
    shapes = {name: weight.shape for name, weight in zip(KINDS, weights)}
    arrays = dict(glate=chained["out_late"])
    for name, moment, weight in zip(KINDS, moments, weights):
        if ringed and name in LARGE:
            arrays["n" + name], arrays["m" + name] = chained["out_o" + name], chained["out_p" + name]
        else:
            arrays["p" + name], arrays["w" + name] = moment, weight
    if ringed:
        arrays |= tokens
    else:
        arrays.update(gmid=chained["out_mid"], gdr=chained["out_dr"])
    first = ["glate", "psq", "pinl", *(kind + name for name in LARGE for kind in "nm")]
    first = [name for name in first if name in arrays]
    loaded = first + [name for name in arrays if name not in first]
    in_hbm = {"hbm_" + name: array for name, array in arrays.items()}
    out_hbm, stored = {}, {}
    scratch = {name: pltpu.VMEM(arrays[name].shape, jnp.float32) for name in loaded}
    for name, shape in shapes.items():
        for kind, dtype in (("m", jnp.float32), ("n", jnp.float32), ("c", jnp.bfloat16)):
            through = ringed and name in LARGE and kind in "mn"
            target = ("new_" if through else "") + kind + name
            out_hbm["hbm_" + target] = jax.ShapeDtypeStruct(shape, dtype)
            stored[target] = kind + name
            scratch.setdefault(kind + name, pltpu.VMEM(shape, dtype))
        if not (ringed and name in LARGE):
            scratch["o" + name] = pltpu.VMEM(shape, jnp.float32)
    if ringed:
        for name, array in tokens.items():
            out_hbm["hbm_new_" + name] = jax.ShapeDtypeStruct(array.shape, jnp.float32)
            stored["new_" + name] = name
    in_vmem, out_vmem = {}, {}
    for name, (weight, first, second) in small.items():
        in_vmem[name + "w"], in_vmem[name + "1"], in_vmem[name + "2"] = weight, first, second
        for suffix in ("1n", "2n", "n"):
            out_vmem[name + suffix] = jax.ShapeDtypeStruct(weight.shape, jnp.float32)
        out_vmem[name + "c"] = jax.ShapeDtypeStruct(weight.shape, jnp.bfloat16)
    if not ringed:
        size = shapes["dr"]
        scratch.update({n: pltpu.VMEM(size, jnp.float32) for n in ("x", "a")})
        for name in ("xh", "xl", "ah", "al", "ph", "pl"):
            scratch[name] = pltpu.VMEM(size, jnp.bfloat16)
    scratch["read_sem"] = pltpu.SemaphoreType.DMA((len(loaded),))
    scratch["write_sem"] = pltpu.SemaphoreType.DMA((len(stored),))
    vmem = pl.BlockSpec(memory_space=pltpu.VMEM)
    hbm = pl.BlockSpec(memory_space=pl.ANY)
    names = [*in_hbm, *in_vmem, *out_hbm, *out_vmem, *scratch]
    results = pl.pallas_call(
        functools.partial(update_kernel, names, loaded, stored, ringed),
        out_shape=[*out_hbm.values(), *out_vmem.values()],
        in_specs=[hbm] * len(in_hbm) + [vmem] * len(in_vmem),
        out_specs=[hbm] * len(out_hbm) + [vmem] * len(out_vmem),
        scratch_shapes=list(scratch.values()),
        compiler_params=pltpu.CompilerParams(vmem_limit_bytes=60 * 2**20),
        name="update",
    )(*in_hbm.values(), *in_vmem.values())
    new = dict(zip([*out_hbm, *out_vmem], results))
    return {name.removeprefix("hbm_").removeprefix("new_"): value for name, value in new.items()}


def per_device(
    block_input,
    out_grad,
    lengths,
    square_factors,
    square_moment,
    input_left,
    input_left_moment,
    up_left,
    up_left_moment,
    down_right,
    down_right_moment,
    down_left,
    down_left_moment,
    vectors,
    vectors_first,
    vectors_second,
    filter_hidden,
    hidden_first,
    hidden_second,
    filter_out,
    filter_out_first,
    filter_out_second,
):
    weights = (square_factors[:, 0], input_left[0], up_left[0], down_right[0], down_left[0].T)
    moments = (
        square_moment[:, 0],
        input_left_moment[0],
        up_left_moment[0],
        down_right_moment[0],
        down_left_moment[0].T,
    )
    block_output, input_grad, chained = run_chain(
        block_input, out_grad, lengths, weights, moments, vectors, filter_hidden, filter_out.T
    )
    small = dict(
        v=(vectors, vectors_first, vectors_second),
        h=(filter_hidden, hidden_first, hidden_second),
        f=(filter_out.T, filter_out_first.T, filter_out_second.T),
    )
    tokens = dict(block_out=block_output, input_grad=input_grad)
    new = tokens | run_update(chained, tokens, moments, weights, small)
    return (
        new["block_out"].reshape(block_input.shape),
        new["input_grad"].reshape(block_input.shape),
        *[new[kind + "sq"][:, None] for kind in "mnc"],
        *[new[kind + name][None] for name in ("inl", "ul", "dr") for kind in "mnc"],
        *[new[kind + "dl"].T[None] for kind in "mnc"],
        *[new[name + suffix] for name in "vh" for suffix in ("1n", "2n", "n", "c")],
        *[new["f" + suffix].T for suffix in ("1n", "2n", "n", "c")],
    )


def solution(mesh):
    tokens = P(None, "seq", "mp")
    square = P(None, "mp", None, None)
    block = P("mp", None, None)
    row = P(None, "mp")
    return jax.shard_map(
        per_device,
        mesh=mesh,
        in_specs=(tokens, tokens, P(), square, square)
        + (block,) * 8
        + (row,) * 3
        + (P(),) * 3
        + (row,) * 3,
        out_specs=(tokens, tokens)
        + (square,) * 3
        + (block,) * 12
        + (row,) * 4
        + (P(),) * 4
        + (row,) * 4,
        check_vma=False,
    )
```
